32 devices in a mesh: lat: 4 (over y, core), lon: 8 (over z, x).
Axes of the slice: x: 2, y: 2, z: 4, core: 2. Of those that a mesh axis runs over, the one named last changes fastest.
Arguments:
- signal: bfloat16 [32, 384, 1024], P(None, 'lat', 'lon'), may hold values from -6 to 6
- cotangent: bfloat16 [32, 384, 1024], P(None, 'lat', 'lon'), may hold values from -6 to 6
- edge_weights: bfloat16 [3, 384, 1024], P(None, 'lat', 'lon'), may hold values from 0.25 to 1
- circle_shift: int32 [384], P('lat'), may hold values from 0 to 1
- mixing: bfloat16 [6, 32, 32], replicated, may hold values from -0.4375 to 0.4375
Outputs:
- output: bfloat16 [32, 384, 1024], P(None, 'lat', 'lon')
- signal_grad: bfloat16 [32, 384, 1024], P(None, 'lat', 'lon')
- mixing_grad: float32 [6, 32, 32], replicated
The draws below stay inside these ranges and needn't reach their ends.
All inputs are finite; a program needn't handle non-finite values.
Results may differ from the reference program's by a relative error of at most 0.0064.
Values may be sent and summed in bfloat16 or wider, within the bound.
No kernel may reach another device: no remote copies, remote signals or barrier semaphores. Data moves between devices by JAX's collectives and lax.ppermute only.
A program may use at most 128 MiB of HBM per device.

```python
import math
import jax
import jax.numpy as jnp
from jax import lax

CH = 32
ORDER = 6
CIRCLES = 384
CIRCLE_PIX = 1024


def plant(result, key, least, high):
    index_at = [jax.random.randint(jax.random.fold_in(key, axis), (), 0, length) for axis, length in enumerate(result.shape)]
    longest = result.shape.index(max(result.shape))
    beside = index_at[:longest] + [(index_at[longest] + 1) % result.shape[longest]] + index_at[longest + 1:]
    return result.at[tuple(index_at)].set(least).at[tuple(beside)].set(high)


def block_scale(stream_key, extent, shards, smallest, largest):
    gain = 1.0
    for dim, blocks in shards:
        draws = jax.random.uniform(jax.random.fold_in(jax.random.fold_in(stream_key, 6), dim), (blocks,), jnp.float32, smallest / len(shards), largest / len(shards))
        gain = gain * jnp.repeat(jnp.exp(draws), extent[dim] // blocks).reshape((-1,) + (1,) * (len(extent) - 1 - dim))
    return gain


def noise(stream_key, dims, scale, limit, cuts=(), kind=jnp.bfloat16):
    loudness = block_scale(stream_key, dims, cuts, -0.22, 0.18) if cuts else 1.0
    drawn = jax.random.normal(stream_key, dims, jnp.float32) * scale * loudness
    return jnp.minimum(jnp.maximum(drawn, -limit), limit).astype(kind)


def setup_inputs(seed: int = 0) -> dict:
    key_of = jax.random.split(jax.random.key(seed), 6)
    return {
        "signal": noise(key_of[0], (CH, CIRCLES, CIRCLE_PIX), 1.0, 6.0, ((1, 4), (2, 8))),
        "cotangent": noise(key_of[1], (CH, CIRCLES, CIRCLE_PIX), 1.0, 6.0, ((1, 4), (2, 8))),
        "edge_weights": jnp.clip(0.25 + 0.75 * jax.random.uniform(key_of[2], (3, CIRCLES, CIRCLE_PIX), jnp.float32) ** block_scale(key_of[2], (3, CIRCLES, CIRCLE_PIX), ((1, 4), (2, 8)), -0.2, 0.2), 0.25, 1.0).astype(jnp.bfloat16),
        "circle_shift": plant(jax.random.randint(key_of[3], (CIRCLES,), 0, 2), jax.random.fold_in(key_of[3], 1), 0, 1).astype(jnp.int32),
        "mixing": noise(key_of[4], (ORDER, CH, CH), (ORDER * CH) ** -0.5, 0.4375),
    }


def widen(array):
    padded = jnp.pad(array, ((0, 0), (1, 1), (0, 0)))
    return jnp.concatenate([padded[:, :, -1:], padded, padded[:, :, :1]], axis=2)

def channel_laplacian(source_in, weights):
    source = source_in.astype(jnp.float32)
    w_east = weights[0].astype(jnp.float32)
    w_south = weights[1].astype(jnp.float32)
    w_diag = weights[2].astype(jnp.float32)
    parity_all = weights[3].astype(jnp.float32)
    centre = source[1:-1, 1:-1]
    parity_here = parity_all[1:-1, 1:-1]
    parity_above = parity_all[:-2, 1:-1]
    neighbours = w_east[1:-1, 1:-1] * source[1:-1, 2:] + w_east[1:-1, :-2] * source[1:-1, :-2]
    neighbours = neighbours + w_south[1:-1, 1:-1] * source[2:, 1:-1] + w_south[:-2, 1:-1] * source[:-2, 1:-1]
    neighbours = neighbours + w_diag[1:-1, 1:-1] * (parity_here * source[2:, 2:] + (1.0 - parity_here) * source[2:, :-2])
    neighbours = neighbours + parity_above * w_diag[:-2, :-2] * source[:-2, :-2] + (1.0 - parity_above) * w_diag[:-2, 2:] * source[:-2, 2:]
    degree = w_east[1:-1, 1:-1] + w_east[1:-1, :-2] + w_south[1:-1, 1:-1] + w_south[:-2, 1:-1] + w_diag[1:-1, 1:-1]
    degree = degree + parity_above * w_diag[:-2, :-2] + (1.0 - parity_above) * w_diag[:-2, 2:]
    return (degree * centre - neighbours) / 6.0 - centre

def reference(signal, cotangent, edge_weights, circle_shift, mixing):
    parity = jnp.broadcast_to((circle_shift == 1).astype(jnp.bfloat16)[None, :, None], (1,) + signal.shape[1:])
    wide_weights = widen(jnp.concatenate([edge_weights, parity], axis=0))

    def operate(values):
        return lax.map(lambda single: channel_laplacian(single, wide_weights), widen(values))
    mixing_f = mixing.astype(jnp.float32)
    output_sum = jnp.zeros(signal.shape, jnp.float32)
    grads = []
    older_term = None
    later_term = signal
    for position in range(ORDER):
        if position == 0:
            current = signal
        elif position == 1:
            current = operate(signal).astype(jnp.bfloat16)
        else:
            current = (2.0 * operate(later_term) - older_term.astype(jnp.float32)).astype(jnp.bfloat16)
        if position > 0:
            older_term = later_term
            later_term = current
        output_sum = output_sum + jnp.einsum('crp,co->orp', current.astype(jnp.float32), mixing_f[position])
        grads.append(jnp.einsum('crp,orp->co', current.astype(jnp.float32), cotangent.astype(jnp.float32)))
    output = output_sum.astype(jnp.bfloat16)
    mixing_grad = jnp.stack(grads) * (1.0 / math.sqrt(CIRCLES * CIRCLE_PIX))

    def hidden_term(position):
        return jnp.einsum('co,orp->crp', mixing_f[position], cotangent.astype(jnp.float32)).astype(jnp.bfloat16)
    back_later = hidden_term(ORDER - 1)
    back_older = None
    for position in range(ORDER - 2, 0, -1):
        summed = hidden_term(position).astype(jnp.float32) + 2.0 * operate(back_later)
        if back_older is not None:
            summed = summed - back_older.astype(jnp.float32)
        back_older = back_later
        back_later = summed.astype(jnp.bfloat16)
    signal_grad = (hidden_term(0).astype(jnp.float32) + operate(back_later) - back_older.astype(jnp.float32)).astype(jnp.bfloat16)
    return (output, signal_grad, mixing_grad)
```

```python
import math

import jax
import jax.numpy as jnp
from jax import lax
from jax.experimental import pallas as pl
from jax.experimental.pallas import tpu as pltpu
from jax.sharding import PartitionSpec as P

F32 = jnp.float32
BF16 = jnp.bfloat16
HALO = 5
LANES = 128
BLOCKS = 4
GROUP = LANES // BLOCKS
SIDE = GROUP // 2
PACKED = 80
TILE = 16


def params():
    return pltpu.CompilerParams(vmem_limit_bytes=56 * 1024 * 1024)


def lane_index(shape):
    return lax.broadcasted_iota(jnp.int32, shape, 1)


def pack_kernel(signal, cotangent, weights, shift, rows_out, edges_out, strips_out, wide):
    channels, rows, _ = signal.shape
    block = rows // BLOCKS
    per_row = block // 3

    def widen(c, _):
        wide[pl.ds(c * rows, rows), :] = signal[c].astype(F32)
        wide[pl.ds((channels + c) * rows, rows), :] = cotangent[c].astype(F32)
        return 0

    lax.fori_loop(0, channels, widen, 0)
    base = 2 * channels * rows
    for i in range(3):
        wide[base + i * rows:base + (i + 1) * rows, :] = weights[i].astype(F32)
    wide[base + 3 * rows:base + 8 * rows, :] = jnp.zeros((5 * rows, LANES), F32)

    count = 2 * channels + 8
    lane = lane_index((count, LANES))
    sub = lax.broadcasted_iota(jnp.int32, (8, LANES), 0)

    def load_row(r):
        body = wide[pl.ds(r, 2 * channels, stride=rows), :]
        tail = wide[pl.ds(base + r, 8, stride=rows), :]
        parity = jnp.where(shift[r] == 1, 1.0, 0.0).astype(F32)
        tail = jnp.where(sub == 3, parity, tail)
        return jnp.concatenate([body, tail], axis=0)

    def to_packed(x):
        return jnp.concatenate([x, jnp.zeros((PACKED - count, LANES), F32)], axis=0).astype(BF16)

    def per_edge_row(t, _):
        edges = jnp.zeros((count, LANES), F32)
        strips = [jnp.zeros((count, LANES), F32) for _ in range(3)]
        for b in range(BLOCKS):
            for m in range(3):
                r = block * b + per_row * m + t
                x = load_row(r)
                rows_out[r] = to_packed(x)
                first = GROUP * b + 10 * m
                moved = pltpu.roll(x, (first + 5) % LANES, 1)
                edges = jnp.where((lane >= first) & (lane < first + 10), moved, edges)
                west = pltpu.roll(x, GROUP * b + 5, 1)
                east = pltpu.roll(x, (GROUP * b + SIDE + 11) % LANES, 1)
                strip = strips[m]
                strip = jnp.where((lane >= GROUP * b + 5) & (lane < GROUP * b + SIDE), west, strip)
                strips[m] = jnp.where((lane >= GROUP * b + SIDE) & (lane < GROUP * b + SIDE + 11), east, strip)
        edges_out[t] = to_packed(edges)
        for m in range(3):
            strips_out[per_row * m + t] = to_packed(strips[m])
        return 0

    lax.fori_loop(0, per_row, per_edge_row, 0)


def merge_kernel(rows_in, strips_in, from_west, from_east, strips_out, north_out, south_out):
    block = strips_in.shape[0]
    rows = rows_in.shape[0]
    per_row = block // 3
    lane = lane_index((PACKED, LANES)) % GROUP

    def each(t, _):
        west = from_west[t].astype(F32)
        east = from_east[t].astype(F32)
        for m in range(3):
            strip = strips_in[per_row * m + t].astype(F32)
            w = pltpu.roll(west, (-10 * m) % LANES, 1)
            e = pltpu.roll(east, (22 - 10 * m) % LANES, 1)
            strip = jnp.where(lane < 5, w, strip)
            strip = jnp.where(lane >= GROUP - 5, e, strip)
            strips_out[per_row * m + t] = strip.astype(BF16)
        return 0

    lax.fori_loop(0, per_row, each, 0)
    group = lane_index((PACKED, LANES)) // GROUP
    for out, first_row, first_strip, side in ((north_out, 0, 0, 0), (south_out, rows - HALO, block - HALO, BLOCKS - 1)):
        for i in range(HALO):
            out[i] = rows_in[first_row + i]
        corner = strips_out[first_strip].astype(F32)
        corner = pltpu.roll(corner, (-GROUP * side) % LANES, 1) if side else corner
        for g in range(1, BLOCKS):
            amount = GROUP * (g - side) % LANES
            piece = strips_out[first_strip + g].astype(F32)
            piece = pltpu.roll(piece, amount, 1) if amount else piece
            corner = jnp.where(group == g, piece, corner)
        out[HALO] = corner.astype(BF16)
        last = strips_out[first_strip + HALO - 1].astype(F32)
        amount = -GROUP * side % LANES
        out[HALO + 1] = (pltpu.roll(last, amount, 1) if amount else last).astype(BF16)


def sizes(rows):
    block = rows // BLOCKS
    main = rows + 2 * HALO
    strip_base = -(-(main + 6) // 8) * 8
    total = -(-(strip_base + block + 2 * HALO + 6) // 8) * 8
    return block, main, strip_base, total


def each_row(rows_in, strips_in, north, south, channel, width, put):
    rows = rows_in.shape[0]
    block, main, strip_base, _ = sizes(rows)
    part = pl.ds(channel, width)

    for i in range(HALO):
        put(1 + i, north[i, part, :].astype(F32))
        put(1 + HALO + rows + i, south[i, part, :].astype(F32))

    def copy_main(r, _):
        put(1 + HALO + r, rows_in[r, part, :].astype(F32))
        return 0

    lax.fori_loop(0, rows, copy_main, 0)

    def copy_strip(s, _):
        put(strip_base + 1 + HALO + s, strips_in[s, part, :].astype(F32))
        return 0

    lax.fori_loop(0, block, copy_strip, 0)
    lane = lane_index((width, LANES))
    for i in range(HALO):
        above = pltpu.roll(strips_in[block - HALO + i, part, :].astype(F32), GROUP, 1)
        corner = north[HALO + (i == HALO - 1), part, :].astype(F32)
        amount = 0 if i == HALO - 1 else -GROUP * i % LANES
        corner = pltpu.roll(corner, amount, 1) if amount else corner
        put(strip_base + 1 + i, jnp.where(lane < GROUP, corner, above))
        below = pltpu.roll(strips_in[i, part, :].astype(F32), LANES - GROUP, 1)
        corner = south[HALO + (i == HALO - 1), part, :].astype(F32)
        amount = (LANES - GROUP - (0 if i == HALO - 1 else GROUP * i)) % LANES
        corner = pltpu.roll(corner, amount, 1) if amount else corner
        put(strip_base + 1 + HALO + block + i, jnp.where(lane >= LANES - GROUP, corner, below))


def coefficient_kernel(is_last, rows_in, strips_in, north, south, coef_out, parity_out, wide):
    rows = rows_in.shape[0]
    block, main, strip_base, total = sizes(rows)
    wide[...] = jnp.zeros(wide.shape, F32)

    def put(index, tile):
        wide[pl.ds(pl.multiple_of(index * 8, 8), 8), :] = tile[:8]

    each_row(rows_in, strips_in, north, south, PACKED - TILE, TILE, put)
    w_east, w_south, w_diag, parity = [wide[pl.ds(i, total, stride=8), :] for i in range(4)]
    w_back = jnp.where(parity > 0.5, pltpu.roll(w_diag, 1, 1), pltpu.roll(w_diag, LANES - 1, 1))
    w_west = pltpu.roll(w_east, 1, 1)
    to_south = w_south + w_back
    wide[0:8, :] = jnp.zeros((8, LANES), F32)
    wide[8:8 + total, :] = to_south
    degree = w_east + w_west + w_south + w_diag + wide[7:7 + total, :]
    row = lax.broadcasted_iota(jnp.int32, (total, LANES), 0)
    lane = lane_index((total, LANES))
    edge = (row == HALO + rows) | ((row == strip_base + HALO + block) & (lane >= LANES - GROUP))
    keep = jnp.where(edge & (is_last[0] == 1), 0.0, 1.0).astype(F32)
    third = -1.0 / 3.0
    coef_out[0] = degree * (1.0 / 3.0) - 2.0
    coef_out[1] = w_east * third
    coef_out[2] = w_west * third
    coef_out[3] = w_south * keep * third
    coef_out[4] = w_diag * keep * third
    coef_out[5] = w_back * keep * third
    parity_out[...] = parity


def chain_body(first, with_grad, rows_in, strips_in, north, south, coef, parity, mix, out, grad, term_a, term_b, kept, strip_out, wide):
    rows = rows_in.shape[0]
    channels = mix.shape[0]
    order = mix.shape[1] // channels
    block, main, strip_base, total = sizes(rows)
    for index in (0, main + 1, main + 2, main + 3, main + 4, strip_base, strip_base + block + 2 * HALO + 1,
                  strip_base + block + 2 * HALO + 2, strip_base + block + 2 * HALO + 3, strip_base + block + 2 * HALO + 4):
        term_a[index] = jnp.zeros((channels, LANES), F32)
        term_b[index] = jnp.zeros((channels, LANES), F32)

    def put(index, tile):
        term_a[index] = tile
        kept[index, 0:channels, :] = tile.astype(BF16)

    each_row(rows_in, strips_in, north, south, first, channels, put)

    def step(position, now, older):
        def one_row(index, accumulated, down):
            def row_of(i, at):
                return coef[i, pl.ds(at, 1), :]
            v = now[index]
            v_east = pltpu.roll(v, LANES - 1, 1)
            v_west = pltpu.roll(v, 1, 1)
            above = parity[pl.ds(index - 1, 1), :] > 0.5
            here = parity[pl.ds(index, 1), :] > 0.5
            above = jnp.broadcast_to(above, v.shape)
            here = jnp.broadcast_to(here, v.shape)
            up = row_of(3, index - 1) * v + row_of(4, index - 1) * jnp.where(above, v_east, v_west)
            new = accumulated + up
            if position == 1:
                new = new * 0.5
            level = row_of(0, index) * v + row_of(1, index) * v_east + row_of(2, index) * v_west + down
            if position > 1:
                level = level - older[index]
            down = row_of(3, index) * v + row_of(5, index) * jnp.where(here, v_west, v_east)
            older[index - 1] = new
            kept[index - 1, position * channels:(position + 1) * channels, :] = new.astype(BF16)
            return level, down

        for base, count in ((0, main), (strip_base, block + 2 * HALO)):
            start = base + position
            span = count + 2 - 2 * position
            unroll = 4
            trips = -(-span // unroll)

            def several(trip, carry):
                for j in range(unroll):
                    carry = one_row(start + trip * unroll + j, *carry)
                return carry

            zero = jnp.zeros((channels, LANES), F32)
            lax.fori_loop(0, trips, several, (zero, zero))

    buffers = (term_a, term_b)
    for position in range(1, order):
        step(position, buffers[(position - 1) % 2], buffers[position % 2])

    mixed = mix[...]
    lane = lane_index((channels, LANES))
    lane_in = lane % GROUP
    strip_valid = ((lane_in >= 5) & (lane_in < 10)) | ((lane_in >= SIDE + 6) & (lane_in < SIDE + 11))
    main_valid = (lane >= HALO) & (lane < LANES - HALO)
    contract_lanes = (((1,), (1,)), ((), ()))

    def strip_rows(s, total_grad):
        terms = kept[strip_base + 1 + HALO + s]
        strip_out[s] = jnp.dot(mixed, terms, preferred_element_type=F32)
        if with_grad:
            paired = jnp.where(strip_valid, strips_in[s, channels:2 * channels, :].astype(F32), 0.0).astype(BF16)
            total_grad = total_grad + lax.dot_general(paired, terms, contract_lanes, preferred_element_type=F32)
        return total_grad

    total_grad = jnp.zeros((channels, order * channels), F32) if with_grad else 0
    total_grad = lax.fori_loop(0, block, strip_rows, total_grad)

    for b in range(BLOCKS):
        def main_rows(s, total_grad):
            r = block * b + s
            terms = kept[1 + HALO + r]
            value = jnp.dot(mixed, terms, preferred_element_type=F32)
            strip = strip_out[s]
            west = pltpu.roll(strip, -(GROUP * b + 5) % LANES, 1)
            east = pltpu.roll(strip, (LANES - 5 - (GROUP * b + SIDE + 6)) % LANES, 1)
            value = jnp.where(lane < HALO, west, jnp.where(lane >= LANES - HALO, east, value))
            wide[pl.ds(r, channels, stride=rows), :] = value
            if with_grad:
                paired = jnp.where(main_valid, rows_in[r, channels:2 * channels, :].astype(F32), 0.0).astype(BF16)
                total_grad = total_grad + lax.dot_general(paired, terms, contract_lanes, preferred_element_type=F32)
            return total_grad

        total_grad = lax.fori_loop(0, block, main_rows, total_grad)

    def narrow(o, _):
        out[o] = wide[pl.ds(pl.multiple_of(o * rows, 8), rows), :].astype(BF16)
        return 0

    lax.fori_loop(0, channels, narrow, 0)
    if with_grad:
        grad[...] = total_grad


def forward_kernel(rows_in, strips_in, north, south, coef, parity, mix, out, grad, *scratch):
    chain_body(0, True, rows_in, strips_in, north, south, coef, parity, mix, out, grad, *scratch)


def backward_kernel(rows_in, strips_in, north, south, coef, parity, mix, out, *scratch):
    chain_body(mix.shape[0], False, rows_in, strips_in, north, south, coef, parity, mix, out, None, *scratch)


def on_device(signal, cotangent, edge_weights, circle_shift, mixing):
    channels, rows, sector = signal.shape
    order = mixing.shape[0]
    block, main, strip_base, total = sizes(rows)
    per_row = block // 3
    lat, lon = lax.axis_size("lat"), lax.axis_size("lon")
    vmem = pl.BlockSpec(memory_space=pltpu.VMEM)
    smem = pl.BlockSpec(memory_space=pltpu.SMEM)

    def packed(count):
        return jax.ShapeDtypeStruct((count, PACKED, LANES), BF16)

    rows_in, edges, strips = pl.pallas_call(
        pack_kernel,
        out_shape=(packed(rows), packed(per_row), packed(block)),
        in_specs=[vmem, vmem, vmem, smem],
        out_specs=(vmem, vmem, vmem),
        scratch_shapes=[pltpu.VMEM(((2 * channels + 8) * rows, LANES), F32)],
        compiler_params=params(),
    )(signal, cotangent, edge_weights, circle_shift)

    eastward = [(i, (i + 1) % lon) for i in range(lon)]
    westward = [(j, i) for i, j in eastward]
    from_west = lax.ppermute(edges, "lon", eastward)
    from_east = lax.ppermute(edges, "lon", westward)

    strips, to_north, to_south = pl.pallas_call(
        merge_kernel,
        out_shape=(packed(block), packed(HALO + 2), packed(HALO + 2)),
        in_specs=[vmem] * 4,
        out_specs=(vmem,) * 3,
        compiler_params=params(),
    )(rows_in, strips, from_west, from_east)

    southward = [(i, i + 1) for i in range(lat - 1)]
    northward = [(j, i) for i, j in southward]
    north = lax.ppermute(to_south, "lat", southward)
    south = lax.ppermute(to_north, "lat", northward)

    is_last = (lax.axis_index("lat") == lat - 1).astype(jnp.int32).reshape(1)
    halo_args = (rows_in, strips, north, south)
    coef, parity = pl.pallas_call(
        coefficient_kernel,
        out_shape=(jax.ShapeDtypeStruct((6, total, LANES), F32), jax.ShapeDtypeStruct((total, LANES), F32)),
        in_specs=[smem] + [vmem] * 4,
        out_specs=(vmem, vmem),
        scratch_shapes=[pltpu.VMEM((total * 8, LANES), F32)],
        compiler_params=params(),
    )(is_last, *halo_args)

    mix_forward = mixing.transpose(2, 0, 1).reshape(channels, order * channels)
    mix_backward = mixing.transpose(1, 0, 2).reshape(channels, order * channels)
    mapped = jax.ShapeDtypeStruct(signal.shape, BF16)
    scratch = [
        pltpu.VMEM((total, channels, LANES), F32),
        pltpu.VMEM((total, channels, LANES), F32),
        pltpu.VMEM((total, order * channels, LANES), BF16),
        pltpu.VMEM((block, channels, LANES), F32),
        pltpu.VMEM((channels * rows, LANES), F32),
    ]
    output, grad = pl.pallas_call(
        forward_kernel,
        out_shape=(mapped, jax.ShapeDtypeStruct((channels, order * channels), F32)),
        in_specs=[vmem] * 7,
        out_specs=(vmem, vmem),
        scratch_shapes=scratch,
        compiler_params=params(),
    )(*halo_args, coef, parity, mix_forward)
    summed = lax.psum(grad, ("lat", "lon"))
    signal_grad = pl.pallas_call(
        backward_kernel,
        out_shape=mapped,
        in_specs=[vmem] * 7,
        out_specs=vmem,
        scratch_shapes=scratch,
        compiler_params=params(),
    )(*halo_args, coef, parity, mix_backward)
    norm_scale = 1.0 / math.sqrt(rows * lat * sector * lon)
    mixing_grad = summed.T.reshape(order, channels, channels) * norm_scale
    return (output, signal_grad, mixing_grad)


def solution(mesh):
    in_specs = (P(None, "lat", "lon"), P(None, "lat", "lon"), P(None, "lat", "lon"), P("lat"), P())
    out_specs = (P(None, "lat", "lon"), P(None, "lat", "lon"), P())
    return jax.shard_map(
        on_device, mesh=mesh, in_specs=in_specs, out_specs=out_specs, check_vma=False
    )
```

```python
import math

import jax
import jax.numpy as jnp
from jax import lax
from jax.experimental import pallas as pl
from jax.experimental.pallas import tpu as pltpu
from jax.sharding import PartitionSpec as P

F32 = jnp.float32
BF16 = jnp.bfloat16
HALO = 5
LANES = 128
BLOCKS = 4
GROUP = LANES // BLOCKS
SIDE = GROUP // 2
PACKED = 80
BAND = 3 * HALO
UNROLL = 4


def params(mib):
    return pltpu.CompilerParams(vmem_limit_bytes=mib * 1024 * 1024)


def lane_index(shape):
    return lax.broadcasted_iota(jnp.int32, shape, len(shape) - 1)


def turned(x, amount):
    amount = amount % LANES
    return pltpu.roll(x, amount, 1) if amount else x


def widen_all(signal, cotangent, weights, wide):
    channels, rows, _ = signal.shape

    def widen(i, _):
        for j in range(4):
            c = i * 4 + j
            wide[pl.ds(pl.multiple_of(c * rows, 8), rows), :] = signal[c].astype(F32)
            wide[pl.ds(pl.multiple_of((channels + c) * rows, 8), rows), :] = cotangent[c].astype(F32)
        return 0

    lax.fori_loop(0, channels // 4, widen, 0)
    base = 2 * channels * rows
    for i in range(3):
        wide[base + i * rows:base + (i + 1) * rows, :] = weights[i].astype(F32)
    wide[base + 3 * rows:base + 8 * rows, :] = jnp.zeros((5 * rows, LANES), F32)


def row_loader(channels, rows, shift, wide):
    base = 2 * channels * rows
    sub = lax.broadcasted_iota(jnp.int32, (8, LANES), 0)

    def load_row(r):
        body = wide[pl.ds(r, 2 * channels, stride=rows), :]
        tail = wide[pl.ds(base + r, 8, stride=rows), :]
        parity = jnp.where(shift[r] == 1, 1.0, 0.0).astype(F32)
        tail = jnp.where(sub == 3, parity, tail)
        return jnp.concatenate([body, tail, jnp.zeros((8, LANES), F32)], axis=0).astype(BF16)

    return load_row


def pack_kernel(signal, cotangent, weights, shift, west_out, east_out, wide):
    channels, rows, _ = signal.shape
    block = rows // BLOCKS
    per_row = block // 6
    widen_all(signal, cotangent, weights, wide)
    load_row = row_loader(channels, rows, shift, wide)
    lane = lane_index((PACKED, LANES))

    def each(t, _):
        west = jnp.zeros((PACKED, LANES), BF16)
        east = jnp.zeros((PACKED, LANES), BF16)
        for b in range(BLOCKS):
            for m in range(6):
                x = load_row(block * b + per_row * m + t)
                first = GROUP * b + 5 * m
                moved = turned(x, first + 5)
                east = jnp.where((lane >= first) & (lane < first + 5), moved, east)
                west = jnp.where((lane - (first + 5)) % LANES < 5, moved, west)
        west_out[t] = west
        east_out[t] = east
        return 0

    lax.fori_loop(0, per_row, each, 0)


def own_kernel(signal, cotangent, weights, shift, strips_out, top_out, bottom_out, wide):
    channels, rows, _ = signal.shape
    block = rows // BLOCKS
    widen_all(signal, cotangent, weights, wide)
    load_row = row_loader(channels, rows, shift, wide)
    lane = lane_index((PACKED, LANES))

    def each(s, _):
        strip = jnp.zeros((PACKED, LANES), BF16)
        for b in range(BLOCKS):
            x = load_row(block * b + s)
            west = turned(x, GROUP * b + 5)
            east = turned(x, GROUP * b + SIDE + 11)
            strip = jnp.where((lane >= GROUP * b + 5) & (lane < GROUP * b + SIDE), west, strip)
            strip = jnp.where((lane >= GROUP * b + SIDE) & (lane < GROUP * b + SIDE + 11), east, strip)
        strips_out[s] = strip
        return 0

    lax.fori_loop(0, block, each, 0)
    for i in range(2 * HALO):
        top_out[i] = load_row(i)
        bottom_out[i] = load_row(rows - 2 * HALO + i)


def merge_kernel(strips_in, top, bottom, from_west, from_east, strips_out, north_out, south_out):
    block = strips_in.shape[0]
    per_row = block // 6
    lane = lane_index((PACKED, LANES))
    lane_in = lane % GROUP

    def each(t, _):
        west = from_west[t]
        east = from_east[t]
        for m in range(6):
            strip = strips_in[per_row * m + t]
            strip = jnp.where(lane_in < 5, turned(west, -5 * m), strip)
            strip = jnp.where(lane_in >= GROUP - 5, turned(east, 22 - 5 * m), strip)
            strips_out[per_row * m + t] = strip
        return 0

    lax.fori_loop(0, per_row, each, 0)
    for out, rows_from, first_row, first_strip, side in (
        (north_out, top, 0, 0, 0), (south_out, bottom, HALO, block - HALO, BLOCKS - 1)):
        for i in range(HALO):
            out[i] = rows_from[first_row + i]
        corner = turned(strips_out[first_strip], -GROUP * side)
        for g in range(1, BLOCKS):
            piece = turned(strips_out[first_strip + g], GROUP * (g - side))
            corner = jnp.where((lane >= GROUP * g) & (lane < GROUP * (g + 1)), piece, corner)
        out[HALO] = corner
        out[HALO + 1] = turned(strips_out[first_strip + HALO - 1], -GROUP * side)


def write_coefficients(total, first, w_east, w_south, w_diag, parity, keep, coef, shifted):
    count = w_east.shape[0]
    w_back = jnp.where(parity > 0.5, turned(w_diag, 1), turned(w_diag, -1))
    w_west = turned(w_east, 1)
    shifted[0:8, :] = jnp.zeros((8, LANES), F32)
    shifted[8:8 + count, :] = w_south + w_back
    degree = w_east + w_west + w_south + w_diag + shifted[7:7 + count, :]
    third = -1.0 / 3.0
    arrays = [degree * (1.0 / 3.0) - 2.0, w_east * third, w_west * third]
    for array in (w_south, w_diag, w_back):
        arrays.append(array * third if keep is None else array * keep * third)
    for i, array in enumerate(arrays + [parity]):
        coef[i * total + first:i * total + first + count, :] = array


def stencil_steps(order, channels, total, coef, buffers, kept, regions):
    groups = channels // 8

    def coef_row(i, at):
        return coef[pl.ds(i * total + at, 8, stride=0), :]

    def step(position, now, older):
        last = position == order - 1

        def chain(base, at):
            now_rows = [[now[at + j, 8 * g:8 * g + 8, :] for g in range(groups)] for j in range(UNROLL)]
            old_rows = None
            if position > 1:
                old_rows = [[older[at + j, 8 * g:8 * g + 8, :] for g in range(groups)] for j in range(UNROLL)]
            coefs = [[coef_row(i, at + j) for i in range(7)] for j in range(UNROLL)]
            before = [None] * 3 + [coef_row(i, at - 1) for i in (3, 4)] + [None, coef_row(6, at - 1)]
            return now_rows, old_rows, [before] + coefs

        def compute(loaded, level, down):
            now_rows, old_rows, coefs = loaded
            level, down = list(level), list(down)
            results = []
            above = coefs[0][6] > 0.5
            for j in range(UNROLL):
                c, e, w, s, d, back, parity = coefs[j + 1]
                s_above, d_above = coefs[j][3], coefs[j][4]
                here = parity > 0.5
                row = []
                for g in range(groups):
                    v = now_rows[j][g]
                    v_east = pltpu.roll(v, LANES - 1, 1)
                    v_west = pltpu.roll(v, 1, 1)
                    new = level[g] + s_above * v + d_above * jnp.where(above, v_east, v_west)
                    if position == 1:
                        new = new * 0.5
                    row.append(new)
                    level[g] = c * v + e * v_east + w * v_west + down[g]
                    if position > 1:
                        level[g] = level[g] - old_rows[j][g]
                    down[g] = s * v + back * jnp.where(here, v_west, v_east)
                results.append(row)
                above = here
            return results, tuple(level), tuple(down)

        def save(at, results):
            for j in range(UNROLL):
                row = results[j]
                if not last:
                    for g in range(groups):
                        older[at + j - 1, 8 * g:8 * g + 8, :] = row[g]
                for h in range(channels // 16):
                    ref, first = kept[h // 2], 32 * position + 16 * (h % 2)
                    pair = jnp.concatenate([row[2 * h], row[2 * h + 1]], axis=0)
                    ref[at + j - 1, first:first + 16, :] = pair.astype(BF16)

        for bases, count in regions:
            span = count + 2 - 2 * position

            def several(trip, carry, bases=bases):
                starts = [base + position + trip * UNROLL for base in bases]
                loaded = [chain(base, at) for base, at in zip(bases, starts)]
                done = [compute(x, *state) for x, state in zip(loaded, carry)]
                for at, (results, _, _) in zip(starts, done):
                    save(at, results)
                return tuple((level, down) for _, level, down in done)

            zeros = tuple(jnp.zeros((8, LANES), F32) for _ in range(groups))
            lax.fori_loop(0, -(-span // UNROLL), several, tuple((zeros, zeros) for _ in bases))

    for position in range(1, order):
        step(position, buffers[(position - 1) % 2], buffers[position % 2])


def zero_guards(buffers, coef, total, guards):
    for first, end in guards:
        for index in range(first, end):
            for buffer in buffers:
                buffer[index] = jnp.zeros(buffer.shape[1:], F32)
        for i in range(7):
            coef[i * total + first:i * total + end, :] = jnp.zeros((end - first, LANES), F32)


CONTRACT_LANES = (((1,), (1,)), ((), ()))


def two_rows(ref, index, size):
    return jnp.concatenate([ref[index, 0:size, :], ref[index + 1, 0:size, :]], axis=1)


def main_body(with_grad, field, other, weights, shift, mix, out, grad, wide, term_a, term_b, kept, coef, paired):
    channels, rows, _ = field.shape
    order = mix.shape[1] // channels
    total = term_a.shape[0]

    def widen(source):
        def each(i, _):
            for j in range(4):
                c = i * 4 + j
                wide[pl.ds(pl.multiple_of(c * rows, 8), rows), :] = source[c].astype(F32)
            return 0
        lax.fori_loop(0, channels // 4, each, 0)

    zero_guards((term_a, term_b), coef, total, ((0, 1), (rows + 1, total)))
    for r in range(rows):
        value = jnp.where(shift[r] == 1, 1.0, 0.0).astype(F32)
        wide[r:r + 1, :] = jnp.broadcast_to(value, (1, LANES))
    parity = wide[0:rows, :]
    w_east, w_south, w_diag = [weights[i].astype(F32) for i in range(3)]
    write_coefficients(total, 1, w_east, w_south, w_diag, parity, None, coef, wide)

    if with_grad:
        widen(other)
        lane = lane_index((channels, LANES))
        valid = (lane >= HALO) & (lane < LANES - HALO)

        def pair_rows(i, _):
            for j in range(8):
                r = i * 8 + j
                paired[r] = jnp.where(valid, wide[pl.ds(r, channels, stride=rows), :], 0.0).astype(BF16)
            return 0

        lax.fori_loop(0, rows // 8, pair_rows, 0)

    widen(field)

    def fill(i, _):
        for j in range(8):
            r = i * 8 + j
            x = wide[pl.ds(r, channels, stride=rows), :]
            term_a[r + 1] = x
            kept[r + 1, 0:channels, :] = x.astype(BF16)
        return 0

    lax.fori_loop(0, rows // 8, fill, 0)
    stencil_steps(order, channels, total, coef, (term_a, term_b), (kept,), (((0,), rows),))

    mixed = mix[...]

    def products(start, pairs, total_grad):
        terms = [two_rows(kept, start + 1 + 2 * i, order * channels) for i in range(pairs)]
        for i, term in enumerate(terms):
            r = start + 2 * i
            value = jnp.dot(mixed, term, preferred_element_type=F32).astype(BF16)
            out[r] = value[:, :LANES]
            out[r + 1] = value[:, LANES:]
        if with_grad:
            for i, term in enumerate(terms):
                left = two_rows(paired, start + 2 * i, channels)
                total_grad = total_grad + lax.dot_general(left, term, CONTRACT_LANES, preferred_element_type=F32)
        return total_grad

    inner = rows - 2 * HALO
    total_grad = jnp.zeros((channels, order * channels), F32) if with_grad else 0
    total_grad = lax.fori_loop(0, inner // 8, lambda i, g: products(HALO + i * 8, 4, g), total_grad)
    if inner % 8:
        total_grad = products(HALO + inner // 8 * 8, inner % 8 // 2, total_grad)
    if with_grad:
        grad[...] = total_grad


def main_forward(signal, cotangent, weights, shift, mix, out, grad, *scratch):
    main_body(True, signal, cotangent, weights, shift, mix, out, grad, *scratch)


def main_backward(cotangent, weights, shift, mix, out, *scratch):
    main_body(False, cotangent, None, weights, shift, mix, out, None, *scratch, None)


def edge_sizes(rows):
    block = rows // BLOCKS
    strips = block + 2 * HALO
    top = strips + 6
    bottom = top + BAND + 5
    return block, top, bottom, -(-(bottom + BAND + 5) // 8) * 8


def edge_kernel(is_last, strips_in, top_rows, bottom_rows, north, south, mix_f, mix_b, grad_main,
                out_f, out_b, grad, term_a, term_b, kept_f, kept_b, coef, wide):
    channels = mix_f.shape[0]
    order = mix_f.shape[1] // channels
    block = strips_in.shape[0]
    top, bottom, total = edge_sizes(block * BLOCKS)[1:]
    strip_count = block + 2 * HALO
    zero_guards((term_a, term_b), coef, total,
                ((0, 1), (1 + strip_count, top + 1), (top + 1 + BAND, bottom + 1), (bottom + 1 + BAND, total)))
    wide[...] = jnp.zeros(wide.shape, F32)

    def put(index, tile):
        wide_tile = tile[2 * channels:PACKED].astype(F32)
        start = index * 8
        start = start if isinstance(start, int) else pl.multiple_of(start, 8)
        wide[pl.ds(start, 8), :] = wide_tile[:8]
        term_a[index] = tile[:2 * channels].astype(F32)
        kept_f[index, 0:channels, :] = tile[:channels]
        kept_b[index, 0:channels, :] = tile[channels:2 * channels]

    def copy_strips(i, _):
        for j in range(4):
            put(1 + HALO + i * 4 + j, strips_in[i * 4 + j])
        return 0

    lax.fori_loop(0, block // 4, copy_strips, 0)
    lane = lane_index((PACKED, LANES))
    for i in range(HALO):
        at_end = i == HALO - 1
        above = turned(strips_in[block - HALO + i], GROUP)
        corner = turned(north[HALO + at_end], 0 if at_end else -GROUP * i)
        put(1 + i, jnp.where(lane < GROUP, corner, above))
        below = turned(strips_in[i], -GROUP)
        corner = turned(south[HALO + at_end], -GROUP - (0 if at_end else GROUP * i))
        put(1 + HALO + block + i, jnp.where(lane >= LANES - GROUP, corner, below))
        put(top + 1 + i, north[i])
        put(bottom + 1 + 2 * HALO + i, south[i])
    for i in range(2 * HALO):
        put(top + 1 + HALO + i, top_rows[i])
        put(bottom + 1 + i, bottom_rows[i])

    w_east, w_south, w_diag, parity = [wide[pl.ds(i, total, stride=8), :] for i in range(4)]
    row = lax.broadcasted_iota(jnp.int32, (total, LANES), 0)
    lane = lane_index((total, LANES))
    edge = (row == bottom + 2 * HALO) | ((row == HALO + block) & (lane >= LANES - GROUP))
    keep = jnp.where(edge & (is_last[0] == 1), 0.0, 1.0).astype(F32)
    write_coefficients(total, 0, w_east, w_south, w_diag, parity, keep, coef, wide)
    stencil_steps(order, 2 * channels, total, coef, (term_a, term_b), (kept_f, kept_b),
                  (((0,), strip_count), ((top, bottom), BAND)))

    lane = lane_index((channels, 2 * LANES)) % LANES
    lane_in = lane % GROUP
    strip_valid = ((lane_in >= 5) & (lane_in < 10)) | ((lane_in >= SIDE + 6) & (lane_in < SIDE + 11))
    main_valid = (lane >= HALO) & (lane < LANES - HALO)
    mixed_f, mixed_b = mix_f[...], mix_b[...]

    def products(places, valid, total_grad):
        for first, second, slot in places:
            for mixed, kept, out in ((mixed_f, kept_f, out_f), (mixed_b, kept_b, out_b)):
                terms = jnp.concatenate([kept[first], kept[second]], axis=1)
                value = jnp.dot(mixed, terms, preferred_element_type=F32).astype(BF16)
                out[slot] = value[:, :LANES]
                out[slot + 1] = value[:, LANES:]
            left = jnp.concatenate([kept_b[first, 0:channels, :], kept_b[second, 0:channels, :]], axis=1)
            left = jnp.where(valid, left, jnp.zeros_like(left))
            terms = jnp.concatenate([kept_f[first], kept_f[second]], axis=1)
            total_grad = total_grad + lax.dot_general(left, terms, CONTRACT_LANES, preferred_element_type=F32)
        return total_grad

    def strip_pairs(i, total_grad):
        places = [(1 + HALO + i * 8 + 2 * j, 2 + HALO + i * 8 + 2 * j, i * 8 + 2 * j) for j in range(4)]
        return products(places, strip_valid, total_grad)

    total_grad = lax.fori_loop(0, block // 8, strip_pairs, grad_main[...])
    indices = [top + 1 + HALO + i for i in range(HALO)] + [bottom + 1 + HALO + i for i in range(HALO)]
    places = [(indices[2 * i], indices[2 * i + 1], block + 2 * i) for i in range(HALO)]
    grad[...] = products(places, main_valid, total_grad)


def assemble_kernel(main_f, main_b, edge_f, edge_b, out_f, out_b, wide):
    rows, channels, _ = main_f.shape
    block = rows // BLOCKS
    lane = lane_index((channels, LANES))
    for main, edges, out in ((main_f, edge_f, out_f), (main_b, edge_b, out_b)):
        def put(r, s, b, value):
            strip = edges[s]
            west = turned(strip, -(GROUP * b + 5))
            east = turned(strip, LANES - 5 - (GROUP * b + SIDE + 6))
            value = jnp.where(lane < HALO, west, jnp.where(lane >= LANES - HALO, east, value))
            wide[pl.ds(r, channels, stride=rows), :] = value.astype(F32)

        for b in range(BLOCKS):
            def several(i, _, b=b):
                for j in range(4):
                    s = i * 4 + j
                    put(block * b + s, s, b, main[block * b + s])
                return 0
            lax.fori_loop(0, block // 4, several, 0)
        for i in range(HALO):
            put(i, i, 0, edges[block + i])
            put(rows - HALO + i, block - HALO + i, BLOCKS - 1, edges[block + HALO + i])

        def narrow(i, _):
            for j in range(4):
                o = i * 4 + j
                out[o] = wide[pl.ds(pl.multiple_of(o * rows, 8), rows), :].astype(BF16)
            return 0

        lax.fori_loop(0, channels // 4, narrow, 0)


def on_device(signal, cotangent, edge_weights, circle_shift, mixing):
    channels, rows, sector = signal.shape
    order = mixing.shape[0]
    block, top, bottom, edge_total = edge_sizes(rows)
    lat, lon = lax.axis_size("lat"), lax.axis_size("lon")
    vmem = pl.BlockSpec(memory_space=pltpu.VMEM)
    smem = pl.BlockSpec(memory_space=pltpu.SMEM)
    shape = jax.ShapeDtypeStruct

    def packed(count):
        return shape((count, PACKED, LANES), BF16)

    all_wide = pltpu.VMEM(((2 * channels + 8) * rows, LANES), F32)
    raw = (signal, cotangent, edge_weights, circle_shift)
    to_west, to_east = pl.pallas_call(
        pack_kernel,
        out_shape=(packed(block // 6), packed(block // 6)),
        in_specs=[vmem, vmem, vmem, smem],
        out_specs=(vmem, vmem),
        scratch_shapes=[all_wide],
        compiler_params=params(16),
        name="pack",
    )(*raw)

    eastward = [(i, (i + 1) % lon) for i in range(lon)]
    westward = [(j, i) for i, j in eastward]
    from_west = lax.ppermute(to_east, "lon", eastward)
    from_east = lax.ppermute(to_west, "lon", westward)

    own_strips, top_rows, bottom_rows = pl.pallas_call(
        own_kernel,
        out_shape=(packed(block), packed(2 * HALO), packed(2 * HALO)),
        in_specs=[vmem, vmem, vmem, smem],
        out_specs=(vmem, vmem, vmem),
        scratch_shapes=[all_wide],
        compiler_params=params(16),
        cost_estimate=pl.CostEstimate(flops=0, bytes_accessed=8 * 1024 * 1024, transcendentals=0),
        name="own",
    )(*raw)

    mix_forward = mixing.transpose(2, 0, 1).reshape(channels, order * channels)
    mix_backward = mixing.transpose(1, 0, 2).reshape(channels, order * channels)
    main_total = rows + 8
    rows_first = shape((rows, channels, LANES), BF16)
    grad_shape = shape((channels, order * channels), F32)
    main_scratch = [
        pltpu.VMEM((channels * rows, LANES), F32),
        pltpu.VMEM((main_total, channels, LANES), F32),
        pltpu.VMEM((main_total, channels, LANES), F32),
        pltpu.VMEM((main_total, order * channels, LANES), BF16),
        pltpu.VMEM((7 * main_total, LANES), F32),
    ]
    heavy = pl.CostEstimate(flops=0, bytes_accessed=24 * 1024 * 1024, transcendentals=0)
    main_f, grad_main = pl.pallas_call(
        main_forward,
        out_shape=(rows_first, grad_shape),
        in_specs=[vmem, vmem, vmem, smem, vmem],
        out_specs=(vmem, vmem),
        scratch_shapes=main_scratch + [pltpu.VMEM((rows, channels, LANES), BF16)],
        compiler_params=params(24),
        cost_estimate=heavy,
        name="main_forward",
    )(*raw, mix_forward)

    strips, to_north, to_south = pl.pallas_call(
        merge_kernel,
        out_shape=(packed(block), packed(HALO + 2), packed(HALO + 2)),
        in_specs=[vmem] * 5,
        out_specs=(vmem,) * 3,
        compiler_params=params(8),
        name="merge",
    )(own_strips, top_rows, bottom_rows, from_west, from_east)

    southward = [(i, i + 1) for i in range(lat - 1)]
    northward = [(j, i) for i, j in southward]
    north = lax.ppermute(to_south, "lat", southward)
    south = lax.ppermute(to_north, "lat", northward)

    main_b = pl.pallas_call(
        main_backward,
        out_shape=rows_first,
        in_specs=[vmem, vmem, smem, vmem],
        out_specs=vmem,
        scratch_shapes=main_scratch,
        compiler_params=params(24),
        cost_estimate=heavy,
        name="main_backward",
    )(cotangent, edge_weights, circle_shift, mix_backward)

    is_last = (lax.axis_index("lat") == lat - 1).astype(jnp.int32).reshape(1)
    edge_out = shape((block + 2 * HALO, channels, LANES), BF16)
    edge_f, edge_b, grad = pl.pallas_call(
        edge_kernel,
        out_shape=(edge_out, edge_out, grad_shape),
        in_specs=[smem] + [vmem] * 8,
        out_specs=(vmem, vmem, vmem),
        scratch_shapes=[
            pltpu.VMEM((edge_total, 2 * channels, LANES), F32),
            pltpu.VMEM((edge_total, 2 * channels, LANES), F32),
            pltpu.VMEM((edge_total, order * channels, LANES), BF16),
            pltpu.VMEM((edge_total, order * channels, LANES), BF16),
            pltpu.VMEM((7 * edge_total, LANES), F32),
            pltpu.VMEM((8 * edge_total + 8, LANES), F32),
        ],
        compiler_params=params(24),
        name="edges",
    )(is_last, strips, top_rows, bottom_rows, north, south, mix_forward, mix_backward, grad_main)

    gathered = lax.all_gather(grad, ("lat", "lon"))
    mapped = shape(signal.shape, BF16)
    output, signal_grad = pl.pallas_call(
        assemble_kernel,
        out_shape=(mapped, mapped),
        in_specs=[vmem] * 4,
        out_specs=(vmem, vmem),
        scratch_shapes=[pltpu.VMEM((channels * rows, LANES), F32)],
        compiler_params=params(16),
        cost_estimate=pl.CostEstimate(flops=0, bytes_accessed=16 * 1024 * 1024, transcendentals=0),
        name="assemble",
    )(main_f, main_b, edge_f, edge_b)
    norm_scale = 1.0 / math.sqrt(rows * lat * sector * lon)
    mixing_grad = gathered.sum(axis=0).T.reshape(order, channels, channels) * norm_scale
    return (output, signal_grad, mixing_grad)


def solution(mesh):
    in_specs = (P(None, "lat", "lon"), P(None, "lat", "lon"), P(None, "lat", "lon"), P("lat"), P())
    out_specs = (P(None, "lat", "lon"), P(None, "lat", "lon"), P())
    return jax.shard_map(
        on_device, mesh=mesh, in_specs=in_specs, out_specs=out_specs, check_vma=False
    )
```

```python
import math

import jax
import jax.numpy as jnp
from jax import lax
from jax.experimental import pallas as pl
from jax.experimental.pallas import tpu as pltpu
from jax.sharding import PartitionSpec as P

F32 = jnp.float32
BF16 = jnp.bfloat16
HALO = 5
LANES = 128
BLOCKS = 4
GROUP = LANES // BLOCKS
SIDE = GROUP // 2
PACKED = 80
BAND = 3 * HALO


def params(mib):
    return pltpu.CompilerParams(vmem_limit_bytes=mib * 1024 * 1024)


def lane_index(shape):
    return lax.broadcasted_iota(jnp.int32, shape, len(shape) - 1)


def turned(x, amount):
    amount = amount % LANES
    return pltpu.roll(x, amount, 1) if amount else x


def spread_size(channels, rows):
    return rows * (3 * channels + 1)


def spread(wide, channels, c, rows, x):
    wide[pl.ds(3 * c, rows, stride=3 * channels + 1), :] = x


def gather(wide, channels, r, first, count):
    return wide[pl.ds(r * (3 * channels + 1) + 3 * first, count, stride=3), :]


def widen_all(signal, cotangent, weights, wide, ready=None):
    channels, rows, _ = signal.shape
    count = 2 * channels + 8
    for i in range(3):
        if ready is not None and i == 0:
            ready(2, 0)
        spread(wide, count, 2 * channels + i, rows, weights[i].astype(F32))
    for i in range(3, 8):
        spread(wide, count, 2 * channels + i, rows, jnp.zeros((rows, LANES), F32))
    for which, source in enumerate((signal, cotangent)):
        for part in range(4):
            if ready is not None:
                ready(which, part)
            size = channels // 4

            def widen(i, _):
                for j in range(4):
                    c = part * size + i * 4 + j
                    spread(wide, count, which * channels + c, rows, source[c].astype(F32))
                return 0

            lax.fori_loop(0, size // 4, widen, 0)


def row_loader(channels, rows, shift, wide):
    count = 2 * channels + 8
    sub = lax.broadcasted_iota(jnp.int32, (8, LANES), 0)

    def load_row(r):
        body = gather(wide, count, r, 0, 2 * channels)
        tail = gather(wide, count, r, 2 * channels, 8)
        parity = jnp.where(shift[r] == 1, 1.0, 0.0).astype(F32)
        tail = jnp.where(sub == 3, parity, tail)
        return jnp.concatenate([body, tail, jnp.zeros((8, LANES), F32)], axis=0).astype(BF16)

    return load_row


def pack_kernel(signal_hbm, cotangent_hbm, weights_hbm, shift, west_out, east_out,
                signal, cotangent, weights, wide, arrived):
    channels, rows, _ = signal.shape
    block = rows // BLOCKS
    per_row = block // 6
    size = channels // 4
    copies = {(2, 0): pltpu.make_async_copy(weights_hbm, weights, arrived.at[8])}
    for which, (source, target) in enumerate(((signal_hbm, signal), (cotangent_hbm, cotangent))):
        for part in range(4):
            span = pl.ds(part * size, size)
            copies[which, part] = pltpu.make_async_copy(source.at[span], target.at[span], arrived.at[4 * which + part])
    for copy in copies.values():
        copy.start()
    widen_all(signal, cotangent, weights, wide, lambda *key: copies[key].wait())
    load_row = row_loader(channels, rows, shift, wide)
    lane = lane_index((PACKED, LANES))

    def each(t, _):
        west = jnp.zeros((PACKED, LANES), BF16)
        east = jnp.zeros((PACKED, LANES), BF16)
        for b in range(BLOCKS):
            for m in range(6):
                x = load_row(block * b + per_row * m + t)
                first = GROUP * b + 5 * m
                moved = turned(x, first + 5)
                east = jnp.where((lane >= first) & (lane < first + 5), moved, east)
                west = jnp.where((lane - (first + 5)) % LANES < 5, moved, west)
        west_out[t] = west
        east_out[t] = east
        return 0

    lax.fori_loop(0, per_row, each, 0)


def own_kernel(signal, cotangent, weights, shift, strips_out, top_out, bottom_out, wide):
    channels, rows, _ = signal.shape
    block = rows // BLOCKS
    widen_all(signal, cotangent, weights, wide)
    load_row = row_loader(channels, rows, shift, wide)
    lane = lane_index((PACKED, LANES))

    def each(s, _):
        strip = jnp.zeros((PACKED, LANES), BF16)
        for b in range(BLOCKS):
            x = load_row(block * b + s)
            west = turned(x, GROUP * b + 5)
            east = turned(x, GROUP * b + SIDE + 11)
            strip = jnp.where((lane >= GROUP * b + 5) & (lane < GROUP * b + SIDE), west, strip)
            strip = jnp.where((lane >= GROUP * b + SIDE) & (lane < GROUP * b + SIDE + 11), east, strip)
        strips_out[s] = strip
        return 0

    lax.fori_loop(0, block, each, 0)
    for i in range(2 * HALO):
        top_out[i] = load_row(i)
        bottom_out[i] = load_row(rows - 2 * HALO + i)


def merge_kernel(strips_in, top, bottom, from_west, from_east, strips_out, north_out, south_out):
    block = strips_in.shape[0]
    per_row = block // 6
    lane = lane_index((PACKED, LANES))
    lane_in = lane % GROUP

    def each(t, _):
        west = from_west[t]
        east = from_east[t]
        for m in range(6):
            strip = strips_in[per_row * m + t]
            strip = jnp.where(lane_in < 5, turned(west, -5 * m), strip)
            strip = jnp.where(lane_in >= GROUP - 5, turned(east, 22 - 5 * m), strip)
            strips_out[per_row * m + t] = strip
        return 0

    lax.fori_loop(0, per_row, each, 0)
    for out, rows_from, first_row, first_strip, side in (
        (north_out, top, 0, 0, 0), (south_out, bottom, HALO, block - HALO, BLOCKS - 1)):
        for i in range(HALO):
            out[i] = rows_from[first_row + i]
        corner = turned(strips_out[first_strip], -GROUP * side)
        for g in range(1, BLOCKS):
            piece = turned(strips_out[first_strip + g], GROUP * (g - side))
            corner = jnp.where((lane >= GROUP * g) & (lane < GROUP * (g + 1)), piece, corner)
        out[HALO] = corner
        out[HALO + 1] = turned(strips_out[first_strip + HALO - 1], -GROUP * side)


def write_coefficients(total, first, w_east, w_south, w_diag, parity, keep, coef, shifted):
    count = w_east.shape[0]
    w_back = jnp.where(parity > 0.5, turned(w_diag, 1), turned(w_diag, -1))
    w_west = turned(w_east, 1)
    shifted[0:8, :] = jnp.zeros((8, LANES), F32)
    shifted[8:8 + count, :] = w_south + w_back
    degree = w_east + w_west + w_south + w_diag + shifted[7:7 + count, :]
    third = -1.0 / 3.0
    arrays = [degree * (1.0 / 3.0) - 2.0, w_east * third, w_west * third]
    for array in (w_south, w_diag, w_back):
        arrays.append(array * third if keep is None else array * keep * third)
    for i, array in enumerate(arrays + [parity]):
        coef[i * total + first:i * total + first + count, :] = array


def stencil_steps(order, channels, total, coef, buffers, kept, trips, regions):
    groups = channels // 8

    def coef_row(i, at):
        return coef[pl.ds(i * total + at, 8, stride=0), :]

    def step(position, now, older):
        last = position == order - 1

        def load(at, count):
            now_rows = [[now[at + j, 8 * g:8 * g + 8, :] for g in range(groups)] for j in range(count)]
            old_rows = None
            if position > 1:
                old_rows = [[older[at + j, 8 * g:8 * g + 8, :] for g in range(groups)] for j in range(count)]
            coefs = [[coef_row(i, at + j) for i in range(7)] for j in range(count)]
            before = [None] * 3 + [coef_row(i, at - 1) for i in (3, 4)] + [None, coef_row(6, at - 1)]
            return now_rows, old_rows, [before] + coefs

        def compute(loaded, level, down):
            now_rows, old_rows, coefs = loaded
            level, down = list(level), list(down)
            results = []
            above = coefs[0][6] > 0.5
            for j in range(len(now_rows)):
                c, e, w, s, d, back, parity = coefs[j + 1]
                s_above, d_above = coefs[j][3], coefs[j][4]
                here = parity > 0.5
                row = []
                for g in range(groups):
                    v = now_rows[j][g]
                    v_east = pltpu.roll(v, LANES - 1, 1)
                    v_west = pltpu.roll(v, 1, 1)
                    new = level[g] + s_above * v + d_above * jnp.where(above, v_east, v_west)
                    if position == 1:
                        new = new * 0.5
                    row.append(new)
                    level[g] = c * v + e * v_east + w * v_west + down[g]
                    if position > 1:
                        level[g] = level[g] - old_rows[j][g]
                    down[g] = s * v + back * jnp.where(here, v_west, v_east)
                results.append(row)
                above = here
            return results, tuple(level), tuple(down)

        def save(at, results):
            for j, row in enumerate(results):
                if not last:
                    for g in range(groups):
                        older[at + j - 1, 8 * g:8 * g + 8, :] = row[g]
                for h in range(groups // 2):
                    first = channels * position + 16 * h
                    pair = jnp.concatenate([row[2 * h], row[2 * h + 1]], axis=0)
                    kept[at + j - 1, first:first + 16, :] = pair.astype(BF16)

        counts = [-(-(count + 2 - 2 * position) // trips) for _, count in regions]

        def several(trip, carry):
            starts = [base + position + trip * count for (base, _), count in zip(regions, counts)]
            loaded = [load(at, count) for at, count in zip(starts, counts)]
            done = [compute(x, *state) for x, state in zip(loaded, carry)]
            for at, (results, _, _) in zip(starts, done):
                save(at, results)
            return tuple((level, down) for _, level, down in done)

        zeros = tuple(jnp.zeros((8, LANES), F32) for _ in range(groups))
        lax.fori_loop(0, trips, several, tuple((zeros, zeros) for _ in regions))

    for position in range(1, order):
        step(position, buffers[(position - 1) % 2], buffers[position % 2])


def zero_guards(buffers, coef, total, guards):
    for first, end in guards:
        for index in range(first, end):
            for buffer in buffers:
                buffer[index] = jnp.zeros(buffer.shape[1:], F32)
        for i in range(7):
            coef[i * total + first:i * total + end, :] = jnp.zeros((end - first, LANES), F32)


CONTRACT_LANES = (((1,), (1,)), ((), ()))


def side_by_side(tiles):
    return jnp.concatenate(tiles, axis=1)


def main_body(with_grad, field, other, weights, shift, mix, out, grad, wide, term_a, term_b, kept, coef, paired):
    channels, rows, _ = field.shape
    order = mix.shape[1] // channels
    total = term_a.shape[0]

    def widen(source):
        def each(i, _):
            for j in range(4):
                c = i * 4 + j
                spread(wide, channels, c, rows, source[c].astype(F32))
            return 0
        lax.fori_loop(0, channels // 4, each, 0)

    zero_guards((term_a, term_b), coef, total, ((0, 1), (rows + 1, total)))
    for r in range(rows):
        value = jnp.where(shift[r] == 1, 1.0, 0.0).astype(F32)
        wide[r:r + 1, :] = jnp.broadcast_to(value, (1, LANES))
    parity = wide[0:rows, :]
    w_east, w_south, w_diag = [weights[i].astype(F32) for i in range(3)]
    write_coefficients(total, 1, w_east, w_south, w_diag, parity, None, coef, wide)

    if with_grad:
        widen(other)
        lane = lane_index((channels, LANES))
        valid = (lane >= HALO) & (lane < LANES - HALO)

        def pair_rows(i, _):
            for j in range(16):
                r = i * 16 + j
                paired[r] = jnp.where(valid, gather(wide, channels, r, 0, channels), 0.0).astype(BF16)
            return 0

        lax.fori_loop(0, rows // 16, pair_rows, 0)

    widen(field)

    def fill(i, _):
        for j in range(16):
            r = i * 16 + j
            x = gather(wide, channels, r, 0, channels)
            term_a[r + 1] = x
            kept[r + 1, 0:channels, :] = x.astype(BF16)
        return 0

    lax.fori_loop(0, rows // 16, fill, 0)
    stencil_steps(order, channels, total, coef, (term_a, term_b), kept, rows // 16, ((0, rows),))

    mixed = mix[...]

    def products(start, count, total_grad):
        terms = side_by_side([kept[start + 1 + i] for i in range(count)])
        value = jnp.dot(mixed, terms, preferred_element_type=F32).astype(BF16)
        for i in range(count):
            out[start + i] = value[:, LANES * i:LANES * (i + 1)]
        if with_grad:
            left = side_by_side([paired[start + i] for i in range(count)])
            total_grad = total_grad + lax.dot_general(left, terms, CONTRACT_LANES, preferred_element_type=F32)
        return total_grad

    inner = rows - 2 * HALO
    total_grad = jnp.zeros((channels, order * channels), F32) if with_grad else 0
    total_grad = lax.fori_loop(0, inner // 16, lambda i, g: products(HALO + i * 16, 16, g), total_grad)
    if inner % 16:
        total_grad = products(HALO + inner // 16 * 16, inner % 16, total_grad)
    if with_grad:
        grad[...] = total_grad


def main_forward(signal, cotangent, weights, shift, mix, out, grad, *scratch):
    main_body(True, signal, cotangent, weights, shift, mix, out, grad, *scratch)


def main_backward(cotangent, weights, shift, mix, _, out, *scratch):
    main_body(False, cotangent, None, weights, shift, mix, out, None, *scratch, None)


def edge_sizes(rows):
    block = rows // BLOCKS
    strips = block + 2 * HALO
    top = strips + 6
    bottom = top + BAND + 5
    return block, top, bottom, -(-(bottom + BAND + 5) // 8) * 8


def edge_body(first, other, is_last, strips_in, top_rows, bottom_rows, north, south, mix, grad_main,
              out, grad, term_a, term_b, kept, paired, coef, wide):
    channels = mix.shape[0]
    order = mix.shape[1] // channels
    block = strips_in.shape[0]
    top, bottom, total = edge_sizes(block * BLOCKS)[1:]
    strip_count = block + 2 * HALO
    zero_guards((term_a, term_b), coef, total,
                ((0, 1), (1 + strip_count, top + 1), (top + 1 + BAND, bottom + 1), (bottom + 1 + BAND, total)))
    wide[...] = jnp.zeros(wide.shape, F32)

    def put(index, tile):
        wide_tile = tile[PACKED - 16:PACKED].astype(F32)
        start = index * 8
        start = start if isinstance(start, int) else pl.multiple_of(start, 8)
        wide[pl.ds(start, 8), :] = wide_tile[:8]
        field = tile[first:first + channels]
        term_a[index] = field.astype(F32)
        kept[index, 0:channels, :] = field
        if other is not None:
            paired[index] = tile[other:other + channels]

    def copy_strips(i, _):
        for j in range(8):
            put(1 + HALO + i * 8 + j, strips_in[i * 8 + j])
        return 0

    lax.fori_loop(0, block // 8, copy_strips, 0)
    lane = lane_index((PACKED, LANES))
    for i in range(HALO):
        at_end = i == HALO - 1
        above = turned(strips_in[block - HALO + i], GROUP)
        corner = turned(north[HALO + at_end], 0 if at_end else -GROUP * i)
        put(1 + i, jnp.where(lane < GROUP, corner, above))
        below = turned(strips_in[i], -GROUP)
        corner = turned(south[HALO + at_end], -GROUP - (0 if at_end else GROUP * i))
        put(1 + HALO + block + i, jnp.where(lane >= LANES - GROUP, corner, below))
        put(top + 1 + i, north[i])
        put(bottom + 1 + 2 * HALO + i, south[i])
    for i in range(2 * HALO):
        put(top + 1 + HALO + i, top_rows[i])
        put(bottom + 1 + i, bottom_rows[i])

    w_east, w_south, w_diag, parity = [wide[pl.ds(i, total, stride=8), :] for i in range(4)]
    row = lax.broadcasted_iota(jnp.int32, (total, LANES), 0)
    lane = lane_index((total, LANES))
    edge = (row == bottom + 2 * HALO) | ((row == HALO + block) & (lane >= LANES - GROUP))
    keep = jnp.where(edge & (is_last[0] == 1), 0.0, 1.0).astype(F32)
    write_coefficients(total, 0, w_east, w_south, w_diag, parity, keep, coef, wide)
    stencil_steps(order, channels, total, coef, (term_a, term_b), kept, 3,
                  ((0, strip_count), (top, BAND), (bottom, BAND)))

    lane = lane_index((channels, LANES))
    lane_in = lane % GROUP
    strip_valid = ((lane_in >= 5) & (lane_in < 10)) | ((lane_in >= SIDE + 6) & (lane_in < SIDE + 11))
    main_valid = (lane >= HALO) & (lane < LANES - HALO)
    strip_rows = [1 + HALO + i for i in range(block)]
    band_rows = [top + 1 + HALO + i for i in range(HALO)] + [bottom + 1 + HALO + i for i in range(HALO)]
    terms = side_by_side([kept[i] for i in strip_rows + band_rows])
    value = jnp.dot(mix[...], terms, preferred_element_type=F32).astype(BF16)
    for i in range(block + 2 * HALO):
        out[i] = value[:, LANES * i:LANES * (i + 1)]
    if other is not None:
        left = [jnp.where(strip_valid, paired[i], jnp.zeros((), BF16)) for i in strip_rows]
        left += [jnp.where(main_valid, paired[i], jnp.zeros((), BF16)) for i in band_rows]
        grad[...] = grad_main[...] + lax.dot_general(
            side_by_side(left), terms, CONTRACT_LANES, preferred_element_type=F32)


def edge_forward(is_last, strips, top_rows, bottom_rows, north, south, mix, grad_main, out, grad,
                 term_a, term_b, kept, paired, coef, wide):
    edge_body(0, mix.shape[0], is_last, strips, top_rows, bottom_rows, north, south, mix, grad_main, out, grad,
              term_a, term_b, kept, paired, coef, wide)


def edge_backward(is_last, strips, top_rows, bottom_rows, north, south, mix, _, out,
                  term_a, term_b, kept, coef, wide):
    edge_body(mix.shape[0], None, is_last, strips, top_rows, bottom_rows, north, south, mix, None, out, None,
              term_a, term_b, kept, None, coef, wide)


def assemble_kernel(main, edges, out, wide):
    rows, channels, _ = main.shape
    block = rows // BLOCKS
    lane = lane_index((channels, LANES))

    def put(r, s, b, value):
        strip = edges[s]
        west = turned(strip, -(GROUP * b + 5))
        east = turned(strip, LANES - 5 - (GROUP * b + SIDE + 6))
        value = jnp.where(lane < HALO, west, jnp.where(lane >= LANES - HALO, east, value))
        wide[pl.ds(r * (3 * channels + 1), channels, stride=3), :] = value.astype(F32)

    for b in range(BLOCKS):
        def several(i, _, b=b):
            for j in range(8):
                s = i * 8 + j
                put(block * b + s, s, b, main[block * b + s])
            return 0
        lax.fori_loop(0, block // 8, several, 0)
    for i in range(HALO):
        put(i, i, 0, edges[block + i])
        put(rows - HALO + i, block - HALO + i, BLOCKS - 1, edges[block + HALO + i])

    def narrow(i, _):
        for j in range(4):
            o = i * 4 + j
            out[o] = wide[pl.ds(3 * o, rows, stride=3 * channels + 1), :].astype(BF16)
        return 0

    lax.fori_loop(0, channels // 4, narrow, 0)


def summed_over(value, axis):
    devices = lax.axis_size(axis)
    reach = 1
    while reach < devices:
        value = value + lax.ppermute(value, axis, [(i, i ^ reach) for i in range(devices)])
        reach *= 2
    return value


def on_device(signal, cotangent, edge_weights, circle_shift, mixing):
    channels, rows, sector = signal.shape
    order = mixing.shape[0]
    block, top, bottom, edge_total = edge_sizes(rows)
    lat, lon = lax.axis_size("lat"), lax.axis_size("lon")
    vmem = pl.BlockSpec(memory_space=pltpu.VMEM)
    smem = pl.BlockSpec(memory_space=pltpu.SMEM)
    hbm = pl.BlockSpec(memory_space=pltpu.HBM)
    anywhere = pl.BlockSpec(memory_space=pl.ANY)
    shape = jax.ShapeDtypeStruct

    def packed(count):
        return shape((count, PACKED, LANES), BF16)

    def weighs(mib):
        return pl.CostEstimate(flops=0, bytes_accessed=mib * 1024 * 1024, transcendentals=0)

    all_wide = pltpu.VMEM((spread_size(2 * channels + 8, rows), LANES), F32)
    raw = (signal, cotangent, edge_weights, circle_shift)
    to_west, to_east = pl.pallas_call(
        pack_kernel,
        out_shape=(packed(block // 6), packed(block // 6)),
        in_specs=[hbm, hbm, hbm, smem],
        out_specs=(vmem, vmem),
        scratch_shapes=[
            pltpu.VMEM(signal.shape, BF16),
            pltpu.VMEM(signal.shape, BF16),
            pltpu.VMEM(edge_weights.shape, BF16),
            all_wide,
            pltpu.SemaphoreType.DMA((9,)),
        ],
        compiler_params=params(20),
        name="pack",
    )(*raw)

    eastward = [(i, (i + 1) % lon) for i in range(lon)]
    westward = [(j, i) for i, j in eastward]
    from_west = lax.ppermute(to_east, "lon", eastward)
    from_east = lax.ppermute(to_west, "lon", westward)

    own_strips, top_rows, bottom_rows = pl.pallas_call(
        own_kernel,
        out_shape=(packed(block), packed(2 * HALO), packed(2 * HALO)),
        in_specs=[vmem, vmem, vmem, smem],
        out_specs=(vmem, vmem, vmem),
        scratch_shapes=[all_wide],
        compiler_params=params(20),
        cost_estimate=weighs(8),
        name="own",
    )(*raw)

    mix_forward = mixing.transpose(2, 0, 1).reshape(channels, order * channels)
    mix_backward = mixing.transpose(1, 0, 2).reshape(channels, order * channels)
    main_total = rows + 8
    rows_first = shape((rows, channels, LANES), BF16)
    grad_shape = shape((channels, order * channels), F32)
    main_scratch = [
        pltpu.VMEM((spread_size(channels, rows), LANES), F32),
        pltpu.VMEM((main_total, channels, LANES), F32),
        pltpu.VMEM((main_total, channels, LANES), F32),
        pltpu.VMEM((main_total, order * channels, LANES), BF16),
        pltpu.VMEM((7 * main_total, LANES), F32),
    ]
    main_f, grad_main = pl.pallas_call(
        main_forward,
        out_shape=(rows_first, grad_shape),
        in_specs=[vmem, vmem, vmem, smem, vmem],
        out_specs=(vmem, vmem),
        scratch_shapes=main_scratch + [pltpu.VMEM((rows, channels, LANES), BF16)],
        compiler_params=params(24),
        cost_estimate=weighs(24),
        name="main_forward",
    )(*raw, mix_forward)

    strips, to_north, to_south = pl.pallas_call(
        merge_kernel,
        out_shape=(packed(block), packed(HALO + 2), packed(HALO + 2)),
        in_specs=[vmem] * 5,
        out_specs=(vmem,) * 3,
        compiler_params=params(8),
        name="merge",
    )(own_strips, top_rows, bottom_rows, from_west, from_east)

    southward = [(i, i + 1) for i in range(lat - 1)]
    northward = [(j, i) for i, j in southward]
    north = lax.ppermute(to_south, "lat", southward)
    south = lax.ppermute(to_north, "lat", northward)

    is_last = (lax.axis_index("lat") == lat - 1).astype(jnp.int32).reshape(1)
    edge_out = shape((block + 2 * HALO, channels, LANES), BF16)
    edge_inputs = (is_last, strips, top_rows, bottom_rows, north, south)
    edge_specs = [smem] + [vmem] * 6
    edge_terms = [
        pltpu.VMEM((edge_total, channels, LANES), F32),
        pltpu.VMEM((edge_total, channels, LANES), F32),
        pltpu.VMEM((edge_total, order * channels, LANES), BF16),
    ]
    edge_rest = [
        pltpu.VMEM((7 * edge_total, LANES), F32),
        pltpu.VMEM((8 * edge_total + 8, LANES), F32),
    ]
    edge_f, grad = pl.pallas_call(
        edge_forward,
        out_shape=(edge_out, grad_shape),
        in_specs=edge_specs + [vmem],
        out_specs=(vmem, vmem),
        scratch_shapes=edge_terms + [pltpu.VMEM((edge_total, channels, LANES), BF16)] + edge_rest,
        compiler_params=params(16),
        cost_estimate=weighs(12),
        name="edge_forward",
    )(*edge_inputs, mix_forward, grad_main)

    summed = summed_over(summed_over(grad, "lon"), "lat")
    main_b = pl.pallas_call(
        main_backward,
        out_shape=rows_first,
        in_specs=[vmem, vmem, smem, vmem, anywhere],
        out_specs=vmem,
        scratch_shapes=main_scratch,
        compiler_params=params(24),
        cost_estimate=weighs(24),
        name="main_backward",
    )(cotangent, edge_weights, circle_shift, mix_backward, grad)
    edge_b = pl.pallas_call(
        edge_backward,
        out_shape=edge_out,
        in_specs=edge_specs + [anywhere],
        out_specs=vmem,
        scratch_shapes=edge_terms + edge_rest,
        compiler_params=params(16),
        cost_estimate=weighs(12),
        name="edge_backward",
    )(*edge_inputs, mix_backward, grad)

    def assemble(main, edges, name):
        return pl.pallas_call(
            assemble_kernel,
            out_shape=shape(signal.shape, BF16),
            in_specs=[vmem] * 2,
            out_specs=vmem,
            scratch_shapes=[pltpu.VMEM((spread_size(channels, rows), LANES), F32)],
            compiler_params=params(12),
            cost_estimate=weighs(8),
            name=name,
        )(main, edges)

    output = assemble(main_f, edge_f, "assemble_forward")
    signal_grad = assemble(main_b, edge_b, "assemble_backward")
    norm_scale = 1.0 / math.sqrt(rows * lat * sector * lon)
    mixing_grad = summed.T.reshape(order, channels, channels) * norm_scale
    return (output, signal_grad, mixing_grad)


def solution(mesh):
    in_specs = (P(None, "lat", "lon"), P(None, "lat", "lon"), P(None, "lat", "lon"), P("lat"), P())
    out_specs = (P(None, "lat", "lon"), P(None, "lat", "lon"), P())
    return jax.shard_map(
        on_device, mesh=mesh, in_specs=in_specs, out_specs=out_specs, check_vma=False
    )
```

```python
import functools
import math

import jax
import jax.numpy as jnp
from jax import lax
from jax.experimental import pallas as pl
from jax.experimental.pallas import tpu as pltpu
from jax.sharding import PartitionSpec as P

F32 = jnp.float32
BF16 = jnp.bfloat16
HALO = 5
LANES = 128
BLOCKS = 4
GROUP = LANES // BLOCKS
SIDE = GROUP // 2
PACKED = 80
BAND = 3 * HALO
PACK_VMEM = 63_400_000


def params(mib):
    return pltpu.CompilerParams(vmem_limit_bytes=mib * 1024 * 1024)


def lane_index(shape):
    return lax.broadcasted_iota(jnp.int32, shape, len(shape) - 1)


def turned(x, amount):
    amount = amount % LANES
    return pltpu.roll(x, amount, 1) if amount else x


def spread_size(channels, rows):
    return rows * (3 * channels + 1)


def spread(wide, channels, c, rows, x):
    wide[pl.ds(3 * c, rows, stride=3 * channels + 1), :] = x


def gather(wide, channels, r, first, count):
    return wide[pl.ds(r * (3 * channels + 1) + 3 * first, count, stride=3), :]


def widen_all(signal, cotangent, weights, wide, ready=None):
    channels, rows, _ = signal.shape
    count = 2 * channels + 8
    for i in range(3):
        if ready is not None and i == 0:
            ready(2, 0)
        spread(wide, count, 2 * channels + i, rows, weights[i].astype(F32))
    for i in range(3, 8):
        spread(wide, count, 2 * channels + i, rows, jnp.zeros((rows, LANES), F32))
    for which, source in enumerate((signal, cotangent)):
        for part in range(4):
            if ready is not None:
                ready(which, part)
            size = channels // 4

            def widen(i, _):
                for j in range(4):
                    c = part * size + i * 4 + j
                    spread(wide, count, which * channels + c, rows, source[c].astype(F32))
                return 0

            lax.fori_loop(0, size // 4, widen, 0)


def row_loader(channels, rows, shift, wide):
    count = 2 * channels + 8
    sub = lax.broadcasted_iota(jnp.int32, (8, LANES), 0)

    def load_row(r):
        body = gather(wide, count, r, 0, 2 * channels)
        tail = gather(wide, count, r, 2 * channels, 8)
        parity = jnp.where(shift[r] == 1, 1.0, 0.0).astype(F32)
        tail = jnp.where(sub == 3, parity, tail)
        return jnp.concatenate([body, tail, jnp.zeros((8, LANES), F32)], axis=0).astype(BF16)

    return load_row


def pack_kernel(signal_hbm, cotangent_hbm, weights_hbm, shift, west_out, east_out,
                signal, cotangent, weights, wide, arrived):
    channels, rows, _ = signal.shape
    block = rows // BLOCKS
    per_row = block // 6
    size = channels // 4
    copies = {(2, 0): pltpu.make_async_copy(weights_hbm, weights, arrived.at[8])}
    for which, (source, target) in enumerate(((signal_hbm, signal), (cotangent_hbm, cotangent))):
        for part in range(4):
            span = pl.ds(part * size, size)
            copies[which, part] = pltpu.make_async_copy(source.at[span], target.at[span], arrived.at[4 * which + part])
    for copy in copies.values():
        copy.start()
    widen_all(signal, cotangent, weights, wide, lambda *key: copies[key].wait())
    load_row = row_loader(channels, rows, shift, wide)
    lane = lane_index((PACKED, LANES))

    def each(t, _):
        west = jnp.zeros((PACKED, LANES), BF16)
        east = jnp.zeros((PACKED, LANES), BF16)
        for b in range(BLOCKS):
            for m in range(6):
                x = load_row(block * b + per_row * m + t)
                first = GROUP * b + 5 * m
                moved = turned(x, first + 5)
                east = jnp.where((lane >= first) & (lane < first + 5), moved, east)
                west = jnp.where((lane - (first + 5)) % LANES < 5, moved, west)
        west_out[t] = west
        east_out[t] = east
        return 0

    lax.fori_loop(0, per_row, each, 0)


def own_kernel(signal, cotangent, weights, shift, strips_out, rows_out, wide):
    channels, rows, _ = signal.shape
    block = rows // BLOCKS
    widen_all(signal, cotangent, weights, wide)
    load_row = row_loader(channels, rows, shift, wide)
    lane = lane_index((PACKED, LANES))

    def each(i, _):
        for j in range(2):
            s = i * 2 + j
            strip = jnp.zeros((PACKED, LANES), BF16)
            for b in range(BLOCKS):
                x = load_row(block * b + s)
                rows_out[block * b + s] = x
                west = turned(x, GROUP * b + 5)
                east = turned(x, GROUP * b + SIDE + 11)
                strip = jnp.where((lane >= GROUP * b + 5) & (lane < GROUP * b + SIDE), west, strip)
                strip = jnp.where((lane >= GROUP * b + SIDE) & (lane < GROUP * b + SIDE + 11), east, strip)
            strips_out[s] = strip
        return 0

    lax.fori_loop(0, block // 2, each, 0)


def merge_kernel(strips_in, rows_in, from_west, from_east, strips_out, north_out, south_out):
    block = strips_in.shape[0]
    rows = rows_in.shape[0]
    per_row = block // 6
    lane = lane_index((PACKED, LANES))
    lane_in = lane % GROUP

    def each(t, _):
        west = from_west[t]
        east = from_east[t]
        for m in range(6):
            strip = strips_in[per_row * m + t]
            strip = jnp.where(lane_in < 5, turned(west, -5 * m), strip)
            strip = jnp.where(lane_in >= GROUP - 5, turned(east, 22 - 5 * m), strip)
            strips_out[per_row * m + t] = strip
        return 0

    lax.fori_loop(0, per_row, each, 0)
    for out, first_row, first_strip, side in (
        (north_out, 0, 0, 0), (south_out, rows - HALO, block - HALO, BLOCKS - 1)):
        for i in range(HALO):
            out[i] = rows_in[first_row + i]
        corner = turned(strips_out[first_strip], -GROUP * side)
        for g in range(1, BLOCKS):
            piece = turned(strips_out[first_strip + g], GROUP * (g - side))
            corner = jnp.where((lane >= GROUP * g) & (lane < GROUP * (g + 1)), piece, corner)
        out[HALO] = corner
        out[HALO + 1] = turned(strips_out[first_strip + HALO - 1], -GROUP * side)


def write_coefficients(total, first, w_east, w_south, w_diag, parity, keep, coef, shifted):
    count = w_east.shape[0]
    w_back = jnp.where(parity > 0.5, turned(w_diag, 1), turned(w_diag, -1))
    w_west = turned(w_east, 1)
    shifted[0:8, :] = jnp.zeros((8, LANES), F32)
    shifted[8:8 + count, :] = w_south + w_back
    degree = w_east + w_west + w_south + w_diag + shifted[7:7 + count, :]
    third = -1.0 / 3.0
    arrays = [degree * (1.0 / 3.0) - 2.0, w_east * third, w_west * third]
    for array in (w_south, w_diag, w_back):
        arrays.append(array * third if keep is None else array * keep * third)
    for i, array in enumerate(arrays + [parity]):
        coef[i * total + first:i * total + first + count, :] = array


def stencil_steps(order, channels, total, coef, buffers, kept, trips, regions):
    groups = channels // 8

    def coef_row(i, at):
        return coef[pl.ds(i * total + at, 8, stride=0), :]

    def step(position, now, older):
        last = position == order - 1

        def load(at, count):
            now_rows = [[now[at + j, 8 * g:8 * g + 8, :] for g in range(groups)] for j in range(count)]
            old_rows = None
            if position > 1:
                old_rows = [[older[at + j, 8 * g:8 * g + 8, :] for g in range(groups)] for j in range(count)]
            coefs = [[coef_row(i, at + j) for i in range(7)] for j in range(count)]
            before = [None] * 3 + [coef_row(i, at - 1) for i in (3, 4)] + [None, coef_row(6, at - 1)]
            return now_rows, old_rows, [before] + coefs

        def compute(loaded, level, down):
            now_rows, old_rows, coefs = loaded
            level, down = list(level), list(down)
            results = []
            above = coefs[0][6] > 0.5
            for j in range(len(now_rows)):
                c, e, w, s, d, back, parity = coefs[j + 1]
                s_above, d_above = coefs[j][3], coefs[j][4]
                here = parity > 0.5
                row = []
                for g in range(groups):
                    v = now_rows[j][g]
                    v_east = pltpu.roll(v, LANES - 1, 1)
                    v_west = pltpu.roll(v, 1, 1)
                    new = level[g] + s_above * v + d_above * jnp.where(above, v_east, v_west)
                    if position == 1:
                        new = new * 0.5
                    row.append(new)
                    level[g] = c * v + e * v_east + w * v_west + down[g]
                    if position > 1:
                        level[g] = level[g] - old_rows[j][g]
                    down[g] = s * v + back * jnp.where(here, v_west, v_east)
                results.append(row)
                above = here
            return results, tuple(level), tuple(down)

        def save(at, results):
            for j, row in enumerate(results):
                if not last:
                    for g in range(groups):
                        older[at + j - 1, 8 * g:8 * g + 8, :] = row[g]
                for h in range(groups // 2):
                    first = channels * position + 16 * h
                    pair = jnp.concatenate([row[2 * h], row[2 * h + 1]], axis=0)
                    kept[at + j - 1, first:first + 16, :] = pair.astype(BF16)

        counts = [-(-(count + 2 - 2 * position) // trips) for _, count in regions]

        def several(trip, carry):
            starts = [base + position + trip * count for (base, _), count in zip(regions, counts)]
            loaded = [load(at, count) for at, count in zip(starts, counts)]
            done = [compute(x, *state) for x, state in zip(loaded, carry)]
            for at, (results, _, _) in zip(starts, done):
                save(at, results)
            return tuple((level, down) for _, level, down in done)

        zeros = tuple(jnp.zeros((8, LANES), F32) for _ in range(groups))
        lax.fori_loop(0, trips, several, tuple((zeros, zeros) for _ in regions))

    for position in range(1, order):
        step(position, buffers[(position - 1) % 2], buffers[position % 2])


def zero_guards(buffers, coef, total, guards):
    for first, end in guards:
        for index in range(first, end):
            for buffer in buffers:
                buffer[index] = jnp.zeros(buffer.shape[1:], F32)
        for i in range(7):
            coef[i * total + first:i * total + end, :] = jnp.zeros((end - first, LANES), F32)


CONTRACT_LANES = (((1,), (1,)), ((), ()))
CONTRACT_ROWS = (((0,), (0,)), ((), ()))


def side_by_side(tiles):
    return jnp.concatenate(tiles, axis=1)


class Chain:
    def __init__(self, first, other, mixing, guards, scratch):
        self.term_a, self.term_b, self.kept, self.coef, self.wide = scratch[:5]
        self.paired = scratch[5] if other is not None else None
        self.first, self.other, self.mixing = first, other, mixing
        self.order, self.channels = mixing.shape[:2]
        self.total = self.term_a.shape[0]
        zero_guards((self.term_a, self.term_b), self.coef, self.total, guards)
        for begin, end in guards:
            self.wide[8 * begin:8 * end, :] = jnp.zeros((8 * (end - begin), LANES), F32)

    def put(self, index, ref, at, tile=None):
        def part(begin, count):
            return ref[at, begin:begin + count, :] if tile is None else tile[begin:begin + count]
        start = index * 8
        start = start if isinstance(start, int) else pl.multiple_of(start, 8)
        self.wide[pl.ds(start, 8), :] = part(PACKED - 16, 16).astype(F32)[:8]
        field = part(self.first, self.channels)
        self.term_a[index] = field.astype(F32)
        self.kept[index, 0:self.channels, :] = field
        if self.other is not None:
            self.paired[index] = part(self.other, self.channels)

    def put_all(self, index, ref, unroll):
        count = ref.shape[0]

        def several(i, _):
            for j in range(unroll):
                self.put(index + i * unroll + j, ref, i * unroll + j)
            return 0

        lax.fori_loop(0, count // unroll, several, 0)

    def put_strips(self, strips, north, south):
        block = strips.shape[0]
        self.put_all(1 + HALO, strips, 8)
        lane = lane_index((PACKED, LANES))
        for i in range(HALO):
            at_end = i == HALO - 1
            above = turned(strips[block - HALO + i], GROUP)
            corner = turned(north[HALO + at_end], 0 if at_end else -GROUP * i)
            self.put(1 + i, None, None, jnp.where(lane < GROUP, corner, above))
            below = turned(strips[i], -GROUP)
            corner = turned(south[HALO + at_end], -GROUP - (0 if at_end else GROUP * i))
            self.put(1 + HALO + block + i, None, None, jnp.where(lane >= LANES - GROUP, corner, below))

    def run(self, trips, regions, closed=None):
        total = self.total
        w_east, w_south, w_diag, parity = [self.wide[pl.ds(i, total, stride=8), :] for i in range(4)]
        keep = None
        if closed is not None:
            is_end, where = closed
            row = lax.broadcasted_iota(jnp.int32, (total, LANES), 0)
            keep = jnp.where(where(row, lane_index((total, LANES))) & is_end, 0.0, 1.0).astype(F32)
        write_coefficients(total, 0, w_east, w_south, w_diag, parity, keep, self.coef, self.wide)
        stencil_steps(self.order, self.channels, total, self.coef, (self.term_a, self.term_b), self.kept, trips, regions)

    def terms(self, indices):
        return side_by_side([self.kept[i] for i in indices])

    def mixed(self, terms):
        if self.other is not None:
            matrix = self.mixing[...].reshape(self.order * self.channels, self.channels)
            value = lax.dot_general(matrix, terms, CONTRACT_ROWS, preferred_element_type=F32)
        else:
            matrix = side_by_side([self.mixing[k] for k in range(self.order)])
            value = jnp.dot(matrix, terms, preferred_element_type=F32)
        return value.astype(BF16)

    def paired_with(self, indices, valid, terms):
        left = [jnp.where(valid, self.paired[i], jnp.zeros((), BF16)) for i in indices]
        return lax.dot_general(side_by_side(left), terms, CONTRACT_LANES, preferred_element_type=F32)


def valid_lanes(channels):
    lane = lane_index((channels, LANES))
    lane_in = lane % GROUP
    in_strips = ((lane_in >= 5) & (lane_in < 10)) | ((lane_in >= SIDE + 6) & (lane_in < SIDE + 11))
    return (lane >= HALO) & (lane < LANES - HALO), in_strips


def main_forward(rows_in, mixing, out, grad, *scratch):
    rows = rows_in.shape[0]
    order, channels = mixing.shape[:2]
    chain = Chain(0, channels, mixing, ((0, 1), (rows + 1, rows + 8)), scratch)
    chain.put_all(1, rows_in, 16)
    chain.run(rows // 16, ((0, rows),))
    valid, _ = valid_lanes(channels)

    def products(start, count, total_grad):
        indices = [start + 1 + i for i in range(count)]
        terms = chain.terms(indices)
        value = chain.mixed(terms)
        for i in range(count):
            out[start + i] = value[:, LANES * i:LANES * (i + 1)]
        return total_grad + chain.paired_with(indices, valid, terms)

    inner = rows - 2 * HALO
    total_grad = jnp.zeros(grad.shape, F32)
    total_grad = lax.fori_loop(0, inner // 16, lambda i, g: products(HALO + i * 16, 16, g), total_grad)
    if inner % 16:
        total_grad = products(HALO + inner // 16 * 16, inner % 16, total_grad)
    grad[...] = total_grad


def main_backward(is_last, rows_in, north, south, mixing, summed, out, summed_out, *scratch):
    rows = rows_in.shape[0]
    channels = mixing.shape[1]
    count = rows + 2 * HALO
    chain = Chain(channels, None, mixing, ((0, 1), (count + 1, scratch[0].shape[0])), scratch)
    for i in range(HALO):
        chain.put(1 + i, north, i)
        chain.put(1 + HALO + rows + i, south, i)
    chain.put_all(1 + HALO, rows_in, 16)
    chain.run(7, ((0, count),), (is_last[0] == 1, lambda row, lane: row == HALO + rows))

    def products(i, _):
        value = chain.mixed(chain.terms([1 + HALO + i * 16 + j for j in range(16)]))
        for j in range(16):
            out[i * 16 + j] = value[:, LANES * j:LANES * (j + 1)]
        return 0

    lax.fori_loop(0, rows // 16, products, 0)
    summed_out[...] = summed[...]


def edge_sizes(rows):
    block = rows // BLOCKS
    strips = block + 2 * HALO
    top = strips + 6
    bottom = top + BAND + 5
    return block, top, bottom, -(-(bottom + BAND + 5) // 8) * 8


def edge_forward(is_last, strips_in, rows_in, north, south, mixing, grad_main, out, grad, *scratch):
    rows = rows_in.shape[0]
    block, top, bottom, total = edge_sizes(rows)
    channels = mixing.shape[1]
    count = block + 2 * HALO
    chain = Chain(0, channels, mixing, ((0, 1), (1 + count, top + 1), (top + 1 + BAND, bottom + 1),
                                        (bottom + 1 + BAND, total)), scratch)
    chain.put_strips(strips_in, north, south)
    for i in range(HALO):
        chain.put(top + 1 + i, north, i)
        chain.put(bottom + 1 + 2 * HALO + i, south, i)
    for i in range(2 * HALO):
        chain.put(top + 1 + HALO + i, rows_in, i)
        chain.put(bottom + 1 + i, rows_in, rows - 2 * HALO + i)

    def closed(row, lane):
        return (row == bottom + 2 * HALO) | ((row == HALO + block) & (lane >= LANES - GROUP))

    chain.run(3, ((0, count), (top, BAND), (bottom, BAND)), (is_last[0] == 1, closed))
    main_valid, strip_valid = valid_lanes(channels)
    strip_rows = [1 + HALO + i for i in range(block)]
    band_rows = [top + 1 + HALO + i for i in range(HALO)] + [bottom + 1 + HALO + i for i in range(HALO)]
    total_grad = grad_main[...]
    slot = 0
    for indices, valid in ((strip_rows, strip_valid), (band_rows, main_valid)):
        terms = chain.terms(indices)
        value = chain.mixed(terms)
        for i in range(len(indices)):
            out[slot + i] = value[:, LANES * i:LANES * (i + 1)]
        slot += len(indices)
        total_grad = total_grad + chain.paired_with(indices, valid, terms)
    grad[...] = total_grad


def edge_backward(is_last, strips_in, north, south, mixing, summed, out, summed_out, *scratch):
    block = strips_in.shape[0]
    count = block + 2 * HALO
    chain = Chain(mixing.shape[1], None, mixing, ((0, 1), (1 + count, scratch[0].shape[0])), scratch)
    chain.put_strips(strips_in, north, south)
    chain.run(2, ((0, count),), (is_last[0] == 1, lambda row, lane: (row == HALO + block) & (lane >= LANES - GROUP)))
    value = chain.mixed(chain.terms([1 + HALO + i for i in range(block)]))
    for i in range(block):
        out[i] = value[:, LANES * i:LANES * (i + 1)]
    summed_out[...] = summed[...]


def assemble_kernel(main, edges, summed, out, summed_out, wide):
    summed_out[...] = summed[...]
    rows, channels, _ = main.shape
    block = rows // BLOCKS
    lane = lane_index((channels, LANES))

    def put(r, s, b, value):
        strip = edges[s]
        west = turned(strip, -(GROUP * b + 5))
        east = turned(strip, LANES - 5 - (GROUP * b + SIDE + 6))
        value = jnp.where(lane < HALO, west, jnp.where(lane >= LANES - HALO, east, value))
        wide[pl.ds(r * (3 * channels + 1), channels, stride=3), :] = value.astype(F32)

    for b in range(BLOCKS):
        def several(i, _, b=b):
            for j in range(8):
                s = i * 8 + j
                put(block * b + s, s, b, main[block * b + s])
            return 0
        lax.fori_loop(0, block // 8, several, 0)
    if edges.shape[0] > block:
        for i in range(HALO):
            put(i, i, 0, edges[block + i])
            put(rows - HALO + i, block - HALO + i, BLOCKS - 1, edges[block + HALO + i])

    def narrow(i, _):
        for j in range(4):
            o = i * 4 + j
            out[o] = wide[pl.ds(3 * o, rows, stride=3 * channels + 1), :].astype(BF16)
        return 0

    lax.fori_loop(0, channels // 4, narrow, 0)


def finish_kernel(scale, mine, theirs, out):
    order, channels = out.shape[:2]
    out[...] = ((mine[...] + theirs[...]) * scale).T.reshape(order, channels, channels)


def on_device(signal, cotangent, edge_weights, circle_shift, mixing):
    channels, rows, sector = signal.shape
    order = mixing.shape[0]
    block, top, bottom, edge_total = edge_sizes(rows)
    lat, lon = lax.axis_size("lat"), lax.axis_size("lon")
    vmem = pl.BlockSpec(memory_space=pltpu.VMEM)
    smem = pl.BlockSpec(memory_space=pltpu.SMEM)
    hbm = pl.BlockSpec(memory_space=pltpu.HBM)
    shape = jax.ShapeDtypeStruct

    def packed(count):
        return shape((count, PACKED, LANES), BF16)

    def weighs(mib):
        return pl.CostEstimate(flops=0, bytes_accessed=mib * 1024 * 1024, transcendentals=0)

    all_wide = pltpu.VMEM((spread_size(2 * channels + 8, rows), LANES), F32)
    raw = (signal, cotangent, edge_weights, circle_shift)
    to_west, to_east = pl.pallas_call(
        pack_kernel,
        out_shape=(packed(block // 6), packed(block // 6)),
        in_specs=[hbm, hbm, hbm, smem],
        out_specs=(vmem, vmem),
        scratch_shapes=[
            pltpu.VMEM(signal.shape, BF16),
            pltpu.VMEM(signal.shape, BF16),
            pltpu.VMEM(edge_weights.shape, BF16),
            all_wide,
            pltpu.SemaphoreType.DMA((9,)),
        ],
        compiler_params=pltpu.CompilerParams(vmem_limit_bytes=PACK_VMEM),
        name="pack",
    )(*raw)

    eastward = [(i, (i + 1) % lon) for i in range(lon)]
    westward = [(j, i) for i, j in eastward]
    from_west = lax.ppermute(to_east, "lon", eastward)
    from_east = lax.ppermute(to_west, "lon", westward)

    own_strips, rows_in = pl.pallas_call(
        own_kernel,
        out_shape=(packed(block), packed(rows)),
        in_specs=[vmem, vmem, vmem, smem],
        out_specs=(vmem, vmem),
        scratch_shapes=[all_wide],
        compiler_params=params(20),
        cost_estimate=weighs(8),
        name="own",
    )(*raw)

    strips, to_north, to_south = pl.pallas_call(
        merge_kernel,
        out_shape=(packed(block), packed(HALO + 2), packed(HALO + 2)),
        in_specs=[vmem] * 4,
        out_specs=(vmem,) * 3,
        compiler_params=params(8),
        name="merge",
    )(own_strips, rows_in, from_west, from_east)

    southward = [(i, i + 1) for i in range(lat - 1)]
    northward = [(j, i) for i, j in southward]
    north = lax.ppermute(to_south, "lat", southward)
    south = lax.ppermute(to_north, "lat", northward)

    rows_first = shape((rows, channels, LANES), BF16)
    grad_shape = shape((channels, order * channels), F32)

    def chain_scratch(total, with_pairs):
        scratch = [
            pltpu.VMEM((total, channels, LANES), F32),
            pltpu.VMEM((total, channels, LANES), F32),
            pltpu.VMEM((total, order * channels, LANES), BF16),
            pltpu.VMEM((7 * total, LANES), F32),
            pltpu.VMEM((8 * total + 8, LANES), F32),
        ]
        return scratch + [pltpu.VMEM((total, channels, LANES), BF16)] * with_pairs

    main_f, grad_main = pl.pallas_call(
        main_forward,
        out_shape=(rows_first, grad_shape),
        in_specs=[vmem, vmem],
        out_specs=(vmem, vmem),
        scratch_shapes=chain_scratch(rows + 8, True),
        compiler_params=params(20),
        cost_estimate=weighs(24),
        name="main_forward",
    )(rows_in, mixing)

    is_last = (lax.axis_index("lat") == lat - 1).astype(jnp.int32).reshape(1)
    edge_f, grad = pl.pallas_call(
        edge_forward,
        out_shape=(shape((block + 2 * HALO, channels, LANES), BF16), grad_shape),
        in_specs=[smem] + [vmem] * 6,
        out_specs=(vmem, vmem),
        scratch_shapes=chain_scratch(edge_total, True),
        compiler_params=params(16),
        cost_estimate=weighs(12),
        name="edge_forward",
    )(is_last, strips, rows_in, north, south, mixing, grad_main)

    rounds = []
    for axis, devices in (("lon", lon), ("lat", lat)):
        reach = 1
        while reach < devices:
            rounds.append((axis, [(i, i ^ reach) for i in range(devices)]))
            reach *= 2

    results = {}

    def run_main_backward(share):
        results["main"], share = pl.pallas_call(
            main_backward,
            out_shape=(rows_first, grad_shape),
            in_specs=[smem] + [vmem] * 5,
            out_specs=(vmem, vmem),
            scratch_shapes=chain_scratch(-(-(rows + 2 * HALO + 8) // 8) * 8, False),
            compiler_params=params(20),
            cost_estimate=weighs(24),
            name="main_backward",
        )(is_last, rows_in, north, south, mixing, share)
        return share

    def run_edge_backward(share):
        results["edge"], share = pl.pallas_call(
            edge_backward,
            out_shape=(shape((block, channels, LANES), BF16), grad_shape),
            in_specs=[smem] + [vmem] * 5,
            out_specs=(vmem, vmem),
            scratch_shapes=chain_scratch(-(-(block + 2 * HALO + 8) // 8) * 8, False),
            compiler_params=params(12),
            cost_estimate=weighs(12),
            name="edge_backward",
        )(is_last, strips, north, south, mixing, share)
        return share

    def assemble(main, edges, share, name):
        return pl.pallas_call(
            assemble_kernel,
            out_shape=(shape(signal.shape, BF16), grad_shape),
            in_specs=[vmem] * 3,
            out_specs=(vmem, vmem),
            scratch_shapes=[pltpu.VMEM((spread_size(channels, rows), LANES), F32)],
            compiler_params=params(12),
            cost_estimate=weighs(8),
            name=name,
        )(main, edges, share)

    def run_assemble_forward(share):
        results["output"], share = assemble(main_f, edge_f, share, "assemble_forward")
        return share

    def run_assemble_backward(share):
        results["signal_grad"], share = assemble(results["main"], results["edge"], share, "assemble_backward")
        return share

    beside = [run_main_backward, run_assemble_forward, run_edge_backward, run_assemble_backward]
    share = grad
    theirs = jnp.zeros_like(grad)
    for number in range(max(len(rounds), len(beside))):
        if number:
            share = share + theirs
        theirs = lax.ppermute(share, *rounds[number]) if number < len(rounds) else jnp.zeros_like(grad)
        if number < len(beside):
            share = beside[number](share)

    norm_scale = 1.0 / math.sqrt(rows * lat * sector * lon)
    mixing_grad = pl.pallas_call(
        functools.partial(finish_kernel, norm_scale),
        out_shape=shape(mixing.shape, F32),
        in_specs=[vmem, vmem],
        out_specs=vmem,
        name="finish",
    )(share, theirs)
    return (results["output"], results["signal_grad"], mixing_grad)


def solution(mesh):
    in_specs = (P(None, "lat", "lon"), P(None, "lat", "lon"), P(None, "lat", "lon"), P("lat"), P())
    out_specs = (P(None, "lat", "lon"), P(None, "lat", "lon"), P())
    return jax.shard_map(
        on_device, mesh=mesh, in_specs=in_specs, out_specs=out_specs, check_vma=False
    )
```

```python
import functools
import math

import jax
import jax.numpy as jnp
from jax import lax
from jax.experimental import pallas as pl
from jax.experimental.pallas import tpu as pltpu
from jax.sharding import PartitionSpec as P

F32 = jnp.float32
BF16 = jnp.bfloat16
HALO = 5
LANES = 128
BLOCKS = 4
GROUP = LANES // BLOCKS
SIDE = GROUP // 2
PACKED = 80
BAND = 3 * HALO
PACK_VMEM = 63_400_000


def params(mib):
    return pltpu.CompilerParams(vmem_limit_bytes=mib * 1024 * 1024)


def lane_index(shape):
    return lax.broadcasted_iota(jnp.int32, shape, len(shape) - 1)


def turned(x, amount):
    amount = amount % LANES
    return pltpu.roll(x, amount, 1) if amount else x


def spread_size(channels, rows):
    return rows * (3 * channels + 1)


def spread(wide, channels, c, rows, x):
    wide[pl.ds(3 * c, rows, stride=3 * channels + 1), :] = x


def gather(wide, channels, r, first, count):
    return wide[pl.ds(r * (3 * channels + 1) + 3 * first, count, stride=3), :]


def widen_all(signal, cotangent, weights, wide, ready=None):
    channels, rows, _ = signal.shape
    count = 2 * channels + 8
    for i in range(3):
        if ready is not None and i == 0:
            ready(2, 0)
        spread(wide, count, 2 * channels + i, rows, weights[i].astype(F32))
    for i in range(3, 8):
        spread(wide, count, 2 * channels + i, rows, jnp.zeros((rows, LANES), F32))
    for which, source in enumerate((signal, cotangent)):
        for part in range(4):
            if ready is not None:
                ready(which, part)
            size = channels // 4

            def widen(i, _):
                for j in range(4):
                    c = part * size + i * 4 + j
                    spread(wide, count, which * channels + c, rows, source[c].astype(F32))
                return 0

            lax.fori_loop(0, size // 4, widen, 0)


def row_loader(channels, rows, shift, wide):
    count = 2 * channels + 8
    sub = lax.broadcasted_iota(jnp.int32, (8, LANES), 0)

    def load_row(r):
        body = gather(wide, count, r, 0, 2 * channels)
        tail = gather(wide, count, r, 2 * channels, 8)
        parity = jnp.where(shift[r] == 1, 1.0, 0.0).astype(F32)
        tail = jnp.where(sub == 3, parity, tail)
        return jnp.concatenate([body, tail, jnp.zeros((8, LANES), F32)], axis=0).astype(BF16)

    return load_row


def pack_kernel(signal_hbm, cotangent_hbm, weights_hbm, shift, west_out, east_out,
                signal, cotangent, weights, wide, arrived):
    channels, rows, _ = signal.shape
    block = rows // BLOCKS
    per_row = block // 6
    size = channels // 4
    copies = {(2, 0): pltpu.make_async_copy(weights_hbm, weights, arrived.at[8])}
    for which, (source, target) in enumerate(((signal_hbm, signal), (cotangent_hbm, cotangent))):
        for part in range(4):
            span = pl.ds(part * size, size)
            copies[which, part] = pltpu.make_async_copy(source.at[span], target.at[span], arrived.at[4 * which + part])
    for copy in copies.values():
        copy.start()
    widen_all(signal, cotangent, weights, wide, lambda *key: copies[key].wait())
    load_row = row_loader(channels, rows, shift, wide)
    lane = lane_index((PACKED, LANES))

    def each(t, _):
        west = jnp.zeros((PACKED, LANES), BF16)
        east = jnp.zeros((PACKED, LANES), BF16)
        for b in range(BLOCKS):
            for m in range(6):
                x = load_row(block * b + per_row * m + t)
                first = GROUP * b + 5 * m
                moved = turned(x, first + 5)
                east = jnp.where((lane >= first) & (lane < first + 5), moved, east)
                west = jnp.where((lane - (first + 5)) % LANES < 5, moved, west)
        west_out[t] = west
        east_out[t] = east
        return 0

    lax.fori_loop(0, per_row, each, 0)


def own_kernel(signal, cotangent, weights, shift, strips_out, rows_out, wide):
    channels, rows, _ = signal.shape
    block = rows // BLOCKS
    widen_all(signal, cotangent, weights, wide)
    load_row = row_loader(channels, rows, shift, wide)
    lane = lane_index((PACKED, LANES))

    def each(i, _):
        for j in range(2):
            s = i * 2 + j
            strip = jnp.zeros((PACKED, LANES), BF16)
            for b in range(BLOCKS):
                x = load_row(block * b + s)
                rows_out[block * b + s] = x
                west = turned(x, GROUP * b + 5)
                east = turned(x, GROUP * b + SIDE + 11)
                strip = jnp.where((lane >= GROUP * b + 5) & (lane < GROUP * b + SIDE), west, strip)
                strip = jnp.where((lane >= GROUP * b + SIDE) & (lane < GROUP * b + SIDE + 11), east, strip)
            strips_out[s] = strip
        return 0

    lax.fori_loop(0, block // 2, each, 0)


def merge_kernel(strips_in, rows_in, from_west, from_east, strips_out, north_out, south_out):
    block = strips_in.shape[0]
    rows = rows_in.shape[0]
    per_row = block // 6
    lane = lane_index((PACKED, LANES))
    lane_in = lane % GROUP

    def each(t, _):
        west = from_west[t]
        east = from_east[t]
        for m in range(6):
            strip = strips_in[per_row * m + t]
            strip = jnp.where(lane_in < 5, turned(west, -5 * m), strip)
            strip = jnp.where(lane_in >= GROUP - 5, turned(east, 22 - 5 * m), strip)
            strips_out[per_row * m + t] = strip
        return 0

    lax.fori_loop(0, per_row, each, 0)
    for out, first_row, first_strip, side in (
        (north_out, 0, 0, 0), (south_out, rows - HALO, block - HALO, BLOCKS - 1)):
        for i in range(HALO):
            out[i] = rows_in[first_row + i]
        corner = turned(strips_out[first_strip], -GROUP * side)
        for g in range(1, BLOCKS):
            piece = turned(strips_out[first_strip + g], GROUP * (g - side))
            corner = jnp.where((lane >= GROUP * g) & (lane < GROUP * (g + 1)), piece, corner)
        out[HALO] = corner
        out[HALO + 1] = turned(strips_out[first_strip + HALO - 1], -GROUP * side)


def write_coefficients(total, w_east, w_south, w_diag, parity, keep, centre, spread_out, wide):
    w_back = jnp.where(parity > 0.5, turned(w_diag, 1), turned(w_diag, -1))
    w_west = turned(w_east, 1)
    wide[0:8, :] = jnp.zeros((8, LANES), F32)
    wide[8:8 + total, :] = w_south + w_back
    degree = w_east + w_west + w_south + w_diag + wide[7:7 + total, :]
    centre[...] = degree * (1.0 / 3.0) - 2.0
    if keep is not None:
        w_south, w_diag, w_back = w_south * keep, w_diag * keep, w_back * keep
    arrays = (w_east, w_west, w_south, w_diag, w_back, parity)
    for i, array in enumerate(arrays):
        wide[i * total:(i + 1) * total, :] = array

    def several(trip, _):
        for j in range(8):
            row = trip * 8 + j
            for i in range(len(arrays)):
                spread_out[i, row] = wide[pl.ds(i * total + row, 16, stride=0), :].astype(BF16)
        return 0

    lax.fori_loop(0, total // 8, several, 0)


def stencil_steps(order, channels, centre, weights, buffers, kept, trips, regions):
    halves = channels // 16
    row = lax.broadcasted_iota(jnp.int32, (channels, 6 * channels), 0)
    column = lax.broadcasted_iota(jnp.int32, (channels, 6 * channels), 1)
    adder = jnp.where(column % channels == row, 1.0, 0.0).astype(BF16)

    def step(position, now, older):
        first = channels * (position - 1)

        def products(at, count):
            own, up, down = {}, {}, {}
            for j in range(-1, count + 1):
                q = at + j
                east, west, south, diag, back = [weights[i, q] for i in range(5)]
                here = weights[5, q] > 0.5
                if j >= 0:
                    south_above, diag_above = weights[2, q - 1], weights[3, q - 1]
                    above = weights[5, q - 1] > 0.5
                own[j], up[j - 1], down[j + 1] = [], [], []
                for h in range(halves):
                    v = kept[q, first + 16 * h:first + 16 * h + 16, :]
                    v_east = pltpu.roll(v, LANES - 1, 1)
                    v_west = pltpu.roll(v, 1, 1)
                    if 0 <= j < count:
                        own[j].append((east * v_east, west * v_west))
                    if j >= 1:
                        up[j - 1].append((south_above * v, diag_above * jnp.where(above, v_east, v_west)))
                    elif j == 0:
                        pass
                    if j < count - 1:
                        down[j + 1].append((south * v, back * jnp.where(here, v_west, v_east)))
            columns = []
            for j in range(count):
                parts = []
                for group in (own[j], up[j], down[j]):
                    for which in range(2):
                        parts += [group[h][which] for h in range(halves)]
                columns.append(jnp.concatenate(parts, axis=0))
            return columns

        counts = [-(-(count - 2 * position) // trips) for _, count in regions]

        def several(trip, carry):
            places, columns = [], []
            for (base, _), count in zip(regions, counts):
                at = base + 1 + position + trip * count
                places += [at + j for j in range(count)]
                columns += products(at, count)
            total = jnp.dot(adder, side_by_side(columns), preferred_element_type=F32)
            results = []
            for j, at in enumerate(places):
                middle = centre[pl.ds(at, channels, stride=0), :]
                new = middle * now[at] - total[:, LANES * j:LANES * (j + 1)] * (1.0 / 3.0)
                results.append(new * 0.5 if position == 1 else new - older[at])
            for at, new in zip(places, results):
                if position < order - 1:
                    older[at] = new
                kept[at, first + channels:first + 2 * channels, :] = new.astype(BF16)
            return carry

        lax.fori_loop(0, trips, several, 0)

    for position in range(1, order):
        step(position, buffers[(position - 1) % 2], buffers[position % 2])


CONTRACT_LANES = (((1,), (1,)), ((), ()))
CONTRACT_ROWS = (((0,), (0,)), ((), ()))


def side_by_side(tiles):
    return jnp.concatenate(tiles, axis=1)


class Chain:
    def __init__(self, first, other, mixing, guards, scratch):
        self.term_a, self.term_b, self.kept, self.centre, self.weights, self.wide = scratch[:6]
        self.paired = scratch[6] if other is not None else None
        self.first, self.other, self.mixing = first, other, mixing
        self.order, self.channels = mixing.shape[:2]
        self.total = self.term_a.shape[0]
        for begin, end in guards:
            for i in range(4):
                at = i * (self.total + 1)
                self.wide[at + begin:at + end, :] = jnp.zeros((end - begin, LANES), F32)
            for index in range(begin, end):
                self.term_a[index] = jnp.zeros((self.channels, LANES), F32)
                self.term_b[index] = jnp.zeros((self.channels, LANES), F32)
                self.kept[index] = jnp.zeros((self.order * self.channels, LANES), BF16)

    def put(self, index, ref, at, tile=None):
        def part(begin, count):
            return ref[at, begin:begin + count, :] if tile is None else tile[begin:begin + count]
        self.wide[pl.ds(index, 8, stride=self.total + 1), :] = part(PACKED - 16, 16).astype(F32)[:8]
        field = part(self.first, self.channels)
        self.term_a[index] = field.astype(F32)
        self.kept[index, 0:self.channels, :] = field
        if self.other is not None:
            self.paired[index] = part(self.other, self.channels)

    def put_all(self, index, ref, unroll):
        count = ref.shape[0]

        def several(i, _):
            for j in range(unroll):
                self.put(index + i * unroll + j, ref, i * unroll + j)
            return 0

        lax.fori_loop(0, count // unroll, several, 0)

    def put_strips(self, strips, north, south):
        block = strips.shape[0]
        self.put_all(1 + HALO, strips, 8)
        lane = lane_index((PACKED, LANES))
        for i in range(HALO):
            at_end = i == HALO - 1
            above = turned(strips[block - HALO + i], GROUP)
            corner = turned(north[HALO + at_end], 0 if at_end else -GROUP * i)
            self.put(1 + i, None, None, jnp.where(lane < GROUP, corner, above))
            below = turned(strips[i], -GROUP)
            corner = turned(south[HALO + at_end], -GROUP - (0 if at_end else GROUP * i))
            self.put(1 + HALO + block + i, None, None, jnp.where(lane >= LANES - GROUP, corner, below))

    def run(self, trips, regions, closed=None):
        total = self.total
        starts = [i * (total + 1) for i in range(4)]
        w_east, w_south, w_diag, parity = [self.wide[at:at + total, :] for at in starts]
        keep = None
        if closed is not None:
            is_end, where = closed
            row = lax.broadcasted_iota(jnp.int32, (total, LANES), 0)
            keep = jnp.where(where(row, lane_index((total, LANES))) & is_end, 0.0, 1.0).astype(F32)
        write_coefficients(total, w_east, w_south, w_diag, parity, keep, self.centre, self.weights, self.wide)
        stencil_steps(self.order, self.channels, self.centre, self.weights, (self.term_a, self.term_b), self.kept,
                      trips, regions)

    def terms(self, indices):
        return side_by_side([self.kept[i] for i in indices])

    def mixed(self, terms):
        if self.other is not None:
            matrix = self.mixing[...].reshape(self.order * self.channels, self.channels)
            value = lax.dot_general(matrix, terms, CONTRACT_ROWS, preferred_element_type=F32)
        else:
            matrix = side_by_side([self.mixing[k] for k in range(self.order)])
            value = jnp.dot(matrix, terms, preferred_element_type=F32)
        return value.astype(BF16)

    def paired_with(self, indices, valid, terms):
        left = [jnp.where(valid, self.paired[i], jnp.zeros((), BF16)) for i in indices]
        return lax.dot_general(side_by_side(left), terms, CONTRACT_LANES, preferred_element_type=F32)


def valid_lanes(channels):
    lane = lane_index((channels, LANES))
    lane_in = lane % GROUP
    in_strips = ((lane_in >= 5) & (lane_in < 10)) | ((lane_in >= SIDE + 6) & (lane_in < SIDE + 11))
    return (lane >= HALO) & (lane < LANES - HALO), in_strips


def main_forward(rows_in, mixing, out, grad, *scratch):
    rows = rows_in.shape[0]
    order, channels = mixing.shape[:2]
    chain = Chain(0, channels, mixing, ((0, 1), (rows + 1, rows + 8)), scratch)
    chain.put_all(1, rows_in, 16)
    chain.run(rows // 16, ((0, rows),))
    valid, _ = valid_lanes(channels)

    def products(start, count, total_grad):
        indices = [start + 1 + i for i in range(count)]
        terms = chain.terms(indices)
        value = chain.mixed(terms)
        for i in range(count):
            out[start + i] = value[:, LANES * i:LANES * (i + 1)]
        return total_grad + chain.paired_with(indices, valid, terms)

    inner = rows - 2 * HALO
    total_grad = jnp.zeros(grad.shape, F32)
    total_grad = lax.fori_loop(0, inner // 16, lambda i, g: products(HALO + i * 16, 16, g), total_grad)
    if inner % 16:
        total_grad = products(HALO + inner // 16 * 16, inner % 16, total_grad)
    grad[...] = total_grad


def main_backward(is_last, rows_in, north, south, mixing, summed, out, summed_out, *scratch):
    rows = rows_in.shape[0]
    channels = mixing.shape[1]
    count = rows + 2 * HALO
    chain = Chain(channels, None, mixing, ((0, 1), (count + 1, scratch[0].shape[0])), scratch)
    for i in range(HALO):
        chain.put(1 + i, north, i)
        chain.put(1 + HALO + rows + i, south, i)
    chain.put_all(1 + HALO, rows_in, 16)
    chain.run(7, ((0, count),), (is_last[0] == 1, lambda row, lane: row == HALO + rows))

    def products(i, _):
        value = chain.mixed(chain.terms([1 + HALO + i * 16 + j for j in range(16)]))
        for j in range(16):
            out[i * 16 + j] = value[:, LANES * j:LANES * (j + 1)]
        return 0

    lax.fori_loop(0, rows // 16, products, 0)
    summed_out[...] = summed[...]


def edge_sizes(rows):
    block = rows // BLOCKS
    strips = block + 2 * HALO
    top = strips + 6
    bottom = top + BAND + 5
    return block, top, bottom, -(-(bottom + BAND + 5) // 8) * 8


def edge_forward(scale, is_last, strips_in, rows_in, north, south, mixing, grad_main, out, grad, *scratch):
    rows = rows_in.shape[0]
    block, top, bottom, total = edge_sizes(rows)
    channels = mixing.shape[1]
    count = block + 2 * HALO
    chain = Chain(0, channels, mixing, ((0, 1), (1 + count, top + 1), (top + 1 + BAND, bottom + 1),
                                        (bottom + 1 + BAND, total)), scratch)
    chain.put_strips(strips_in, north, south)
    for i in range(HALO):
        chain.put(top + 1 + i, north, i)
        chain.put(bottom + 1 + 2 * HALO + i, south, i)
    for i in range(2 * HALO):
        chain.put(top + 1 + HALO + i, rows_in, i)
        chain.put(bottom + 1 + i, rows_in, rows - 2 * HALO + i)

    def closed(row, lane):
        return (row == bottom + 2 * HALO) | ((row == HALO + block) & (lane >= LANES - GROUP))

    chain.run(3, ((0, count), (top, BAND), (bottom, BAND)), (is_last[0] == 1, closed))
    main_valid, strip_valid = valid_lanes(channels)
    strip_rows = [1 + HALO + i for i in range(block)]
    band_rows = [top + 1 + HALO + i for i in range(HALO)] + [bottom + 1 + HALO + i for i in range(HALO)]
    total_grad = grad_main[...]
    slot = 0
    for indices, valid in ((strip_rows, strip_valid), (band_rows, main_valid)):
        terms = chain.terms(indices)
        value = chain.mixed(terms)
        for i in range(len(indices)):
            out[slot + i] = value[:, LANES * i:LANES * (i + 1)]
        slot += len(indices)
        total_grad = total_grad + chain.paired_with(indices, valid, terms)
    turned_grad = (total_grad * scale).T
    quarter = turned_grad.shape[0] // BLOCKS
    grad[...] = side_by_side([turned_grad[i * quarter:(i + 1) * quarter] for i in range(BLOCKS)])


def edge_backward(is_last, strips_in, north, south, mixing, summed, out, summed_out, *scratch):
    block = strips_in.shape[0]
    count = block + 2 * HALO
    chain = Chain(mixing.shape[1], None, mixing, ((0, 1), (1 + count, scratch[0].shape[0])), scratch)
    chain.put_strips(strips_in, north, south)
    chain.run(2, ((0, count),), (is_last[0] == 1, lambda row, lane: (row == HALO + block) & (lane >= LANES - GROUP)))
    value = chain.mixed(chain.terms([1 + HALO + i for i in range(block)]))
    for i in range(block):
        out[i] = value[:, LANES * i:LANES * (i + 1)]
    summed_out[...] = summed[...]


def assemble_kernel(main, edges, summed, out, summed_out, wide):
    summed_out[...] = summed[...]
    rows, channels, _ = main.shape
    block = rows // BLOCKS
    lane = lane_index((channels, LANES))

    def put(r, s, b, value):
        strip = edges[s]
        west = turned(strip, -(GROUP * b + 5))
        east = turned(strip, LANES - 5 - (GROUP * b + SIDE + 6))
        value = jnp.where(lane < HALO, west, jnp.where(lane >= LANES - HALO, east, value))
        wide[pl.ds(r * (3 * channels + 1), channels, stride=3), :] = value.astype(F32)

    for b in range(BLOCKS):
        def several(i, _, b=b):
            for j in range(8):
                s = i * 8 + j
                put(block * b + s, s, b, main[block * b + s])
            return 0
        lax.fori_loop(0, block // 8, several, 0)
    if edges.shape[0] > block:
        for i in range(HALO):
            put(i, i, 0, edges[block + i])
            put(rows - HALO + i, block - HALO + i, BLOCKS - 1, edges[block + HALO + i])

    def narrow(i, _):
        for j in range(4):
            o = i * 4 + j
            out[o] = wide[pl.ds(3 * o, rows, stride=3 * channels + 1), :].astype(BF16)
        return 0

    lax.fori_loop(0, channels // 4, narrow, 0)


def finish_kernel(mine, theirs, out):
    order, channels = out.shape[:2]
    total = mine[...] + theirs[...]
    quarter = total.shape[0]
    for k in range(order):
        for first in range(0, channels, 16):
            block, at = divmod(k * channels + first, quarter)
            out[k, first:first + 16, :] = total[at:at + 16, block * channels:(block + 1) * channels]


def on_device(signal, cotangent, edge_weights, circle_shift, mixing):
    channels, rows, sector = signal.shape
    order = mixing.shape[0]
    block, top, bottom, edge_total = edge_sizes(rows)
    lat, lon = lax.axis_size("lat"), lax.axis_size("lon")
    vmem = pl.BlockSpec(memory_space=pltpu.VMEM)
    smem = pl.BlockSpec(memory_space=pltpu.SMEM)
    hbm = pl.BlockSpec(memory_space=pltpu.HBM)
    shape = jax.ShapeDtypeStruct

    def packed(count):
        return shape((count, PACKED, LANES), BF16)

    def weighs(mib):
        return pl.CostEstimate(flops=0, bytes_accessed=mib * 1024 * 1024, transcendentals=0)

    all_wide = pltpu.VMEM((spread_size(2 * channels + 8, rows), LANES), F32)
    raw = (signal, cotangent, edge_weights, circle_shift)
    to_west, to_east = pl.pallas_call(
        pack_kernel,
        out_shape=(packed(block // 6), packed(block // 6)),
        in_specs=[hbm, hbm, hbm, smem],
        out_specs=(vmem, vmem),
        scratch_shapes=[
            pltpu.VMEM(signal.shape, BF16),
            pltpu.VMEM(signal.shape, BF16),
            pltpu.VMEM(edge_weights.shape, BF16),
            all_wide,
            pltpu.SemaphoreType.DMA((9,)),
        ],
        compiler_params=pltpu.CompilerParams(vmem_limit_bytes=PACK_VMEM),
        name="pack",
    )(*raw)

    eastward = [(i, (i + 1) % lon) for i in range(lon)]
    westward = [(j, i) for i, j in eastward]
    from_west = lax.ppermute(to_east, "lon", eastward)
    from_east = lax.ppermute(to_west, "lon", westward)

    own_strips, rows_in = pl.pallas_call(
        own_kernel,
        out_shape=(packed(block), packed(rows)),
        in_specs=[vmem, vmem, vmem, smem],
        out_specs=(vmem, vmem),
        scratch_shapes=[all_wide],
        compiler_params=params(20),
        cost_estimate=weighs(8),
        name="own",
    )(*raw)

    strips, to_north, to_south = pl.pallas_call(
        merge_kernel,
        out_shape=(packed(block), packed(HALO + 2), packed(HALO + 2)),
        in_specs=[vmem] * 4,
        out_specs=(vmem,) * 3,
        compiler_params=params(8),
        name="merge",
    )(own_strips, rows_in, from_west, from_east)

    southward = [(i, i + 1) for i in range(lat - 1)]
    northward = [(j, i) for i, j in southward]
    north = lax.ppermute(to_south, "lat", southward)
    south = lax.ppermute(to_north, "lat", northward)

    rows_first = shape((rows, channels, LANES), BF16)
    grad_shape = shape((channels, order * channels), F32)
    share_shape = shape((order * channels // BLOCKS, BLOCKS * channels), F32)

    def chain_scratch(total, with_pairs):
        scratch = [
            pltpu.VMEM((total, channels, LANES), F32),
            pltpu.VMEM((total, channels, LANES), F32),
            pltpu.VMEM((total, order * channels, LANES), BF16),
            pltpu.VMEM((total, LANES), F32),
            pltpu.VMEM((6, total, 16, LANES), BF16),
            pltpu.VMEM((8 * (total + 1), LANES), F32),
        ]
        return scratch + [pltpu.VMEM((total, channels, LANES), BF16)] * with_pairs

    main_f, grad_main = pl.pallas_call(
        main_forward,
        out_shape=(rows_first, grad_shape),
        in_specs=[vmem, vmem],
        out_specs=(vmem, vmem),
        scratch_shapes=chain_scratch(rows + 8, True),
        compiler_params=params(20),
        cost_estimate=weighs(24),
        name="main_forward",
    )(rows_in, mixing)

    is_last = (lax.axis_index("lat") == lat - 1).astype(jnp.int32).reshape(1)
    norm_scale = 1.0 / math.sqrt(rows * lat * sector * lon)
    edge_f, grad = pl.pallas_call(
        functools.partial(edge_forward, norm_scale),
        out_shape=(shape((block + 2 * HALO, channels, LANES), BF16), share_shape),
        in_specs=[smem] + [vmem] * 6,
        out_specs=(vmem, vmem),
        scratch_shapes=chain_scratch(edge_total, True),
        compiler_params=params(16),
        cost_estimate=weighs(12),
        name="edge_forward",
    )(is_last, strips, rows_in, north, south, mixing, grad_main)

    rounds = []
    for axis, devices in (("lon", lon), ("lat", lat)):
        reach = 1
        while reach < devices:
            rounds.append((axis, [(i, i ^ reach) for i in range(devices)]))
            reach *= 2

    results = {}

    def run_main_backward(share):
        results["main"], share = pl.pallas_call(
            main_backward,
            out_shape=(rows_first, share_shape),
            in_specs=[smem] + [vmem] * 5,
            out_specs=(vmem, vmem),
            scratch_shapes=chain_scratch(-(-(rows + 2 * HALO + 8) // 8) * 8, False),
            compiler_params=params(20),
            cost_estimate=weighs(24),
            name="main_backward",
        )(is_last, rows_in, north, south, mixing, share)
        return share

    def run_edge_backward(share):
        results["edge"], share = pl.pallas_call(
            edge_backward,
            out_shape=(shape((block, channels, LANES), BF16), share_shape),
            in_specs=[smem] + [vmem] * 5,
            out_specs=(vmem, vmem),
            scratch_shapes=chain_scratch(-(-(block + 2 * HALO + 8) // 8) * 8, False),
            compiler_params=params(12),
            cost_estimate=weighs(12),
            name="edge_backward",
        )(is_last, strips, north, south, mixing, share)
        return share

    def assemble(main, edges, share, name):
        return pl.pallas_call(
            assemble_kernel,
            out_shape=(shape(signal.shape, BF16), share_shape),
            in_specs=[vmem] * 3,
            out_specs=(vmem, vmem),
            scratch_shapes=[pltpu.VMEM((spread_size(channels, rows), LANES), F32)],
            compiler_params=params(12),
            cost_estimate=weighs(8),
            name=name,
        )(main, edges, share)

    def run_assemble_forward(share):
        results["output"], share = assemble(main_f, edge_f, share, "assemble_forward")
        return share

    def run_assemble_backward(share):
        results["signal_grad"], share = assemble(results["main"], results["edge"], share, "assemble_backward")
        return share

    beside = [run_main_backward, run_assemble_forward, run_edge_backward, run_assemble_backward]
    share = grad
    theirs = jnp.zeros_like(grad)
    for number in range(max(len(rounds), len(beside))):
        if number:
            share = share + theirs
        theirs = lax.ppermute(share, *rounds[number]) if number < len(rounds) else jnp.zeros_like(grad)
        if number < len(beside):
            share = beside[number](share)

    mixing_grad = pl.pallas_call(
        finish_kernel,
        out_shape=shape(mixing.shape, F32),
        in_specs=[vmem, vmem],
        out_specs=vmem,
        name="finish",
    )(share, theirs)
    return (results["output"], results["signal_grad"], mixing_grad)


def solution(mesh):
    in_specs = (P(None, "lat", "lon"), P(None, "lat", "lon"), P(None, "lat", "lon"), P("lat"), P())
    out_specs = (P(None, "lat", "lon"), P(None, "lat", "lon"), P())
    return jax.shard_map(
        on_device, mesh=mesh, in_specs=in_specs, out_specs=out_specs, check_vma=False
    )
```

```python
import functools
import math

import jax
import jax.numpy as jnp
from jax import lax
from jax.experimental import pallas as pl
from jax.experimental.pallas import tpu as pltpu
from jax.sharding import PartitionSpec as P

F32 = jnp.float32
BF16 = jnp.bfloat16
HALO = 5
LANES = 128
BLOCKS = 4
GROUP = LANES // BLOCKS
SIDE = GROUP // 2
PACKED = 80
BAND = 3 * HALO
PACK_VMEM = 63_400_000


def params(mib):
    return pltpu.CompilerParams(vmem_limit_bytes=mib * 1024 * 1024)


def lane_index(shape):
    return lax.broadcasted_iota(jnp.int32, shape, len(shape) - 1)


def turned(x, amount):
    amount = amount % LANES
    return pltpu.roll(x, amount, 1) if amount else x


def spread_size(channels, rows):
    return rows * (3 * channels + 1)


def spread(wide, channels, c, rows, x):
    wide[pl.ds(3 * c, rows, stride=3 * channels + 1), :] = x


def gather(wide, channels, r, first, count):
    return wide[pl.ds(r * (3 * channels + 1) + 3 * first, count, stride=3), :]


def widen_all(signal, cotangent, weights, wide, ready=None):
    channels, rows, _ = signal.shape
    count = 2 * channels + 8
    for i in range(3):
        if ready is not None and i == 0:
            ready(2, 0)
        spread(wide, count, 2 * channels + i, rows, weights[i].astype(F32))
    for i in range(3, 8):
        spread(wide, count, 2 * channels + i, rows, jnp.zeros((rows, LANES), F32))
    for which, source in enumerate((signal, cotangent)):
        for part in range(4):
            if ready is not None:
                ready(which, part)
            size = channels // 4

            def widen(i, _):
                for j in range(4):
                    c = part * size + i * 4 + j
                    spread(wide, count, which * channels + c, rows, source[c].astype(F32))
                return 0

            lax.fori_loop(0, size // 4, widen, 0)


def row_loader(channels, rows, shift, wide):
    count = 2 * channels + 8
    sub = lax.broadcasted_iota(jnp.int32, (8, LANES), 0)

    def load_row(r):
        body = gather(wide, count, r, 0, 2 * channels)
        tail = gather(wide, count, r, 2 * channels, 8)
        parity = jnp.where(shift[r] == 1, 1.0, 0.0).astype(F32)
        tail = jnp.where(sub == 3, parity, tail)
        return jnp.concatenate([body, tail, jnp.zeros((8, LANES), F32)], axis=0).astype(BF16)

    return load_row


def pack_kernel(signal_hbm, cotangent_hbm, weights_hbm, shift, west_out, east_out,
                signal, cotangent, weights, wide, arrived):
    channels, rows, _ = signal.shape
    block = rows // BLOCKS
    per_row = block // 6
    size = channels // 4
    copies = {(2, 0): pltpu.make_async_copy(weights_hbm, weights, arrived.at[8])}
    for which, (source, target) in enumerate(((signal_hbm, signal), (cotangent_hbm, cotangent))):
        for part in range(4):
            span = pl.ds(part * size, size)
            copies[which, part] = pltpu.make_async_copy(source.at[span], target.at[span], arrived.at[4 * which + part])
    for copy in copies.values():
        copy.start()
    widen_all(signal, cotangent, weights, wide, lambda *key: copies[key].wait())
    load_row = row_loader(channels, rows, shift, wide)
    lane = lane_index((PACKED, LANES))

    def each(t, _):
        west = jnp.zeros((PACKED, LANES), BF16)
        east = jnp.zeros((PACKED, LANES), BF16)
        for b in range(BLOCKS):
            for m in range(6):
                x = load_row(block * b + per_row * m + t)
                first = GROUP * b + 5 * m
                moved = turned(x, first + 5)
                east = jnp.where((lane >= first) & (lane < first + 5), moved, east)
                west = jnp.where((lane - (first + 5)) % LANES < 5, moved, west)
        west_out[t] = west
        east_out[t] = east
        return 0

    lax.fori_loop(0, per_row, each, 0)


def own_kernel(signal, cotangent, weights, shift, strips_out, rows_out, wide):
    channels, rows, _ = signal.shape
    block = rows // BLOCKS
    widen_all(signal, cotangent, weights, wide)
    load_row = row_loader(channels, rows, shift, wide)
    lane = lane_index((PACKED, LANES))

    def each(i, _):
        for j in range(2):
            s = i * 2 + j
            strip = jnp.zeros((PACKED, LANES), BF16)
            for b in range(BLOCKS):
                x = load_row(block * b + s)
                rows_out[block * b + s] = x
                west = turned(x, GROUP * b + 5)
                east = turned(x, GROUP * b + SIDE + 11)
                strip = jnp.where((lane >= GROUP * b + 5) & (lane < GROUP * b + SIDE), west, strip)
                strip = jnp.where((lane >= GROUP * b + SIDE) & (lane < GROUP * b + SIDE + 11), east, strip)
            strips_out[s] = strip
        return 0

    lax.fori_loop(0, block // 2, each, 0)


def merge_kernel(strips_in, rows_in, from_west, from_east, strips_out, north_out, south_out):
    block = strips_in.shape[0]
    rows = rows_in.shape[0]
    per_row = block // 6
    lane = lane_index((PACKED, LANES))
    lane_in = lane % GROUP

    def each(t, _):
        west = from_west[t]
        east = from_east[t]
        for m in range(6):
            strip = strips_in[per_row * m + t]
            strip = jnp.where(lane_in < 5, turned(west, -5 * m), strip)
            strip = jnp.where(lane_in >= GROUP - 5, turned(east, 22 - 5 * m), strip)
            strips_out[per_row * m + t] = strip
        return 0

    lax.fori_loop(0, per_row, each, 0)
    for out, first_row, first_strip, side in (
        (north_out, 0, 0, 0), (south_out, rows - HALO, block - HALO, BLOCKS - 1)):
        for i in range(HALO):
            out[i] = rows_in[first_row + i]
        corner = turned(strips_out[first_strip], -GROUP * side)
        for g in range(1, BLOCKS):
            piece = turned(strips_out[first_strip + g], GROUP * (g - side))
            corner = jnp.where((lane >= GROUP * g) & (lane < GROUP * (g + 1)), piece, corner)
        out[HALO] = corner
        out[HALO + 1] = turned(strips_out[first_strip + HALO - 1], -GROUP * side)


def write_coefficients(total, first, w_east, w_south, w_diag, parity, keep, coef, shifted):
    count = w_east.shape[0]
    w_back = jnp.where(parity > 0.5, turned(w_diag, 1), turned(w_diag, -1))
    w_west = turned(w_east, 1)
    shifted[0:8, :] = jnp.zeros((8, LANES), F32)
    shifted[8:8 + count, :] = w_south + w_back
    degree = w_east + w_west + w_south + w_diag + shifted[7:7 + count, :]
    third = -1.0 / 3.0
    arrays = [degree * (1.0 / 3.0) - 2.0, w_east * third, w_west * third]
    for array in (w_south, w_diag, w_back):
        arrays.append(array * third if keep is None else array * keep * third)
    for i, array in enumerate(arrays + [parity]):
        coef[i * total + first:i * total + first + count, :] = array


def stencil_steps(order, channels, total, coef, buffers, kept, trips, regions):
    groups = channels // 8

    def coef_row(i, at):
        return coef[pl.ds(i * total + at, 8, stride=0), :]

    def step(position, now, older, newer):
        last = position == order - 1

        def one_row(at, level, down, before):
            coefs = [coef_row(i, at) for i in range(7)]
            c, e, w, s, d, back, parity = coefs
            here = parity > 0.5
            s_above, d_above, above = before
            new, next_level, next_down = [], [], []
            for g in range(groups):
                span = slice(8 * g, 8 * g + 8)
                v = now[at, span, :]
                v_east = pltpu.roll(v, LANES - 1, 1)
                v_west = pltpu.roll(v, 1, 1)
                value = level[g] + s_above * v + d_above * jnp.where(above, v_east, v_west)
                new.append(value * 0.5 if position == 1 else value)
                value = c * v + e * v_east + w * v_west + down[g]
                next_level.append(value if position == 1 else value - older[at, span, :])
                next_down.append(s * v + back * jnp.where(here, v_west, v_east))
            if not last:
                for g in range(groups):
                    newer[at - 1, 8 * g:8 * g + 8, :] = new[g]
            for h in range(groups // 2):
                first = channels * position + 16 * h
                pair = jnp.concatenate([new[2 * h], new[2 * h + 1]], axis=0)
                kept[at - 1, first:first + 16, :] = pair.astype(BF16)
            return tuple(next_level), tuple(next_down), (s, d, here)

        counts = [-(-(count + 2 - 2 * position) // trips) for _, count in regions]

        def several(trip, carry):
            states = []
            for (base, _), count, (level, down) in zip(regions, counts, carry):
                at = base + position + trip * count
                before = (coef_row(3, at - 1), coef_row(4, at - 1), coef_row(6, at - 1) > 0.5)
                states.append([at, level, down, before])
            for j in range(max(counts)):
                for state, count in zip(states, counts):
                    if j < count:
                        state[1:] = one_row(state[0] + j, *state[1:])
            return tuple((level, down) for _, level, down, _ in states)

        zeros = tuple(jnp.zeros((8, LANES), F32) for _ in range(groups))
        lax.fori_loop(0, trips, several, tuple((zeros, zeros) for _ in regions))

    for position in range(1, order):
        step(position, buffers[(position - 1) % 3], buffers[(position - 2) % 3], buffers[position % 3])


def zero_guards(buffers, coef, total, guards):
    for first, end in guards:
        for index in range(first, end):
            for buffer in buffers:
                buffer[index] = jnp.zeros(buffer.shape[1:], F32)
        for i in range(7):
            coef[i * total + first:i * total + end, :] = jnp.zeros((end - first, LANES), F32)


CONTRACT_LANES = (((1,), (1,)), ((), ()))
CONTRACT_ROWS = (((0,), (0,)), ((), ()))


def side_by_side(tiles):
    return jnp.concatenate(tiles, axis=1)


class Chain:
    def __init__(self, first, other, mixing, guards, scratch):
        self.buffers, self.kept, self.coef, self.wide = scratch[:3], *scratch[3:6]
        self.paired = scratch[6] if other is not None else None
        self.first, self.other, self.mixing = first, other, mixing
        self.order, self.channels = mixing.shape[:2]
        self.total = self.kept.shape[0]
        zero_guards(self.buffers, self.coef, self.total, guards)
        for begin, end in guards:
            for i in range(4):
                at = i * (self.total + 1)
                self.wide[at + begin:at + end, :] = jnp.zeros((end - begin, LANES), F32)

    def put(self, index, ref, at, tile=None):
        def part(begin, count):
            return ref[at, begin:begin + count, :] if tile is None else tile[begin:begin + count]
        self.wide[pl.ds(index, 8, stride=self.total + 1), :] = part(PACKED - 16, 16).astype(F32)[:8]
        field = part(self.first, self.channels)
        self.buffers[0][index] = field.astype(F32)
        self.kept[index, 0:self.channels, :] = field
        if self.other is not None:
            self.paired[index] = part(self.other, self.channels)

    def put_all(self, index, ref, unroll):
        count = ref.shape[0]

        def several(i, _):
            for j in range(unroll):
                self.put(index + i * unroll + j, ref, i * unroll + j)
            return 0

        lax.fori_loop(0, count // unroll, several, 0)

    def put_strips(self, strips, north, south):
        block = strips.shape[0]
        self.put_all(1 + HALO, strips, 8)
        lane = lane_index((PACKED, LANES))
        for i in range(HALO):
            at_end = i == HALO - 1
            above = turned(strips[block - HALO + i], GROUP)
            corner = turned(north[HALO + at_end], 0 if at_end else -GROUP * i)
            self.put(1 + i, None, None, jnp.where(lane < GROUP, corner, above))
            below = turned(strips[i], -GROUP)
            corner = turned(south[HALO + at_end], -GROUP - (0 if at_end else GROUP * i))
            self.put(1 + HALO + block + i, None, None, jnp.where(lane >= LANES - GROUP, corner, below))

    def run(self, trips, regions, closed=None):
        total = self.total
        starts = [i * (total + 1) for i in range(4)]
        w_east, w_south, w_diag, parity = [self.wide[at:at + total, :] for at in starts]
        keep = None
        if closed is not None:
            is_end, where = closed
            row = lax.broadcasted_iota(jnp.int32, (total, LANES), 0)
            keep = jnp.where(where(row, lane_index((total, LANES))) & is_end, 0.0, 1.0).astype(F32)
        write_coefficients(total, 0, w_east, w_south, w_diag, parity, keep, self.coef, self.wide)
        stencil_steps(self.order, self.channels, total, self.coef, self.buffers, self.kept, trips, regions)

    def terms(self, indices):
        return side_by_side([self.kept[i] for i in indices])

    def mixed(self, terms):
        if self.other is not None:
            matrix = self.mixing[...].reshape(self.order * self.channels, self.channels)
            value = lax.dot_general(matrix, terms, CONTRACT_ROWS, preferred_element_type=F32)
        else:
            matrix = side_by_side([self.mixing[k] for k in range(self.order)])
            value = jnp.dot(matrix, terms, preferred_element_type=F32)
        return value.astype(BF16)

    def paired_with(self, indices, valid, terms):
        left = [jnp.where(valid, self.paired[i], jnp.zeros((), BF16)) for i in indices]
        return lax.dot_general(side_by_side(left), terms, CONTRACT_LANES, preferred_element_type=F32)


def valid_lanes(channels):
    lane = lane_index((channels, LANES))
    lane_in = lane % GROUP
    in_strips = ((lane_in >= 5) & (lane_in < 10)) | ((lane_in >= SIDE + 6) & (lane_in < SIDE + 11))
    return (lane >= HALO) & (lane < LANES - HALO), in_strips


def main_forward(rows_in, mixing, out, grad, mixing_out, *scratch):
    mixing_out[...] = mixing[...]
    rows = rows_in.shape[0]
    order, channels = mixing.shape[:2]
    chain = Chain(0, channels, mixing, ((0, 1), (rows + 1, rows + 8)), scratch)
    chain.put_all(1, rows_in, 16)
    chain.run(rows // 16, ((0, rows),))
    valid, _ = valid_lanes(channels)

    def products(start, count, total_grad):
        indices = [start + 1 + i for i in range(count)]
        terms = chain.terms(indices)
        value = chain.mixed(terms)
        for i in range(count):
            out[start + i] = value[:, LANES * i:LANES * (i + 1)]
        return total_grad + chain.paired_with(indices, valid, terms)

    inner = rows - 2 * HALO
    total_grad = jnp.zeros(grad.shape, F32)
    total_grad = lax.fori_loop(0, inner // 16, lambda i, g: products(HALO + i * 16, 16, g), total_grad)
    if inner % 16:
        total_grad = products(HALO + inner // 16 * 16, inner % 16, total_grad)
    grad[...] = total_grad


def main_backward(is_last, rows_in, north, south, mixing, summed, out, summed_out, *scratch):
    rows = rows_in.shape[0]
    channels = mixing.shape[1]
    count = rows + 2 * HALO
    chain = Chain(channels, None, mixing, ((0, 1), (count + 1, scratch[0].shape[0])), scratch)
    for i in range(HALO):
        chain.put(1 + i, north, i)
        chain.put(1 + HALO + rows + i, south, i)
    chain.put_all(1 + HALO, rows_in, 16)
    chain.run(7, ((0, count),), (is_last[0] == 1, lambda row, lane: row == HALO + rows))

    def products(i, _):
        value = chain.mixed(chain.terms([1 + HALO + i * 16 + j for j in range(16)]))
        for j in range(16):
            out[i * 16 + j] = value[:, LANES * j:LANES * (j + 1)]
        return 0

    lax.fori_loop(0, rows // 16, products, 0)
    summed_out[...] = summed[...]


def edge_sizes(rows):
    block = rows // BLOCKS
    strips = block + 2 * HALO
    top = strips + 6
    bottom = top + BAND + 5
    return block, top, bottom, -(-(bottom + BAND + 5) // 8) * 8


def edge_forward(is_last, strips_in, rows_in, north, south, mixing, out, grad, *scratch):
    rows = rows_in.shape[0]
    block, top, bottom, total = edge_sizes(rows)
    channels = mixing.shape[1]
    count = block + 2 * HALO
    chain = Chain(0, channels, mixing, ((0, 1), (1 + count, top + 1), (top + 1 + BAND, bottom + 1),
                                        (bottom + 1 + BAND, total)), scratch)
    chain.put_strips(strips_in, north, south)
    for i in range(HALO):
        chain.put(top + 1 + i, north, i)
        chain.put(bottom + 1 + 2 * HALO + i, south, i)
    for i in range(2 * HALO):
        chain.put(top + 1 + HALO + i, rows_in, i)
        chain.put(bottom + 1 + i, rows_in, rows - 2 * HALO + i)

    def closed(row, lane):
        return (row == bottom + 2 * HALO) | ((row == HALO + block) & (lane >= LANES - GROUP))

    chain.run(3, ((0, count), (top, BAND), (bottom, BAND)), (is_last[0] == 1, closed))
    main_valid, strip_valid = valid_lanes(channels)
    strip_rows = [1 + HALO + i for i in range(block)]
    band_rows = [top + 1 + HALO + i for i in range(HALO)] + [bottom + 1 + HALO + i for i in range(HALO)]
    total_grad = jnp.zeros(grad.shape, F32)
    slot = 0
    for indices, valid in ((strip_rows, strip_valid), (band_rows, main_valid)):
        terms = chain.terms(indices)
        value = chain.mixed(terms)
        for i in range(len(indices)):
            out[slot + i] = value[:, LANES * i:LANES * (i + 1)]
        slot += len(indices)
        total_grad = total_grad + chain.paired_with(indices, valid, terms)
    grad[...] = total_grad


def edge_backward(is_last, strips_in, north, south, mixing, summed, out, summed_out, *scratch):
    block = strips_in.shape[0]
    count = block + 2 * HALO
    chain = Chain(mixing.shape[1], None, mixing, ((0, 1), (1 + count, scratch[0].shape[0])), scratch)
    chain.put_strips(strips_in, north, south)
    chain.run(2, ((0, count),), (is_last[0] == 1, lambda row, lane: (row == HALO + block) & (lane >= LANES - GROUP)))
    value = chain.mixed(chain.terms([1 + HALO + i for i in range(block)]))
    for i in range(block):
        out[i] = value[:, LANES * i:LANES * (i + 1)]
    summed_out[...] = summed[...]


def assemble_kernel(main, edges, summed, out_hbm, summed_out, wide, out, sent):
    summed_out[...] = summed[...]
    rows, channels, _ = main.shape
    block = rows // BLOCKS
    lane = lane_index((channels, LANES))

    def put(r, s, b, value):
        strip = edges[s]
        west = turned(strip, -(GROUP * b + 5))
        east = turned(strip, LANES - 5 - (GROUP * b + SIDE + 6))
        value = jnp.where(lane < HALO, west, jnp.where(lane >= LANES - HALO, east, value))
        wide[pl.ds(r * (3 * channels + 1), channels, stride=3), :] = value.astype(F32)

    for b in range(BLOCKS):
        def several(i, _, b=b):
            for j in range(8):
                s = i * 8 + j
                put(block * b + s, s, b, main[block * b + s])
            return 0
        lax.fori_loop(0, block // 8, several, 0)
    if edges.shape[0] > block:
        for i in range(HALO):
            put(i, i, 0, edges[block + i])
            put(rows - HALO + i, block - HALO + i, BLOCKS - 1, edges[block + HALO + i])

    pieces = 4
    size = channels // pieces

    def narrow(i, _):
        for j in range(size):
            o = i * size + j
            out[o] = wide[pl.ds(3 * o, rows, stride=3 * channels + 1), :].astype(BF16)
        copy(i).start()
        return 0

    def copy(i):
        span = pl.ds(i * size, size)
        return pltpu.make_async_copy(out.at[span], out_hbm.at[span], sent.at[i])

    lax.fori_loop(0, pieces, narrow, 0)
    for i in range(pieces):
        copy(i).wait()


def finish_kernel(scale, mine, theirs, out):
    order, channels = out.shape[:2]
    out[...] = ((mine[...] + theirs[...]) * scale).T.reshape(order, channels, channels)


def on_device(signal, cotangent, edge_weights, circle_shift, mixing):
    channels, rows, sector = signal.shape
    order = mixing.shape[0]
    block, top, bottom, edge_total = edge_sizes(rows)
    lat, lon = lax.axis_size("lat"), lax.axis_size("lon")
    vmem = pl.BlockSpec(memory_space=pltpu.VMEM)
    smem = pl.BlockSpec(memory_space=pltpu.SMEM)
    hbm = pl.BlockSpec(memory_space=pltpu.HBM)
    shape = jax.ShapeDtypeStruct

    def packed(count):
        return shape((count, PACKED, LANES), BF16)

    def weighs(mib):
        return pl.CostEstimate(flops=0, bytes_accessed=mib * 1024 * 1024, transcendentals=0)

    all_wide = pltpu.VMEM((spread_size(2 * channels + 8, rows), LANES), F32)
    raw = (signal, cotangent, edge_weights, circle_shift)
    to_west, to_east = pl.pallas_call(
        pack_kernel,
        out_shape=(packed(block // 6), packed(block // 6)),
        in_specs=[hbm, hbm, hbm, smem],
        out_specs=(vmem, vmem),
        scratch_shapes=[
            pltpu.VMEM(signal.shape, BF16),
            pltpu.VMEM(signal.shape, BF16),
            pltpu.VMEM(edge_weights.shape, BF16),
            all_wide,
            pltpu.SemaphoreType.DMA((9,)),
        ],
        compiler_params=pltpu.CompilerParams(vmem_limit_bytes=PACK_VMEM),
        name="pack",
    )(*raw)

    eastward = [(i, (i + 1) % lon) for i in range(lon)]
    westward = [(j, i) for i, j in eastward]
    from_west = lax.ppermute(to_east, "lon", eastward)
    from_east = lax.ppermute(to_west, "lon", westward)

    own_strips, rows_in = pl.pallas_call(
        own_kernel,
        out_shape=(packed(block), packed(rows)),
        in_specs=[vmem, vmem, vmem, smem],
        out_specs=(vmem, vmem),
        scratch_shapes=[all_wide],
        compiler_params=params(20),
        cost_estimate=weighs(8),
        name="own",
    )(*raw)

    strips, to_north, to_south = pl.pallas_call(
        merge_kernel,
        out_shape=(packed(block), packed(HALO + 2), packed(HALO + 2)),
        in_specs=[vmem] * 4,
        out_specs=(vmem,) * 3,
        compiler_params=params(8),
        name="merge",
    )(own_strips, rows_in, from_west, from_east)

    southward = [(i, i + 1) for i in range(lat - 1)]
    northward = [(j, i) for i, j in southward]
    north = lax.ppermute(to_south, "lat", southward)
    south = lax.ppermute(to_north, "lat", northward)

    rows_first = shape((rows, channels, LANES), BF16)
    grad_shape = shape((channels, order * channels), F32)

    def chain_scratch(total, with_pairs):
        scratch = [pltpu.VMEM((total, channels, LANES), F32)] * 3 + [
            pltpu.VMEM((total, order * channels, LANES), BF16),
            pltpu.VMEM((7 * total, LANES), F32),
            pltpu.VMEM((8 * (total + 1), LANES), F32),
        ]
        return scratch + [pltpu.VMEM((total, channels, LANES), BF16)] * with_pairs

    main_f, grad_main, mixing = pl.pallas_call(
        main_forward,
        out_shape=(rows_first, grad_shape, shape(mixing.shape, BF16)),
        in_specs=[vmem, vmem],
        out_specs=(vmem, vmem, vmem),
        scratch_shapes=chain_scratch(rows + 8, True),
        compiler_params=params(20),
        cost_estimate=weighs(24),
        name="main_forward",
    )(rows_in, mixing)

    is_last = (lax.axis_index("lat") == lat - 1).astype(jnp.int32).reshape(1)
    edge_f, grad_edge = pl.pallas_call(
        edge_forward,
        out_shape=(shape((block + 2 * HALO, channels, LANES), BF16), grad_shape),
        in_specs=[smem] + [vmem] * 5,
        out_specs=(vmem, vmem),
        scratch_shapes=chain_scratch(edge_total, True),
        compiler_params=params(16),
        cost_estimate=weighs(12),
        name="edge_forward",
    )(is_last, strips, rows_in, north, south, mixing)

    rounds = []
    for axis, devices in (("lon", lon), ("lat", lat)):
        reach = 1
        while reach < devices:
            rounds.append((axis, [(i, i ^ reach) for i in range(devices)]))
            reach *= 2
    rounds = [r for r in rounds if r[0] == "lon"] + [r for r in rounds if r[0] == "lat"][::-1]

    results = {}

    def run_main_backward(share):
        results["main"], share = pl.pallas_call(
            main_backward,
            out_shape=(rows_first, grad_shape),
            in_specs=[smem] + [vmem] * 5,
            out_specs=(vmem, vmem),
            scratch_shapes=chain_scratch(-(-(rows + 2 * HALO + 8) // 8) * 8, False),
            compiler_params=params(20),
            cost_estimate=weighs(24),
            name="main_backward",
        )(is_last, rows_in, north, south, mixing, share)
        return share

    def run_edge_backward(share):
        results["edge"], share = pl.pallas_call(
            edge_backward,
            out_shape=(shape((block, channels, LANES), BF16), grad_shape),
            in_specs=[smem] + [vmem] * 5,
            out_specs=(vmem, vmem),
            scratch_shapes=chain_scratch(-(-(block + 2 * HALO + 8) // 8) * 8, False),
            compiler_params=params(12),
            cost_estimate=weighs(12),
            name="edge_backward",
        )(is_last, strips, north, south, mixing, share)
        return share

    def assemble(main, edges, share, name):
        return pl.pallas_call(
            assemble_kernel,
            out_shape=(shape(signal.shape, BF16), grad_shape),
            in_specs=[vmem] * 3,
            out_specs=(hbm, vmem),
            scratch_shapes=[
                pltpu.VMEM((spread_size(channels, rows), LANES), F32),
                pltpu.VMEM(signal.shape, BF16),
                pltpu.SemaphoreType.DMA((4,)),
            ],
            compiler_params=params(12),
            cost_estimate=weighs(8),
            name=name,
        )(main, edges, share)

    def run_assemble_forward(share):
        results["output"], share = assemble(main_f, edge_f, share, "assemble_forward")
        return share

    def run_assemble_backward(share):
        results["signal_grad"], share = assemble(results["main"], results["edge"], share, "assemble_backward")
        return share

    beside = [run_main_backward, run_assemble_forward, run_edge_backward, run_assemble_backward]
    share = grad_main + grad_edge
    theirs = jnp.zeros_like(share)
    for number in range(max(len(rounds), len(beside))):
        if number:
            share = share + theirs
        theirs = lax.ppermute(share, *rounds[number]) if number < len(rounds) else jnp.zeros_like(share)
        if number < len(beside):
            share = beside[number](share)

    norm_scale = 1.0 / math.sqrt(rows * lat * sector * lon)
    mixing_grad = pl.pallas_call(
        functools.partial(finish_kernel, norm_scale),
        out_shape=shape(mixing.shape, F32),
        in_specs=[vmem, vmem],
        out_specs=vmem,
        compiler_params=params(4),
        name="finish",
    )(share, theirs)
    return (results["output"], results["signal_grad"], mixing_grad)


def solution(mesh):
    in_specs = (P(None, "lat", "lon"), P(None, "lat", "lon"), P(None, "lat", "lon"), P("lat"), P())
    out_specs = (P(None, "lat", "lon"), P(None, "lat", "lon"), P())
    return jax.shard_map(
        on_device, mesh=mesh, in_specs=in_specs, out_specs=out_specs, check_vma=False
    )
```

```python
import functools
import math

import jax
import jax.numpy as jnp
from jax import lax
from jax.experimental import pallas as pl
from jax.experimental.pallas import tpu as pltpu
from jax.sharding import PartitionSpec as P

F32 = jnp.float32
BF16 = jnp.bfloat16
HALO = 5
LANES = 128
BLOCKS = 4
GROUP = LANES // BLOCKS
SIDE = GROUP // 2
PACKED = 80
BAND = 3 * HALO
PACK_VMEM = 63_400_000


def params(mib):
    return pltpu.CompilerParams(vmem_limit_bytes=mib * 1024 * 1024)


def lane_index(shape):
    return lax.broadcasted_iota(jnp.int32, shape, len(shape) - 1)


def turned(x, amount):
    amount = amount % LANES
    return pltpu.roll(x, amount, 1) if amount else x


def spread_size(channels, rows):
    return rows * (3 * channels + 1)


def spread(wide, channels, c, rows, x):
    wide[pl.ds(3 * c, rows, stride=3 * channels + 1), :] = x


def gather(wide, channels, r, first, count):
    return wide[pl.ds(r * (3 * channels + 1) + 3 * first, count, stride=3), :]


def widen_all(signal, cotangent, weights, wide, ready=None):
    channels, rows, _ = signal.shape
    count = 2 * channels + 8
    for which, source in enumerate((signal, cotangent)):
        for part in range(4):
            if ready is not None:
                ready(which, part)
            size = channels // 4

            def widen(i, _):
                for j in range(4):
                    c = part * size + i * 4 + j
                    spread(wide, count, which * channels + c, rows, source[c].astype(F32))
                return 0

            lax.fori_loop(0, size // 4, widen, 0)
    if ready is not None:
        ready(2, 0)
    for i in range(8):
        x = weights[i].astype(F32) if i < 3 else jnp.zeros((rows, LANES), F32)
        spread(wide, count, 2 * channels + i, rows, x)


def row_loader(channels, rows, shift, wide):
    count = 2 * channels + 8
    sub = lax.broadcasted_iota(jnp.int32, (8, LANES), 0)

    def load_row(r):
        body = gather(wide, count, r, 0, 2 * channels)
        tail = gather(wide, count, r, 2 * channels, 8)
        parity = jnp.where(shift[r] == 1, 1.0, 0.0).astype(F32)
        tail = jnp.where(sub == 3, parity, tail)
        return jnp.concatenate([body, tail, jnp.zeros((8, LANES), F32)], axis=0).astype(BF16)

    return load_row


def pack_kernel(signal_hbm, cotangent_hbm, weights_hbm, shift, west_out, east_out,
                signal, cotangent, weights, wide, arrived):
    channels, rows, _ = signal.shape
    block = rows // BLOCKS
    per_row = block // 6
    size = channels // 4
    copies = {(2, 0): pltpu.make_async_copy(weights_hbm, weights, arrived.at[8])}
    for which, (source, target) in enumerate(((signal_hbm, signal), (cotangent_hbm, cotangent))):
        for part in range(4):
            span = pl.ds(part * size, size)
            copies[which, part] = pltpu.make_async_copy(source.at[span], target.at[span], arrived.at[4 * which + part])
    for copy in copies.values():
        copy.start()
    widen_all(signal, cotangent, weights, wide, lambda *key: copies[key].wait())
    load_row = row_loader(channels, rows, shift, wide)
    lane = lane_index((PACKED, LANES))

    def each(t, _):
        west = jnp.zeros((PACKED, LANES), BF16)
        east = jnp.zeros((PACKED, LANES), BF16)
        for b in range(BLOCKS):
            for m in range(6):
                x = load_row(block * b + per_row * m + t)
                first = GROUP * b + 5 * m
                moved = turned(x, first + 5)
                east = jnp.where((lane >= first) & (lane < first + 5), moved, east)
                west = jnp.where((lane - (first + 5)) % LANES < 5, moved, west)
        west_out[t] = west
        east_out[t] = east
        return 0

    lax.fori_loop(0, per_row, each, 0)


def strip_selector():
    source = lax.broadcasted_iota(jnp.int32, (BLOCKS * LANES, LANES), 0)
    lane = lane_index((BLOCKS * LANES, LANES))
    lane_in = lane % GROUP
    wanted = jnp.where(lane_in < SIDE, lane_in - 5, lane_in - SIDE + 117)
    wanted = jnp.where((lane_in >= 5) & (lane_in < SIDE + 11), wanted + LANES * (lane // GROUP), -1)
    return jnp.where(source == wanted, 1.0, 0.0).astype(BF16)


def own_kernel(signal, cotangent, weights_hbm, shift_hbm, mixing_hbm, strips_out, rows_out, mixing_out,
               wide, weights, shift, arrived):
    channels, rows, _ = signal.shape
    block = rows // BLOCKS
    copies = [pltpu.make_async_copy(source, target, arrived.at[i]) for i, (source, target) in enumerate(
        ((weights_hbm, weights), (shift_hbm, shift), (mixing_hbm, mixing_out)))]
    for copy in copies:
        copy.start()
    widen_all(signal, cotangent, weights, wide, lambda which, _: copies[0].wait() if which == 2 else None)
    copies[1].wait()
    load_row = row_loader(channels, rows, shift, wide)
    selector = strip_selector()
    size = 6

    def each(i, _):
        strips = []
        for j in range(size):
            s = i * size + j
            tiles = [load_row(block * b + s) for b in range(BLOCKS)]
            for b in range(BLOCKS):
                rows_out[block * b + s] = tiles[b]
            strips.append(side_by_side(tiles))
        strips = jnp.dot(jnp.concatenate(strips, axis=0), selector, preferred_element_type=F32).astype(BF16)
        for j in range(size):
            strips_out[i * size + j] = strips[PACKED * j:PACKED * (j + 1)]
        return 0

    lax.fori_loop(0, block // size, each, 0)
    copies[2].wait()


def merge_kernel(strips_in, rows_in, from_west, from_east, strips_out, north_out, south_out):
    block = strips_in.shape[0]
    rows = rows_in.shape[0]
    per_row = block // 6
    lane = lane_index((PACKED, LANES))
    lane_in = lane % GROUP

    def each(t, _):
        west = from_west[t]
        east = from_east[t]
        for m in range(6):
            strip = strips_in[per_row * m + t]
            strip = jnp.where(lane_in < 5, turned(west, -5 * m), strip)
            strip = jnp.where(lane_in >= GROUP - 5, turned(east, 22 - 5 * m), strip)
            strips_out[per_row * m + t] = strip
        return 0

    lax.fori_loop(0, per_row, each, 0)
    for out, first_row, first_strip, side in (
        (north_out, 0, 0, 0), (south_out, rows - HALO, block - HALO, BLOCKS - 1)):
        for i in range(HALO):
            out[i] = rows_in[first_row + i]
        corner = turned(strips_out[first_strip], -GROUP * side)
        for g in range(1, BLOCKS):
            piece = turned(strips_out[first_strip + g], GROUP * (g - side))
            corner = jnp.where((lane >= GROUP * g) & (lane < GROUP * (g + 1)), piece, corner)
        out[HALO] = corner
        out[HALO + 1] = turned(strips_out[first_strip + HALO - 1], -GROUP * side)


def write_coefficients(total, first, w_east, w_south, w_diag, parity, keep, coef, shifted):
    count = w_east.shape[0]
    w_back = jnp.where(parity > 0.5, turned(w_diag, 1), turned(w_diag, -1))
    w_west = turned(w_east, 1)
    shifted[0:8, :] = jnp.zeros((8, LANES), F32)
    shifted[8:8 + count, :] = w_south + w_back
    degree = w_east + w_west + w_south + w_diag + shifted[7:7 + count, :]
    third = -1.0 / 3.0
    arrays = [degree * (1.0 / 3.0) - 2.0, w_east * third, w_west * third]
    for array in (w_south, w_diag, w_back):
        arrays.append(array * third if keep is None else array * keep * third)
    for i, array in enumerate(arrays + [parity]):
        coef[i * total + first:i * total + first + count, :] = array


def stencil_steps(order, channels, total, coef, buffers, kept, trips, regions, by_matmul):
    groups = channels // 8
    source = lax.broadcasted_iota(jnp.int32, (LANES, 2 * LANES), 0)
    target = lane_index((LANES, 2 * LANES))
    to_here = jnp.where(target < LANES, (target + 1) % LANES, (target - 1) % LANES)
    shifts = jnp.where(source == to_here, 1.0, 0.0).astype(BF16)

    def coef_row(i, at):
        return coef[pl.ds(i * total + at, 8, stride=0), :]

    def step(position, now, older, newer):
        last = position == order - 1

        def sides(rows):
            if by_matmul:
                both = jnp.dot(jnp.concatenate(rows, axis=0), shifts, preferred_element_type=F32)
                spans = [slice(channels * j, channels * (j + 1)) for j in range(len(rows))]
                return [(both[span, :LANES], both[span, LANES:]) for span in spans]
            return [tuple(pltpu.roll(row, amount, 1).astype(F32) for amount in (LANES - 1, 1)) for row in rows]

        def one_row(at, beside, level, down, before):
            coefs = [coef_row(i, at) for i in range(7)]
            c, e, w, s, d, back, parity = coefs
            here = parity > 0.5
            s_above, d_above, above = before
            new, next_level, next_down = [], [], []
            for g in range(groups):
                span = slice(8 * g, 8 * g + 8)
                v = now[at, span, :]
                v_east, v_west = beside[0][span], beside[1][span]
                value = level[g] + s_above * v + d_above * jnp.where(above, v_east, v_west)
                new.append(value * 0.5 if position == 1 else value)
                value = c * v + e * v_east + w * v_west + down[g]
                next_level.append(value if position == 1 else value - older[at, span, :])
                next_down.append(s * v + back * jnp.where(here, v_west, v_east))
            if not last:
                for g in range(groups):
                    newer[at - 1, 8 * g:8 * g + 8, :] = new[g]
            for h in range(groups // 2):
                first = channels * position + 16 * h
                pair = jnp.concatenate([new[2 * h], new[2 * h + 1]], axis=0)
                kept[at - 1, first:first + 16, :] = pair.astype(BF16)
            return tuple(next_level), tuple(next_down), (s, d, here)

        counts = [-(-(count + 2 - 2 * position) // trips) for _, count in regions]

        def several(trip, carry):
            states, besides = [], []
            field = slice(channels * (position - 1), channels * position)
            for (base, _), count in zip(regions, counts):
                at = base + position + trip * count
                besides.append([kept[at + j, field, :] for j in range(count)])
            flat = iter(sides(sum(besides, [])))
            besides = [[next(flat) for _ in rows] for rows in besides]
            for (base, _), count, (level, down) in zip(regions, counts, carry):
                at = base + position + trip * count
                before = (coef_row(3, at - 1), coef_row(4, at - 1), coef_row(6, at - 1) > 0.5)
                states.append([at, level, down, before])
            for j in range(max(counts)):
                for state, count, beside in zip(states, counts, besides):
                    if j < count:
                        state[1:] = one_row(state[0] + j, beside[j], *state[1:])
            return tuple((level, down) for _, level, down, _ in states)

        zeros = tuple(jnp.zeros((8, LANES), F32) for _ in range(groups))
        lax.fori_loop(0, trips, several, tuple((zeros, zeros) for _ in regions))

    for position in range(1, order):
        step(position, buffers[(position - 1) % 3], buffers[(position - 2) % 3], buffers[position % 3])


def zero_guards(buffers, coef, total, guards):
    for first, end in guards:
        for index in range(first, end):
            for buffer in buffers:
                buffer[index] = jnp.zeros(buffer.shape[1:], F32)
        for i in range(7):
            coef[i * total + first:i * total + end, :] = jnp.zeros((end - first, LANES), F32)


CONTRACT_LANES = (((1,), (1,)), ((), ()))
CONTRACT_ROWS = (((0,), (0,)), ((), ()))


def side_by_side(tiles):
    return jnp.concatenate(tiles, axis=1)


class Chain:
    def __init__(self, first, other, mixing, guards, scratch):
        self.buffers, self.kept, self.coef, self.wide = scratch[:3], *scratch[3:6]
        self.paired = scratch[6] if other is not None else None
        self.first, self.other, self.mixing = first, other, mixing
        self.order, self.channels = mixing.shape[:2]
        self.total = self.kept.shape[0]
        zero_guards(self.buffers, self.coef, self.total, guards)
        for begin, end in guards:
            for i in range(4):
                at = i * (self.total + 1)
                self.wide[at + begin:at + end, :] = jnp.zeros((end - begin, LANES), F32)

    def put(self, index, ref, at, tile=None):
        def part(begin, count):
            return ref[at, begin:begin + count, :] if tile is None else tile[begin:begin + count]
        self.wide[pl.ds(index, 8, stride=self.total + 1), :] = part(PACKED - 16, 16).astype(F32)[:8]
        field = part(self.first, self.channels)
        self.buffers[0][index] = field.astype(F32)
        self.kept[index, 0:self.channels, :] = field
        if self.other is not None:
            self.paired[index] = part(self.other, self.channels)

    def put_all(self, index, ref, unroll):
        count = ref.shape[0]

        def several(i, _):
            for j in range(unroll):
                self.put(index + i * unroll + j, ref, i * unroll + j)
            return 0

        lax.fori_loop(0, count // unroll, several, 0)

    def put_strips(self, strips, north, south):
        block = strips.shape[0]
        self.put_all(1 + HALO, strips, 8)
        lane = lane_index((PACKED, LANES))
        for i in range(HALO):
            at_end = i == HALO - 1
            above = turned(strips[block - HALO + i], GROUP)
            corner = turned(north[HALO + at_end], 0 if at_end else -GROUP * i)
            self.put(1 + i, None, None, jnp.where(lane < GROUP, corner, above))
            below = turned(strips[i], -GROUP)
            corner = turned(south[HALO + at_end], -GROUP - (0 if at_end else GROUP * i))
            self.put(1 + HALO + block + i, None, None, jnp.where(lane >= LANES - GROUP, corner, below))

    def run(self, trips, regions, closed=None):
        total = self.total
        starts = [i * (total + 1) for i in range(4)]
        w_east, w_south, w_diag, parity = [self.wide[at:at + total, :] for at in starts]
        keep = None
        if closed is not None:
            is_end, where = closed
            row = lax.broadcasted_iota(jnp.int32, (total, LANES), 0)
            keep = jnp.where(where(row, lane_index((total, LANES))) & is_end, 0.0, 1.0).astype(F32)
        write_coefficients(total, 0, w_east, w_south, w_diag, parity, keep, self.coef, self.wide)
        stencil_steps(self.order, self.channels, total, self.coef, self.buffers, self.kept, trips, regions,
                      self.other is not None)

    def terms(self, indices):
        return side_by_side([self.kept[i] for i in indices])

    def mixed(self, terms):
        if self.other is not None:
            matrix = self.mixing[...].reshape(self.order * self.channels, self.channels)
            value = lax.dot_general(matrix, terms, CONTRACT_ROWS, preferred_element_type=F32)
        else:
            matrix = side_by_side([self.mixing[k] for k in range(self.order)])
            value = jnp.dot(matrix, terms, preferred_element_type=F32)
        return value.astype(BF16)

    def paired_with(self, indices, valid, terms):
        left = [jnp.where(valid, self.paired[i], jnp.zeros((), BF16)) for i in indices]
        return lax.dot_general(side_by_side(left), terms, CONTRACT_LANES, preferred_element_type=F32)


def valid_lanes(channels):
    lane = lane_index((channels, LANES))
    lane_in = lane % GROUP
    in_strips = ((lane_in >= 5) & (lane_in < 10)) | ((lane_in >= SIDE + 6) & (lane_in < SIDE + 11))
    return (lane >= HALO) & (lane < LANES - HALO), in_strips


def main_forward(rows_in, mixing, out, grad, *scratch):
    rows = rows_in.shape[0]
    order, channels = mixing.shape[:2]
    chain = Chain(0, channels, mixing, ((0, 1), (rows + 1, rows + 8)), scratch)
    chain.put_all(1, rows_in, 16)
    chain.run(rows // 16, ((0, rows),))
    valid, _ = valid_lanes(channels)

    def products(start, count, total_grad):
        indices = [start + 1 + i for i in range(count)]
        terms = chain.terms(indices)
        value = chain.mixed(terms)
        for i in range(count):
            out[start + i] = value[:, LANES * i:LANES * (i + 1)]
        return total_grad + chain.paired_with(indices, valid, terms)

    inner = rows - 2 * HALO
    total_grad = jnp.zeros(grad.shape, F32)
    total_grad = lax.fori_loop(0, inner // 16, lambda i, g: products(HALO + i * 16, 16, g), total_grad)
    if inner % 16:
        total_grad = products(HALO + inner // 16 * 16, inner % 16, total_grad)
    grad[...] = total_grad


def main_backward(is_last, rows_in, north, south, mixing, summed, out, summed_out, *scratch):
    rows = rows_in.shape[0]
    channels = mixing.shape[1]
    count = rows + 2 * HALO
    chain = Chain(channels, None, mixing, ((0, 1), (count + 1, scratch[0].shape[0])), scratch)
    for i in range(HALO):
        chain.put(1 + i, north, i)
        chain.put(1 + HALO + rows + i, south, i)
    chain.put_all(1 + HALO, rows_in, 16)
    chain.run(7, ((0, count),), (is_last[0] == 1, lambda row, lane: row == HALO + rows))

    def products(i, _):
        value = chain.mixed(chain.terms([1 + HALO + i * 16 + j for j in range(16)]))
        for j in range(16):
            out[i * 16 + j] = value[:, LANES * j:LANES * (j + 1)]
        return 0

    lax.fori_loop(0, rows // 16, products, 0)
    summed_out[...] = summed[...]


def edge_sizes(rows):
    block = rows // BLOCKS
    strips = block + 2 * HALO
    top = strips + 6
    bottom = top + BAND + 5
    return block, top, bottom, -(-(bottom + BAND + 5) // 8) * 8


def edge_forward(is_last, strips_in, rows_in, north, south, mixing, out, grad, *scratch):
    rows = rows_in.shape[0]
    block, top, bottom, total = edge_sizes(rows)
    channels = mixing.shape[1]
    count = block + 2 * HALO
    chain = Chain(0, channels, mixing, ((0, 1), (1 + count, top + 1), (top + 1 + BAND, bottom + 1),
                                        (bottom + 1 + BAND, total)), scratch)
    chain.put_strips(strips_in, north, south)
    for i in range(HALO):
        chain.put(top + 1 + i, north, i)
        chain.put(bottom + 1 + 2 * HALO + i, south, i)
    for i in range(2 * HALO):
        chain.put(top + 1 + HALO + i, rows_in, i)
        chain.put(bottom + 1 + i, rows_in, rows - 2 * HALO + i)

    def closed(row, lane):
        return (row == bottom + 2 * HALO) | ((row == HALO + block) & (lane >= LANES - GROUP))

    chain.run(3, ((0, count), (top, BAND), (bottom, BAND)), (is_last[0] == 1, closed))
    main_valid, strip_valid = valid_lanes(channels)
    strip_rows = [1 + HALO + i for i in range(block)]
    band_rows = [top + 1 + HALO + i for i in range(HALO)] + [bottom + 1 + HALO + i for i in range(HALO)]
    total_grad = jnp.zeros(grad.shape, F32)
    slot = 0
    for indices, valid in ((strip_rows, strip_valid), (band_rows, main_valid)):
        terms = chain.terms(indices)
        value = chain.mixed(terms)
        for i in range(len(indices)):
            out[slot + i] = value[:, LANES * i:LANES * (i + 1)]
        slot += len(indices)
        total_grad = total_grad + chain.paired_with(indices, valid, terms)
    grad[...] = total_grad


def edge_backward(is_last, strips_in, north, south, mixing, summed, out, summed_out, *scratch):
    block = strips_in.shape[0]
    count = block + 2 * HALO
    chain = Chain(mixing.shape[1], None, mixing, ((0, 1), (1 + count, scratch[0].shape[0])), scratch)
    chain.put_strips(strips_in, north, south)
    chain.run(2, ((0, count),), (is_last[0] == 1, lambda row, lane: (row == HALO + block) & (lane >= LANES - GROUP)))
    value = chain.mixed(chain.terms([1 + HALO + i for i in range(block)]))
    for i in range(block):
        out[i] = value[:, LANES * i:LANES * (i + 1)]
    summed_out[...] = summed[...]


def assemble_kernel(main, edges, summed, out_hbm, summed_out, wide, out, sent):
    summed_out[...] = summed[...]
    rows, channels, _ = main.shape
    block = rows // BLOCKS
    lane = lane_index((channels, LANES))

    def put(r, s, b, value):
        strip = edges[s]
        west = turned(strip, -(GROUP * b + 5))
        east = turned(strip, LANES - 5 - (GROUP * b + SIDE + 6))
        value = jnp.where(lane < HALO, west, jnp.where(lane >= LANES - HALO, east, value))
        wide[pl.ds(r * (3 * channels + 1), channels, stride=3), :] = value.astype(F32)

    for b in range(BLOCKS):
        def several(i, _, b=b):
            for j in range(8):
                s = i * 8 + j
                put(block * b + s, s, b, main[block * b + s])
            return 0
        lax.fori_loop(0, block // 8, several, 0)
    if edges.shape[0] > block:
        for i in range(HALO):
            put(i, i, 0, edges[block + i])
            put(rows - HALO + i, block - HALO + i, BLOCKS - 1, edges[block + HALO + i])

    pieces = 4
    size = channels // pieces

    def narrow(i, _):
        for j in range(size):
            o = i * size + j
            out[o] = wide[pl.ds(3 * o, rows, stride=3 * channels + 1), :].astype(BF16)
        copy(i).start()
        return 0

    def copy(i):
        span = pl.ds(i * size, size)
        return pltpu.make_async_copy(out.at[span], out_hbm.at[span], sent.at[i])

    lax.fori_loop(0, pieces, narrow, 0)
    for i in range(pieces):
        copy(i).wait()


def finish_kernel(scale, mine, theirs, out):
    order, channels = out.shape[:2]
    out[...] = ((mine[...] + theirs[...]) * scale).T.reshape(order, channels, channels)


def on_device(signal, cotangent, edge_weights, circle_shift, mixing):
    channels, rows, sector = signal.shape
    order = mixing.shape[0]
    block, top, bottom, edge_total = edge_sizes(rows)
    lat, lon = lax.axis_size("lat"), lax.axis_size("lon")
    vmem = pl.BlockSpec(memory_space=pltpu.VMEM)
    smem = pl.BlockSpec(memory_space=pltpu.SMEM)
    hbm = pl.BlockSpec(memory_space=pltpu.HBM)
    shape = jax.ShapeDtypeStruct

    def packed(count):
        return shape((count, PACKED, LANES), BF16)

    def weighs(mib):
        return pl.CostEstimate(flops=0, bytes_accessed=mib * 1024 * 1024, transcendentals=0)

    all_wide = pltpu.VMEM((spread_size(2 * channels + 8, rows), LANES), F32)
    raw = (signal, cotangent, edge_weights, circle_shift)
    to_west, to_east = pl.pallas_call(
        pack_kernel,
        out_shape=(packed(block // 6), packed(block // 6)),
        in_specs=[hbm, hbm, hbm, smem],
        out_specs=(vmem, vmem),
        scratch_shapes=[
            pltpu.VMEM(signal.shape, BF16),
            pltpu.VMEM(signal.shape, BF16),
            pltpu.VMEM(edge_weights.shape, BF16),
            all_wide,
            pltpu.SemaphoreType.DMA((9,)),
        ],
        compiler_params=pltpu.CompilerParams(vmem_limit_bytes=PACK_VMEM),
        name="pack",
    )(*raw)

    eastward = [(i, (i + 1) % lon) for i in range(lon)]
    westward = [(j, i) for i, j in eastward]
    from_west = lax.ppermute(to_east, "lon", eastward)
    from_east = lax.ppermute(to_west, "lon", westward)

    own_strips, rows_in, mixing = pl.pallas_call(
        own_kernel,
        out_shape=(packed(block), packed(rows), shape(mixing.shape, BF16)),
        in_specs=[vmem, vmem, hbm, hbm, hbm],
        out_specs=(vmem, vmem, vmem),
        scratch_shapes=[
            all_wide,
            pltpu.VMEM(edge_weights.shape, BF16),
            pltpu.SMEM(circle_shift.shape, jnp.int32),
            pltpu.SemaphoreType.DMA((3,)),
        ],
        compiler_params=params(20),
        cost_estimate=weighs(8),
        name="own",
    )(*raw, mixing)

    strips, to_north, to_south = pl.pallas_call(
        merge_kernel,
        out_shape=(packed(block), packed(HALO + 2), packed(HALO + 2)),
        in_specs=[vmem] * 4,
        out_specs=(vmem,) * 3,
        compiler_params=params(8),
        name="merge",
    )(own_strips, rows_in, from_west, from_east)

    southward = [(i, i + 1) for i in range(lat - 1)]
    northward = [(j, i) for i, j in southward]
    north = lax.ppermute(to_south, "lat", southward)
    south = lax.ppermute(to_north, "lat", northward)

    rows_first = shape((rows, channels, LANES), BF16)
    grad_shape = shape((channels, order * channels), F32)

    def chain_scratch(total, with_pairs):
        scratch = [pltpu.VMEM((total, channels, LANES), F32)] * 3 + [
            pltpu.VMEM((total, order * channels, LANES), BF16),
            pltpu.VMEM((7 * total, LANES), F32),
            pltpu.VMEM((8 * (total + 1), LANES), F32),
        ]
        return scratch + [pltpu.VMEM((total, channels, LANES), BF16)] * with_pairs

    main_f, grad_main = pl.pallas_call(
        main_forward,
        out_shape=(rows_first, grad_shape),
        in_specs=[vmem, vmem],
        out_specs=(vmem, vmem),
        scratch_shapes=chain_scratch(rows + 8, True),
        compiler_params=params(20),
        cost_estimate=weighs(24),
        name="main_forward",
    )(rows_in, mixing)

    is_last = (lax.axis_index("lat") == lat - 1).astype(jnp.int32).reshape(1)
    edge_f, grad_edge = pl.pallas_call(
        edge_forward,
        out_shape=(shape((block + 2 * HALO, channels, LANES), BF16), grad_shape),
        in_specs=[smem] + [vmem] * 5,
        out_specs=(vmem, vmem),
        scratch_shapes=chain_scratch(edge_total, True),
        compiler_params=params(16),
        cost_estimate=weighs(12),
        name="edge_forward",
    )(is_last, strips, rows_in, north, south, mixing)

    rounds = []
    for axis, devices in (("lon", lon), ("lat", lat)):
        reach = 1
        while reach < devices:
            rounds.append((axis, [(i, i ^ reach) for i in range(devices)]))
            reach *= 2
    rounds = [r for r in rounds if r[0] == "lon"] + [r for r in rounds if r[0] == "lat"][::-1]

    results = {}

    def run_main_backward(share):
        results["main"], share = pl.pallas_call(
            main_backward,
            out_shape=(rows_first, grad_shape),
            in_specs=[smem] + [vmem] * 5,
            out_specs=(vmem, vmem),
            scratch_shapes=chain_scratch(-(-(rows + 2 * HALO + 8) // 8) * 8, False),
            compiler_params=params(20),
            cost_estimate=weighs(24),
            name="main_backward",
        )(is_last, rows_in, north, south, mixing, share)
        return share

    def run_edge_backward(share):
        results["edge"], share = pl.pallas_call(
            edge_backward,
            out_shape=(shape((block, channels, LANES), BF16), grad_shape),
            in_specs=[smem] + [vmem] * 5,
            out_specs=(vmem, vmem),
            scratch_shapes=chain_scratch(-(-(block + 2 * HALO + 8) // 8) * 8, False),
            compiler_params=params(12),
            cost_estimate=weighs(12),
            name="edge_backward",
        )(is_last, strips, north, south, mixing, share)
        return share

    def assemble(main, edges, share, name):
        return pl.pallas_call(
            assemble_kernel,
            out_shape=(shape(signal.shape, BF16), grad_shape),
            in_specs=[vmem] * 3,
            out_specs=(hbm, vmem),
            scratch_shapes=[
                pltpu.VMEM((spread_size(channels, rows), LANES), F32),
                pltpu.VMEM(signal.shape, BF16),
                pltpu.SemaphoreType.DMA((4,)),
            ],
            compiler_params=params(12),
            cost_estimate=weighs(8),
            name=name,
        )(main, edges, share)

    def run_assemble_forward(share):
        results["output"], share = assemble(main_f, edge_f, share, "assemble_forward")
        return share

    def run_assemble_backward(share):
        results["signal_grad"], share = assemble(results["main"], results["edge"], share, "assemble_backward")
        return share

    beside = [run_main_backward, run_assemble_forward, run_edge_backward, run_assemble_backward]
    share = grad_main + grad_edge
    theirs = jnp.zeros_like(share)
    for number in range(max(len(rounds), len(beside))):
        if number:
            share = share + theirs
        theirs = lax.ppermute(share, *rounds[number]) if number < len(rounds) else jnp.zeros_like(share)
        if number < len(beside):
            share = beside[number](share)

    norm_scale = 1.0 / math.sqrt(rows * lat * sector * lon)
    mixing_grad = pl.pallas_call(
        functools.partial(finish_kernel, norm_scale),
        out_shape=shape(mixing.shape, F32),
        in_specs=[vmem, vmem],
        out_specs=vmem,
        compiler_params=params(4),
        name="finish",
    )(share, theirs)
    return (results["output"], results["signal_grad"], mixing_grad)


def solution(mesh):
    in_specs = (P(None, "lat", "lon"), P(None, "lat", "lon"), P(None, "lat", "lon"), P("lat"), P())
    out_specs = (P(None, "lat", "lon"), P(None, "lat", "lon"), P())
    return jax.shard_map(
        on_device, mesh=mesh, in_specs=in_specs, out_specs=out_specs, check_vma=False
    )
```

```python
import functools
import math

import jax
import jax.numpy as jnp
from jax import lax
from jax.experimental import pallas as pl
from jax.experimental.pallas import tpu as pltpu
from jax.sharding import PartitionSpec as P

F32 = jnp.float32
BF16 = jnp.bfloat16
HALO = 5
LANES = 128
BLOCKS = 4
GROUP = LANES // BLOCKS
SIDE = GROUP // 2
PACKED = 80
BAND = 3 * HALO
PACK_VMEM = 63_400_000


def params(mib):
    return pltpu.CompilerParams(vmem_limit_bytes=mib * 1024 * 1024)


def lane_index(shape):
    return lax.broadcasted_iota(jnp.int32, shape, len(shape) - 1)


def turned(x, amount):
    amount = amount % LANES
    return pltpu.roll(x, amount, 1) if amount else x


def spread_size(channels, rows):
    return rows * (3 * channels + 1)


def spread(wide, channels, c, rows, x):
    wide[pl.ds(3 * c, rows, stride=3 * channels + 1), :] = x


def gather(wide, channels, r, first, count):
    return wide[pl.ds(r * (3 * channels + 1) + 3 * first, count, stride=3), :]


def widen_all(signal, cotangent, weights, wide, ready=None):
    channels, rows, _ = signal.shape
    count = 2 * channels + 8
    for which, source in enumerate((signal, cotangent)):
        for part in range(4):
            if ready is not None:
                ready(which, part)
            size = channels // 4

            def widen(i, _):
                for j in range(4):
                    c = part * size + i * 4 + j
                    spread(wide, count, which * channels + c, rows, source[c].astype(F32))
                return 0

            lax.fori_loop(0, size // 4, widen, 0)
    if ready is not None:
        ready(2, 0)
    for i in range(8):
        x = weights[i].astype(F32) if i < 3 else jnp.zeros((rows, LANES), F32)
        spread(wide, count, 2 * channels + i, rows, x)


def row_loader(channels, rows, shift, wide):
    count = 2 * channels + 8
    sub = lax.broadcasted_iota(jnp.int32, (8, LANES), 0)

    def load_row(r):
        body = gather(wide, count, r, 0, 2 * channels)
        tail = gather(wide, count, r, 2 * channels, 8)
        parity = jnp.where(shift[r] == 1, 1.0, 0.0).astype(F32)
        tail = jnp.where(sub == 3, parity, tail)
        return jnp.concatenate([body, tail, jnp.zeros((8, LANES), F32)], axis=0).astype(BF16)

    return load_row


def pack_kernel(signal_hbm, cotangent_hbm, weights_hbm, shift, west_out, east_out,
                signal, cotangent, weights, wide, arrived):
    channels, rows, _ = signal.shape
    block = rows // BLOCKS
    per_row = block // 6
    size = channels // 4
    copies = {(2, 0): pltpu.make_async_copy(weights_hbm, weights, arrived.at[8])}
    for which, (source, target) in enumerate(((signal_hbm, signal), (cotangent_hbm, cotangent))):
        for part in range(4):
            span = pl.ds(part * size, size)
            copies[which, part] = pltpu.make_async_copy(source.at[span], target.at[span], arrived.at[4 * which + part])
    for copy in copies.values():
        copy.start()
    widen_all(signal, cotangent, weights, wide, lambda *key: copies[key].wait())
    load_row = row_loader(channels, rows, shift, wide)
    lane = lane_index((PACKED, LANES))

    def each(t, _):
        west = jnp.zeros((PACKED, LANES), BF16)
        east = jnp.zeros((PACKED, LANES), BF16)
        for b in range(BLOCKS):
            for m in range(6):
                x = load_row(block * b + per_row * m + t)
                first = GROUP * b + 5 * m
                moved = turned(x, first + 5)
                east = jnp.where((lane >= first) & (lane < first + 5), moved, east)
                west = jnp.where((lane - (first + 5)) % LANES < 5, moved, west)
        west_out[t] = west
        east_out[t] = east
        return 0

    lax.fori_loop(0, per_row, each, 0)


def strip_selector():
    source = lax.broadcasted_iota(jnp.int32, (BLOCKS * LANES, LANES), 0)
    lane = lane_index((BLOCKS * LANES, LANES))
    lane_in = lane % GROUP
    wanted = jnp.where(lane_in < SIDE, lane_in - 5, lane_in - SIDE + 117)
    wanted = jnp.where((lane_in >= 5) & (lane_in < SIDE + 11), wanted + LANES * (lane // GROUP), -1)
    return jnp.where(source == wanted, 1.0, 0.0).astype(BF16)


def own_kernel(signal, cotangent, weights_hbm, shift_hbm, mixing_hbm, strips_out, rows_out, mixing_out,
               wide, weights, shift, arrived):
    channels, rows, _ = signal.shape
    block = rows // BLOCKS
    copies = [pltpu.make_async_copy(source, target, arrived.at[i]) for i, (source, target) in enumerate(
        ((weights_hbm, weights), (shift_hbm, shift), (mixing_hbm, mixing_out)))]
    for copy in copies:
        copy.start()
    widen_all(signal, cotangent, weights, wide, lambda which, _: copies[0].wait() if which == 2 else None)
    copies[1].wait()
    load_row = row_loader(channels, rows, shift, wide)
    selector = strip_selector()
    size = 6

    def each(i, _):
        strips = []
        for j in range(size):
            s = i * size + j
            tiles = [load_row(block * b + s) for b in range(BLOCKS)]
            for b in range(BLOCKS):
                rows_out[block * b + s] = tiles[b]
            strips.append(side_by_side(tiles))
        strips = jnp.dot(jnp.concatenate(strips, axis=0), selector, preferred_element_type=F32).astype(BF16)
        for j in range(size):
            strips_out[i * size + j] = strips[PACKED * j:PACKED * (j + 1)]
        return 0

    lax.fori_loop(0, block // size, each, 0)
    copies[2].wait()


def merge_kernel(strips_in, rows_in, from_west, from_east, strips_out, north_out, south_out):
    block = strips_in.shape[0]
    rows = rows_in.shape[0]
    per_row = block // 6
    lane = lane_index((PACKED, LANES))
    lane_in = lane % GROUP

    def each(t, _):
        west = from_west[t]
        east = from_east[t]
        for m in range(6):
            strip = strips_in[per_row * m + t]
            strip = jnp.where(lane_in < 5, turned(west, -5 * m), strip)
            strip = jnp.where(lane_in >= GROUP - 5, turned(east, 22 - 5 * m), strip)
            strips_out[per_row * m + t] = strip
        return 0

    lax.fori_loop(0, per_row, each, 0)
    for out, first_row, first_strip, side in (
        (north_out, 0, 0, 0), (south_out, rows - HALO, block - HALO, BLOCKS - 1)):
        for i in range(HALO):
            out[i] = rows_in[first_row + i]
        corner = turned(strips_out[first_strip], -GROUP * side)
        for g in range(1, BLOCKS):
            piece = turned(strips_out[first_strip + g], GROUP * (g - side))
            corner = jnp.where((lane >= GROUP * g) & (lane < GROUP * (g + 1)), piece, corner)
        out[HALO] = corner
        out[HALO + 1] = turned(strips_out[first_strip + HALO - 1], -GROUP * side)


def write_coefficients(total, w_east, w_south, w_diag, parity, keep, coef, shifted):
    count = w_east.shape[0]
    w_back = jnp.where(parity > 0.5, turned(w_diag, 1), turned(w_diag, -1))
    w_west = turned(w_east, 1)
    shifted[0:8, :] = jnp.zeros((8, LANES), F32)
    shifted[8:8 + count, :] = w_south + w_back
    degree = w_east + w_west + w_south + w_diag + shifted[7:7 + count, :]
    third = -1.0 / 3.0
    arrays = [degree * (1.0 / 3.0) - 2.0, w_east * third, w_west * third]
    for array in (w_south, w_diag, w_back):
        arrays.append(array * third if keep is None else array * keep * third)
    arrays.append(parity)
    for i, array in enumerate(arrays):
        shifted[i * total:(i + 1) * total, :] = array

    def several(trip, _):
        for j in range(8):
            row = trip * 8 + j
            for i in range(len(arrays)):
                coef[i, row] = shifted[pl.ds(i * total + row, 8, stride=0), :]
        return 0

    lax.fori_loop(0, total // 8, several, 0)


def stencil_steps(order, channels, total, coef, buffers, kept, trips, regions, packed):
    groups = channels // 8

    def coef_row(i, at):
        return coef[i, at]

    def step(position, now, older, newer):
        last = position == order - 1

        def sides(rows):
            return [tuple(pltpu.roll(row, amount, 1).astype(F32) for amount in (LANES - 1, 1)) for row in rows]

        def one_row(at, beside, level, down, before):
            coefs = [coef_row(i, at) for i in range(7)]
            c, e, w, s, d, back, parity = coefs
            here = parity > 0.5
            s_above, d_above, above = before
            new, next_level, next_down = [], [], []
            for g in range(groups):
                span = slice(8 * g, 8 * g + 8)
                v = now[at, span, :]
                if packed:
                    v_east, v_west = beside[0][span], beside[1][span]
                else:
                    v_east, v_west = pltpu.roll(v, LANES - 1, 1), pltpu.roll(v, 1, 1)
                value = level[g] + s_above * v + d_above * jnp.where(above, v_east, v_west)
                new.append(value * 0.5 if position == 1 else value)
                value = c * v + e * v_east + w * v_west + down[g]
                next_level.append(value if position == 1 else value - older[at, span, :])
                next_down.append(s * v + back * jnp.where(here, v_west, v_east))
            if not last:
                for g in range(groups):
                    newer[at - 1, 8 * g:8 * g + 8, :] = new[g]
            for h in range(groups // 2):
                first = channels * position + 16 * h
                pair = jnp.concatenate([new[2 * h], new[2 * h + 1]], axis=0)
                kept[at - 1, first:first + 16, :] = pair.astype(BF16)
            return tuple(next_level), tuple(next_down), (s, d, here)

        counts = [-(-(count + 2 - 2 * position) // trips) for _, count in regions]

        def several(trip, carry):
            states, besides = [], []
            field = slice(channels * (position - 1), channels * position)
            for (base, _), count in zip(regions, counts):
                at = base + position + trip * count
                besides.append([kept[at + j, field, :] for j in range(count)])
            besides = [sides(rows) if packed else rows for rows in besides]
            for (base, _), count, (level, down) in zip(regions, counts, carry):
                at = base + position + trip * count
                before = (coef_row(3, at - 1), coef_row(4, at - 1), coef_row(6, at - 1) > 0.5)
                states.append([at, level, down, before])
            for j in range(max(counts)):
                for state, count, beside in zip(states, counts, besides):
                    if j < count:
                        state[1:] = one_row(state[0] + j, beside[j], *state[1:])
            return tuple((level, down) for _, level, down, _ in states)

        zeros = tuple(jnp.zeros((8, LANES), F32) for _ in range(groups))
        lax.fori_loop(0, trips, several, tuple((zeros, zeros) for _ in regions))

    for position in range(1, order):
        step(position, buffers[(position - 1) % 3], buffers[(position - 2) % 3], buffers[position % 3])


def zero_guards(buffers, guards):
    for first, end in guards:
        for index in range(first, end):
            for buffer in buffers:
                buffer[index] = jnp.zeros(buffer.shape[1:], F32)


CONTRACT_LANES = (((1,), (1,)), ((), ()))
CONTRACT_ROWS = (((0,), (0,)), ((), ()))


def side_by_side(tiles):
    return jnp.concatenate(tiles, axis=1)


class Chain:
    def __init__(self, first, other, mixing, guards, scratch):
        self.buffers, self.kept, self.coef, self.wide = scratch[:3], *scratch[3:6]
        self.paired = scratch[6] if other is not None else None
        self.first, self.other, self.mixing = first, other, mixing
        self.order, self.channels = mixing.shape[:2]
        self.total = self.kept.shape[0]
        zero_guards(self.buffers, guards)
        for begin, end in guards:
            for i in range(4):
                at = i * (self.total + 1)
                self.wide[at + begin:at + end, :] = jnp.zeros((end - begin, LANES), F32)

    def put(self, index, ref, at, tile=None):
        def part(begin, count):
            return ref[at, begin:begin + count, :] if tile is None else tile[begin:begin + count]
        self.wide[pl.ds(index, 8, stride=self.total + 1), :] = part(PACKED - 16, 16).astype(F32)[:8]
        field = part(self.first, self.channels)
        self.buffers[0][index] = field.astype(F32)
        self.kept[index, 0:self.channels, :] = field
        if self.other is not None:
            self.paired[index] = part(self.other, self.channels)

    def put_all(self, index, ref, unroll):
        count = ref.shape[0]

        def several(i, _):
            for j in range(unroll):
                self.put(index + i * unroll + j, ref, i * unroll + j)
            return 0

        lax.fori_loop(0, count // unroll, several, 0)

    def put_strips(self, strips, north, south):
        block = strips.shape[0]
        self.put_all(1 + HALO, strips, 8)
        lane = lane_index((PACKED, LANES))
        for i in range(HALO):
            at_end = i == HALO - 1
            above = turned(strips[block - HALO + i], GROUP)
            corner = turned(north[HALO + at_end], 0 if at_end else -GROUP * i)
            self.put(1 + i, None, None, jnp.where(lane < GROUP, corner, above))
            below = turned(strips[i], -GROUP)
            corner = turned(south[HALO + at_end], -GROUP - (0 if at_end else GROUP * i))
            self.put(1 + HALO + block + i, None, None, jnp.where(lane >= LANES - GROUP, corner, below))

    def run(self, trips, regions, closed=None):
        total = self.total
        starts = [i * (total + 1) for i in range(4)]
        w_east, w_south, w_diag, parity = [self.wide[at:at + total, :] for at in starts]
        keep = None
        if closed is not None:
            is_end, where = closed
            row = lax.broadcasted_iota(jnp.int32, (total, LANES), 0)
            keep = jnp.where(where(row, lane_index((total, LANES))) & is_end, 0.0, 1.0).astype(F32)
        write_coefficients(total, w_east, w_south, w_diag, parity, keep, self.coef, self.wide)
        stencil_steps(self.order, self.channels, total, self.coef, self.buffers, self.kept, trips, regions,
                      self.other is None)

    def terms(self, indices):
        return side_by_side([self.kept[i] for i in indices])

    def mixed(self, terms):
        if self.other is not None:
            matrix = self.mixing[...].reshape(self.order * self.channels, self.channels)
            value = lax.dot_general(matrix, terms, CONTRACT_ROWS, preferred_element_type=F32)
        else:
            matrix = side_by_side([self.mixing[k] for k in range(self.order)])
            value = jnp.dot(matrix, terms, preferred_element_type=F32)
        return value.astype(BF16)

    def paired_with(self, indices, valid, terms):
        left = [jnp.where(valid, self.paired[i], jnp.zeros((), BF16)) for i in indices]
        return lax.dot_general(side_by_side(left), terms, CONTRACT_LANES, preferred_element_type=F32)


def valid_lanes(channels):
    lane = lane_index((channels, LANES))
    lane_in = lane % GROUP
    in_strips = ((lane_in >= 5) & (lane_in < 10)) | ((lane_in >= SIDE + 6) & (lane_in < SIDE + 11))
    return (lane >= HALO) & (lane < LANES - HALO), in_strips


def main_forward(rows_in, mixing, out, grad, *scratch):
    rows = rows_in.shape[0]
    order, channels = mixing.shape[:2]
    chain = Chain(0, channels, mixing, ((0, 1), (rows + 1, rows + 8)), scratch)
    chain.put_all(1, rows_in, 16)
    chain.run(rows // 16, ((0, rows),))
    valid, _ = valid_lanes(channels)

    def products(start, count, total_grad):
        indices = [start + 1 + i for i in range(count)]
        terms = chain.terms(indices)
        value = chain.mixed(terms)
        for i in range(count):
            out[start + i] = value[:, LANES * i:LANES * (i + 1)]
        return total_grad + chain.paired_with(indices, valid, terms)

    inner = rows - 2 * HALO
    total_grad = jnp.zeros(grad.shape, F32)
    total_grad = lax.fori_loop(0, inner // 16, lambda i, g: products(HALO + i * 16, 16, g), total_grad)
    if inner % 16:
        total_grad = products(HALO + inner // 16 * 16, inner % 16, total_grad)
    grad[...] = total_grad


def main_backward(is_last, rows_in, north, south, mixing, summed, out, summed_out, *scratch):
    rows = rows_in.shape[0]
    channels = mixing.shape[1]
    count = rows + 2 * HALO
    chain = Chain(channels, None, mixing, ((0, 1), (count + 1, scratch[0].shape[0])), scratch)
    for i in range(HALO):
        chain.put(1 + i, north, i)
        chain.put(1 + HALO + rows + i, south, i)
    chain.put_all(1 + HALO, rows_in, 16)
    chain.run(7, ((0, count),), (is_last[0] == 1, lambda row, lane: row == HALO + rows))

    def products(i, _):
        value = chain.mixed(chain.terms([1 + HALO + i * 16 + j for j in range(16)]))
        for j in range(16):
            out[i * 16 + j] = value[:, LANES * j:LANES * (j + 1)]
        return 0

    lax.fori_loop(0, rows // 16, products, 0)
    summed_out[...] = summed[...]


def edge_sizes(rows):
    block = rows // BLOCKS
    strips = block + 2 * HALO
    top = strips + 6
    bottom = top + BAND + 5
    return block, top, bottom, -(-(bottom + BAND + 5) // 8) * 8


def edge_forward(is_last, strips_in, rows_in, north, south, mixing, out, grad, *scratch):
    rows = rows_in.shape[0]
    block, top, bottom, total = edge_sizes(rows)
    channels = mixing.shape[1]
    count = block + 2 * HALO
    chain = Chain(0, channels, mixing, ((0, 1), (1 + count, top + 1), (top + 1 + BAND, bottom + 1),
                                        (bottom + 1 + BAND, total)), scratch)
    chain.put_strips(strips_in, north, south)
    for i in range(HALO):
        chain.put(top + 1 + i, north, i)
        chain.put(bottom + 1 + 2 * HALO + i, south, i)
    for i in range(2 * HALO):
        chain.put(top + 1 + HALO + i, rows_in, i)
        chain.put(bottom + 1 + i, rows_in, rows - 2 * HALO + i)

    def closed(row, lane):
        return (row == bottom + 2 * HALO) | ((row == HALO + block) & (lane >= LANES - GROUP))

    chain.run(3, ((0, count), (top, BAND), (bottom, BAND)), (is_last[0] == 1, closed))
    main_valid, strip_valid = valid_lanes(channels)
    strip_rows = [1 + HALO + i for i in range(block)]
    band_rows = [top + 1 + HALO + i for i in range(HALO)] + [bottom + 1 + HALO + i for i in range(HALO)]
    total_grad = jnp.zeros(grad.shape, F32)
    slot = 0
    for indices, valid in ((strip_rows, strip_valid), (band_rows, main_valid)):
        terms = chain.terms(indices)
        value = chain.mixed(terms)
        for i in range(len(indices)):
            out[slot + i] = value[:, LANES * i:LANES * (i + 1)]
        slot += len(indices)
        total_grad = total_grad + chain.paired_with(indices, valid, terms)
    grad[...] = total_grad


def edge_backward(is_last, strips_in, north, south, mixing, summed, out, summed_out, *scratch):
    block = strips_in.shape[0]
    count = block + 2 * HALO
    chain = Chain(mixing.shape[1], None, mixing, ((0, 1), (1 + count, scratch[0].shape[0])), scratch)
    chain.put_strips(strips_in, north, south)
    chain.run(2, ((0, count),), (is_last[0] == 1, lambda row, lane: (row == HALO + block) & (lane >= LANES - GROUP)))
    value = chain.mixed(chain.terms([1 + HALO + i for i in range(block)]))
    for i in range(block):
        out[i] = value[:, LANES * i:LANES * (i + 1)]
    summed_out[...] = summed[...]


def assemble_kernel(main, edges, summed, out_hbm, summed_out, wide, out, sent):
    summed_out[...] = summed[...]
    rows, channels, _ = main.shape
    block = rows // BLOCKS
    lane = lane_index((channels, LANES))

    def put(r, s, b, value):
        strip = edges[s]
        west = turned(strip, -(GROUP * b + 5))
        east = turned(strip, LANES - 5 - (GROUP * b + SIDE + 6))
        value = jnp.where(lane < HALO, west, jnp.where(lane >= LANES - HALO, east, value))
        wide[pl.ds(r * (3 * channels + 1), channels, stride=3), :] = value.astype(F32)

    for b in range(BLOCKS):
        def several(i, _, b=b):
            for j in range(8):
                s = i * 8 + j
                put(block * b + s, s, b, main[block * b + s])
            return 0
        lax.fori_loop(0, block // 8, several, 0)
    if edges.shape[0] > block:
        for i in range(HALO):
            put(i, i, 0, edges[block + i])
            put(rows - HALO + i, block - HALO + i, BLOCKS - 1, edges[block + HALO + i])

    pieces = 4
    size = channels // pieces

    def narrow(i, _):
        for j in range(size):
            o = i * size + j
            out[o] = wide[pl.ds(3 * o, rows, stride=3 * channels + 1), :].astype(BF16)
        copy(i).start()
        return 0

    def copy(i):
        span = pl.ds(i * size, size)
        return pltpu.make_async_copy(out.at[span], out_hbm.at[span], sent.at[i])

    lax.fori_loop(0, pieces, narrow, 0)
    for i in range(pieces):
        copy(i).wait()


def finish_kernel(scale, mine, theirs, out):
    order, channels = out.shape[:2]
    out[...] = ((mine[...] + theirs[...]) * scale).T.reshape(order, channels, channels)


def on_device(signal, cotangent, edge_weights, circle_shift, mixing):
    channels, rows, sector = signal.shape
    order = mixing.shape[0]
    block, top, bottom, edge_total = edge_sizes(rows)
    lat, lon = lax.axis_size("lat"), lax.axis_size("lon")
    vmem = pl.BlockSpec(memory_space=pltpu.VMEM)
    smem = pl.BlockSpec(memory_space=pltpu.SMEM)
    hbm = pl.BlockSpec(memory_space=pltpu.HBM)
    shape = jax.ShapeDtypeStruct

    def packed(count):
        return shape((count, PACKED, LANES), BF16)

    def weighs(mib):
        return pl.CostEstimate(flops=0, bytes_accessed=mib * 1024 * 1024, transcendentals=0)

    all_wide = pltpu.VMEM((spread_size(2 * channels + 8, rows), LANES), F32)
    raw = (signal, cotangent, edge_weights, circle_shift)
    to_west, to_east = pl.pallas_call(
        pack_kernel,
        out_shape=(packed(block // 6), packed(block // 6)),
        in_specs=[hbm, hbm, hbm, smem],
        out_specs=(vmem, vmem),
        scratch_shapes=[
            pltpu.VMEM(signal.shape, BF16),
            pltpu.VMEM(signal.shape, BF16),
            pltpu.VMEM(edge_weights.shape, BF16),
            all_wide,
            pltpu.SemaphoreType.DMA((9,)),
        ],
        compiler_params=pltpu.CompilerParams(vmem_limit_bytes=PACK_VMEM),
        name="pack",
    )(*raw)

    eastward = [(i, (i + 1) % lon) for i in range(lon)]
    westward = [(j, i) for i, j in eastward]
    from_west = lax.ppermute(to_east, "lon", eastward)
    from_east = lax.ppermute(to_west, "lon", westward)

    own_strips, rows_in, mixing = pl.pallas_call(
        own_kernel,
        out_shape=(packed(block), packed(rows), shape(mixing.shape, BF16)),
        in_specs=[vmem, vmem, hbm, hbm, hbm],
        out_specs=(vmem, vmem, vmem),
        scratch_shapes=[
            all_wide,
            pltpu.VMEM(edge_weights.shape, BF16),
            pltpu.SMEM(circle_shift.shape, jnp.int32),
            pltpu.SemaphoreType.DMA((3,)),
        ],
        compiler_params=params(20),
        cost_estimate=weighs(8),
        name="own",
    )(*raw, mixing)

    strips, to_north, to_south = pl.pallas_call(
        merge_kernel,
        out_shape=(packed(block), packed(HALO + 2), packed(HALO + 2)),
        in_specs=[vmem] * 4,
        out_specs=(vmem,) * 3,
        compiler_params=params(8),
        name="merge",
    )(own_strips, rows_in, from_west, from_east)

    southward = [(i, i + 1) for i in range(lat - 1)]
    northward = [(j, i) for i, j in southward]
    north = lax.ppermute(to_south, "lat", southward)
    south = lax.ppermute(to_north, "lat", northward)

    rows_first = shape((rows, channels, LANES), BF16)
    grad_shape = shape((channels, order * channels), F32)

    def chain_scratch(total, with_pairs):
        scratch = [pltpu.VMEM((total, channels, LANES), F32)] * 3 + [
            pltpu.VMEM((total, order * channels, LANES), BF16),
            pltpu.VMEM((7, total, 8, LANES), F32),
            pltpu.VMEM((8 * (total + 1), LANES), F32),
        ]
        return scratch + [pltpu.VMEM((total, channels, LANES), BF16)] * with_pairs

    main_f, grad_main = pl.pallas_call(
        main_forward,
        out_shape=(rows_first, grad_shape),
        in_specs=[vmem, vmem],
        out_specs=(vmem, vmem),
        scratch_shapes=chain_scratch(rows + 8, True),
        compiler_params=params(20),
        cost_estimate=weighs(24),
        name="main_forward",
    )(rows_in, mixing)

    is_last = (lax.axis_index("lat") == lat - 1).astype(jnp.int32).reshape(1)
    edge_f, grad_edge = pl.pallas_call(
        edge_forward,
        out_shape=(shape((block + 2 * HALO, channels, LANES), BF16), grad_shape),
        in_specs=[smem] + [vmem] * 5,
        out_specs=(vmem, vmem),
        scratch_shapes=chain_scratch(edge_total, True),
        compiler_params=params(16),
        cost_estimate=weighs(12),
        name="edge_forward",
    )(is_last, strips, rows_in, north, south, mixing)

    rounds = []
    for axis, devices in (("lon", lon), ("lat", lat)):
        reach = 1
        while reach < devices:
            rounds.append((axis, [(i, i ^ reach) for i in range(devices)]))
            reach *= 2
    rounds = [r for r in rounds if r[0] == "lon"] + [r for r in rounds if r[0] == "lat"][::-1]

    results = {}

    def run_main_backward(share):
        results["main"], share = pl.pallas_call(
            main_backward,
            out_shape=(rows_first, grad_shape),
            in_specs=[smem] + [vmem] * 5,
            out_specs=(vmem, vmem),
            scratch_shapes=chain_scratch(-(-(rows + 2 * HALO + 8) // 8) * 8, False),
            compiler_params=params(20),
            cost_estimate=weighs(24),
            name="main_backward",
        )(is_last, rows_in, north, south, mixing, share)
        return share

    def run_edge_backward(share):
        results["edge"], share = pl.pallas_call(
            edge_backward,
            out_shape=(shape((block, channels, LANES), BF16), grad_shape),
            in_specs=[smem] + [vmem] * 5,
            out_specs=(vmem, vmem),
            scratch_shapes=chain_scratch(-(-(block + 2 * HALO + 8) // 8) * 8, False),
            compiler_params=params(12),
            cost_estimate=weighs(12),
            name="edge_backward",
        )(is_last, strips, north, south, mixing, share)
        return share

    def assemble(main, edges, share, name):
        return pl.pallas_call(
            assemble_kernel,
            out_shape=(shape(signal.shape, BF16), grad_shape),
            in_specs=[vmem] * 3,
            out_specs=(hbm, vmem),
            scratch_shapes=[
                pltpu.VMEM((spread_size(channels, rows), LANES), F32),
                pltpu.VMEM(signal.shape, BF16),
                pltpu.SemaphoreType.DMA((4,)),
            ],
            compiler_params=params(12),
            cost_estimate=weighs(8),
            name=name,
        )(main, edges, share)

    def run_assemble_forward(share):
        results["output"], share = assemble(main_f, edge_f, share, "assemble_forward")
        return share

    def run_assemble_backward(share):
        results["signal_grad"], share = assemble(results["main"], results["edge"], share, "assemble_backward")
        return share

    beside = [run_main_backward, run_assemble_forward, run_edge_backward, run_assemble_backward]
    share = grad_main + grad_edge
    theirs = jnp.zeros_like(share)
    for number in range(max(len(rounds), len(beside))):
        if number:
            share = share + theirs
        theirs = lax.ppermute(share, *rounds[number]) if number < len(rounds) else jnp.zeros_like(share)
        if number < len(beside):
            share = beside[number](share)

    norm_scale = 1.0 / math.sqrt(rows * lat * sector * lon)
    mixing_grad = pl.pallas_call(
        functools.partial(finish_kernel, norm_scale),
        out_shape=shape(mixing.shape, F32),
        in_specs=[vmem, vmem],
        out_specs=vmem,
        compiler_params=params(4),
        name="finish",
    )(share, theirs)
    return (results["output"], results["signal_grad"], mixing_grad)


def solution(mesh):
    in_specs = (P(None, "lat", "lon"), P(None, "lat", "lon"), P(None, "lat", "lon"), P("lat"), P())
    out_specs = (P(None, "lat", "lon"), P(None, "lat", "lon"), P())
    return jax.shard_map(
        on_device, mesh=mesh, in_specs=in_specs, out_specs=out_specs, check_vma=False
    )
```

```python
import functools
import math

import jax
import jax.numpy as jnp
from jax import lax
from jax.experimental import pallas as pl
from jax.experimental.pallas import tpu as pltpu
from jax.sharding import PartitionSpec as P

F32 = jnp.float32
BF16 = jnp.bfloat16
HALO = 5
LANES = 128
BLOCKS = 4
GROUP = LANES // BLOCKS
SIDE = GROUP // 2
PACKED = 80
BAND = 3 * HALO
PACK_VMEM = 63_400_000


def params(mib):
    return pltpu.CompilerParams(vmem_limit_bytes=mib * 1024 * 1024)


def lane_index(shape):
    return lax.broadcasted_iota(jnp.int32, shape, len(shape) - 1)


def turned(x, amount):
    amount = amount % LANES
    return pltpu.roll(x, amount, 1) if amount else x


def spread_size(channels, rows):
    return rows * (3 * channels + 1)


def spread(wide, channels, c, rows, x):
    wide[pl.ds(3 * c, rows, stride=3 * channels + 1), :] = x


def gather(wide, channels, r, first, count):
    return wide[pl.ds(r * (3 * channels + 1) + 3 * first, count, stride=3), :]


def widen_all(signal, cotangent, weights, wide, ready=None):
    channels, rows, _ = signal.shape
    count = 2 * channels + 8
    for which, source in enumerate((signal, cotangent)):
        for part in range(4):
            if ready is not None:
                ready(which, part)
            size = channels // 4

            def widen(i, _):
                for j in range(4):
                    c = part * size + i * 4 + j
                    spread(wide, count, which * channels + c, rows, source[c].astype(F32))
                return 0

            lax.fori_loop(0, size // 4, widen, 0)
    if ready is not None:
        ready(2, 0)
    for i in range(8):
        x = weights[i].astype(F32) if i < 3 else jnp.zeros((rows, LANES), F32)
        spread(wide, count, 2 * channels + i, rows, x)


def row_loader(channels, rows, shift, wide):
    count = 2 * channels + 8
    sub = lax.broadcasted_iota(jnp.int32, (8, LANES), 0)

    def load_row(r):
        body = gather(wide, count, r, 0, 2 * channels)
        tail = gather(wide, count, r, 2 * channels, 8)
        parity = jnp.where(shift[r] == 1, 1.0, 0.0).astype(F32)
        tail = jnp.where(sub == 3, parity, tail)
        return jnp.concatenate([body, tail, jnp.zeros((8, LANES), F32)], axis=0).astype(BF16)

    return load_row


def pack_kernel(signal_hbm, cotangent_hbm, weights_hbm, shift, west_out, east_out,
                signal, cotangent, weights, wide, arrived):
    channels, rows, _ = signal.shape
    block = rows // BLOCKS
    per_row = block // 6
    size = channels // 4
    copies = {(2, 0): pltpu.make_async_copy(weights_hbm, weights, arrived.at[8])}
    for which, (source, target) in enumerate(((signal_hbm, signal), (cotangent_hbm, cotangent))):
        for part in range(4):
            span = pl.ds(part * size, size)
            copies[which, part] = pltpu.make_async_copy(source.at[span], target.at[span], arrived.at[4 * which + part])
    for copy in copies.values():
        copy.start()
    widen_all(signal, cotangent, weights, wide, lambda *key: copies[key].wait())
    load_row = row_loader(channels, rows, shift, wide)
    lane = lane_index((PACKED, LANES))

    def each(t, _):
        west = jnp.zeros((PACKED, LANES), BF16)
        east = jnp.zeros((PACKED, LANES), BF16)
        for b in range(BLOCKS):
            for m in range(6):
                x = load_row(block * b + per_row * m + t)
                first = GROUP * b + 5 * m
                moved = turned(x, first + 5)
                east = jnp.where((lane >= first) & (lane < first + 5), moved, east)
                west = jnp.where((lane - (first + 5)) % LANES < 5, moved, west)
        west_out[t] = west
        east_out[t] = east
        return 0

    lax.fori_loop(0, per_row, each, 0)


def strip_selector():
    source = lax.broadcasted_iota(jnp.int32, (BLOCKS * LANES, LANES), 0)
    lane = lane_index((BLOCKS * LANES, LANES))
    lane_in = lane % GROUP
    wanted = jnp.where(lane_in < SIDE, lane_in - 5, lane_in - SIDE + 117)
    wanted = jnp.where((lane_in >= 5) & (lane_in < SIDE + 11), wanted + LANES * (lane // GROUP), -1)
    return jnp.where(source == wanted, 1.0, 0.0).astype(BF16)


def own_kernel(signal, cotangent, weights_hbm, shift_hbm, mixing_hbm, strips_out, rows_out, mixing_out,
               wide, weights, shift, arrived):
    channels, rows, _ = signal.shape
    block = rows // BLOCKS
    copies = [pltpu.make_async_copy(source, target, arrived.at[i]) for i, (source, target) in enumerate(
        ((weights_hbm, weights), (shift_hbm, shift), (mixing_hbm, mixing_out)))]
    for copy in copies:
        copy.start()
    widen_all(signal, cotangent, weights, wide, lambda which, _: copies[0].wait() if which == 2 else None)
    copies[1].wait()
    load_row = row_loader(channels, rows, shift, wide)
    selector = strip_selector()
    size = 6

    def each(i, _):
        strips = []
        for j in range(size):
            s = i * size + j
            tiles = [load_row(block * b + s) for b in range(BLOCKS)]
            for b in range(BLOCKS):
                rows_out[block * b + s] = tiles[b]
            strips.append(side_by_side(tiles))
        strips = jnp.dot(jnp.concatenate(strips, axis=0), selector, preferred_element_type=F32).astype(BF16)
        for j in range(size):
            strips_out[i * size + j] = strips[PACKED * j:PACKED * (j + 1)]
        return 0

    lax.fori_loop(0, block // size, each, 0)
    copies[2].wait()


def merge_kernel(strips_in, rows_in, from_west, from_east, strips_out, north_out, south_out):
    block = strips_in.shape[0]
    rows = rows_in.shape[0]
    per_row = block // 6
    lane = lane_index((PACKED, LANES))
    lane_in = lane % GROUP

    def each(t, _):
        west = from_west[t]
        east = from_east[t]
        for m in range(6):
            strip = strips_in[per_row * m + t]
            strip = jnp.where(lane_in < 5, turned(west, -5 * m), strip)
            strip = jnp.where(lane_in >= GROUP - 5, turned(east, 22 - 5 * m), strip)
            strips_out[per_row * m + t] = strip
        return 0

    lax.fori_loop(0, per_row, each, 0)
    for out, first_row, first_strip, side in (
        (north_out, 0, 0, 0), (south_out, rows - HALO, block - HALO, BLOCKS - 1)):
        for i in range(HALO):
            out[i] = rows_in[first_row + i]
        corner = turned(strips_out[first_strip], -GROUP * side)
        for g in range(1, BLOCKS):
            piece = turned(strips_out[first_strip + g], GROUP * (g - side))
            corner = jnp.where((lane >= GROUP * g) & (lane < GROUP * (g + 1)), piece, corner)
        out[HALO] = corner
        out[HALO + 1] = turned(strips_out[first_strip + HALO - 1], -GROUP * side)


def write_coefficients(total, first, w_east, w_south, w_diag, parity, keep, coef, shifted):
    count = w_east.shape[0]
    w_back = jnp.where(parity > 0.5, turned(w_diag, 1), turned(w_diag, -1))
    w_west = turned(w_east, 1)
    shifted[0:8, :] = jnp.zeros((8, LANES), F32)
    shifted[8:8 + count, :] = w_south + w_back
    degree = w_east + w_west + w_south + w_diag + shifted[7:7 + count, :]
    third = -1.0 / 3.0
    arrays = [degree * (1.0 / 3.0) - 2.0, w_east * third, w_west * third]
    for array in (w_south, w_diag, w_back):
        arrays.append(array * third if keep is None else array * keep * third)
    for i, array in enumerate(arrays + [parity]):
        coef[i * total + first:i * total + first + count, :] = array


def stencil_steps(order, channels, total, coef, buffers, kept, trips, regions):
    groups = channels // 8

    def coef_row(i, at):
        return coef[pl.ds(i * total + at, 8, stride=0), :]

    def step(position, now, older, newer):
        last = position == order - 1

        def one_row(at, level, down, before):
            coefs = [coef_row(i, at) for i in range(7)]
            c, e, w, s, d, back, parity = coefs
            here = parity > 0.5
            s_above, d_above, above = before
            new, next_level, next_down = [], [], []
            for g in range(groups):
                span = slice(8 * g, 8 * g + 8)
                v = now[at, span, :]
                v_east = pltpu.roll(v, LANES - 1, 1)
                v_west = pltpu.roll(v, 1, 1)
                value = level[g] + s_above * v + d_above * jnp.where(above, v_east, v_west)
                new.append(value * 0.5 if position == 1 else value)
                value = c * v + e * v_east + w * v_west + down[g]
                next_level.append(value if position == 1 else value - older[at, span, :])
                next_down.append(s * v + back * jnp.where(here, v_west, v_east))
            if not last:
                for g in range(groups):
                    newer[at - 1, 8 * g:8 * g + 8, :] = new[g]
            for h in range(groups // 2):
                first = channels * position + 16 * h
                pair = jnp.concatenate([new[2 * h], new[2 * h + 1]], axis=0)
                kept[at - 1, first:first + 16, :] = pair.astype(BF16)
            return tuple(next_level), tuple(next_down), (s, d, here)

        counts = [-(-(count + 2 - 2 * position) // trips) for _, count in regions]

        def several(trip, carry):
            states = []
            for (base, _), count, (level, down) in zip(regions, counts, carry):
                at = base + position + trip * count
                before = (coef_row(3, at - 1), coef_row(4, at - 1), coef_row(6, at - 1) > 0.5)
                states.append([at, level, down, before])
            for j in range(max(counts)):
                for state, count in zip(states, counts):
                    if j < count:
                        state[1:] = one_row(state[0] + j, *state[1:])
            return tuple((level, down) for _, level, down, _ in states)

        zeros = tuple(jnp.zeros((8, LANES), F32) for _ in range(groups))
        lax.fori_loop(0, trips, several, tuple((zeros, zeros) for _ in regions))

    for position in range(1, order):
        step(position, buffers[(position - 1) % 3], buffers[(position - 2) % 3], buffers[position % 3])


def write_packed(total, w_east, w_south, w_diag, parity, keep, centre, weights, wide):
    w_back = jnp.where(parity > 0.5, turned(w_diag, 1), turned(w_diag, -1))
    w_west = turned(w_east, 1)
    wide[0:8, :] = jnp.zeros((8, LANES), F32)
    wide[8:8 + total, :] = w_south + w_back
    degree = w_east + w_west + w_south + w_diag + wide[7:7 + total, :]
    centre[0:total, :] = degree * (1.0 / 3.0) - 2.0
    if keep is not None:
        w_south, w_diag, w_back = w_south * keep, w_diag * keep, w_back * keep
    arrays = (w_east, w_west, w_south, w_diag, w_back, parity)
    for i, array in enumerate(arrays):
        wide[i * total:(i + 1) * total, :] = array

    def several(trip, _):
        for j in range(8):
            row = trip * 8 + j
            for i in range(len(arrays)):
                weights[i, row] = wide[pl.ds(i * total + row, 16, stride=0), :].astype(BF16)
        return 0

    lax.fori_loop(0, total // 8, several, 0)


def packed_steps(order, channels, centre, weights, buffers, kept, trips, regions):
    halves = channels // 16

    def step(position, now, older, newer):
        first = channels * (position - 1)

        def neighbour_sums(at, count):
            sums = [[None] * halves for _ in range(count)]
            spans = [slice(first + 16 * h, first + 16 * h + 16) for h in range(halves)]
            masks = {j: weights[5, at + j] > 0.5 for j in range(-1, count)}

            def add(j, h, value):
                sums[j][h] = value if sums[j][h] is None else sums[j][h] + value

            for j in range(-1, count + 1):
                q = at + j
                for h in range(halves):
                    v = kept[q, spans[h], :]
                    v_east = pltpu.roll(v, LANES - 1, 1)
                    v_west = pltpu.roll(v, 1, 1)
                    if j >= 1:
                        diag = jnp.where(masks[j - 1], v_east, v_west)
                        add(j - 1, h, weights[2, q - 1] * v + weights[3, q - 1] * diag)
                    if j < count - 1:
                        diag = jnp.where(masks[j], v_west, v_east)
                        add(j + 1, h, weights[2, q] * v + weights[4, q] * diag)
                    if 0 <= j < count:
                        add(j, h, weights[0, q] * v_east + weights[1, q] * v_west)
            return sums

        counts = [-(-(count - 2 * position) // trips) for _, count in regions]

        def several(trip, carry):
            for (base, _), count in zip(regions, counts):
                at = base + 1 + position + trip * count
                sums = neighbour_sums(at, count)
                results = []
                for j in range(count):
                    row = []
                    for h in range(halves):
                        middle = centre[pl.ds(at + j, 16, stride=0), :]
                        span = slice(16 * h, 16 * h + 16)
                        new = middle * now[at + j, span, :] - sums[j][h].astype(F32) * (1.0 / 3.0)
                        row.append(new * 0.5 if position == 1 else new - older[at + j, span, :])
                    results.append(row)
                for j in range(count):
                    for h in range(halves):
                        if position < order - 1:
                            newer[at + j, 16 * h:16 * h + 16, :] = results[j][h]
                        to = first + channels + 16 * h
                        kept[at + j, to:to + 16, :] = results[j][h].astype(BF16)
            return carry

        lax.fori_loop(0, trips, several, 0)

    for position in range(1, order):
        step(position, buffers[(position - 1) % 3], buffers[(position - 2) % 3], buffers[position % 3])


def zero_guards(buffers, coef, total, guards):
    for first, end in guards:
        for index in range(first, end):
            for buffer in buffers:
                buffer[index] = jnp.zeros(buffer.shape[1:], F32)
        for i in range(7):
            coef[i * total + first:i * total + end, :] = jnp.zeros((end - first, LANES), F32)


CONTRACT_LANES = (((1,), (1,)), ((), ()))
CONTRACT_ROWS = (((0,), (0,)), ((), ()))


def side_by_side(tiles):
    return jnp.concatenate(tiles, axis=1)


class Chain:
    def __init__(self, first, other, mixing, guards, scratch):
        self.buffers, self.kept, self.coef, self.wide = scratch[:3], *scratch[3:6]
        self.paired = scratch[6] if other is not None else None
        self.weights = scratch[6] if other is None else None
        self.first, self.other, self.mixing = first, other, mixing
        self.order, self.channels = mixing.shape[:2]
        self.total = self.kept.shape[0]
        for begin, end in guards:
            for index in range(begin, end):
                self.kept[index] = jnp.zeros((self.order * self.channels, LANES), BF16)
        zero_guards(self.buffers, self.coef, self.total, guards)
        for begin, end in guards:
            for i in range(4):
                at = i * (self.total + 1)
                self.wide[at + begin:at + end, :] = jnp.zeros((end - begin, LANES), F32)

    def put(self, index, ref, at, tile=None):
        def part(begin, count):
            return ref[at, begin:begin + count, :] if tile is None else tile[begin:begin + count]
        self.wide[pl.ds(index, 8, stride=self.total + 1), :] = part(PACKED - 16, 16).astype(F32)[:8]
        field = part(self.first, self.channels)
        self.buffers[0][index] = field.astype(F32)
        self.kept[index, 0:self.channels, :] = field
        if self.other is not None:
            self.paired[index] = part(self.other, self.channels)

    def put_all(self, index, ref, unroll):
        count = ref.shape[0]

        def several(i, _):
            for j in range(unroll):
                self.put(index + i * unroll + j, ref, i * unroll + j)
            return 0

        lax.fori_loop(0, count // unroll, several, 0)

    def put_strips(self, strips, north, south):
        block = strips.shape[0]
        self.put_all(1 + HALO, strips, 8)
        lane = lane_index((PACKED, LANES))
        for i in range(HALO):
            at_end = i == HALO - 1
            above = turned(strips[block - HALO + i], GROUP)
            corner = turned(north[HALO + at_end], 0 if at_end else -GROUP * i)
            self.put(1 + i, None, None, jnp.where(lane < GROUP, corner, above))
            below = turned(strips[i], -GROUP)
            corner = turned(south[HALO + at_end], -GROUP - (0 if at_end else GROUP * i))
            self.put(1 + HALO + block + i, None, None, jnp.where(lane >= LANES - GROUP, corner, below))

    def run(self, trips, regions, closed=None):
        total = self.total
        starts = [i * (total + 1) for i in range(4)]
        w_east, w_south, w_diag, parity = [self.wide[at:at + total, :] for at in starts]
        keep = None
        if closed is not None:
            is_end, where = closed
            row = lax.broadcasted_iota(jnp.int32, (total, LANES), 0)
            keep = jnp.where(where(row, lane_index((total, LANES))) & is_end, 0.0, 1.0).astype(F32)
        arrays = (w_east, w_south, w_diag, parity, keep)
        if self.other is None:
            write_packed(total, *arrays, self.coef, self.weights, self.wide)
            packed_steps(self.order, self.channels, self.coef, self.weights, self.buffers, self.kept, trips, regions)
        else:
            write_coefficients(total, 0, *arrays, self.coef, self.wide)
            stencil_steps(self.order, self.channels, total, self.coef, self.buffers, self.kept, trips, regions)

    def terms(self, indices):
        return side_by_side([self.kept[i] for i in indices])

    def mixed(self, terms):
        if self.other is not None:
            matrix = self.mixing[...].reshape(self.order * self.channels, self.channels)
            value = lax.dot_general(matrix, terms, CONTRACT_ROWS, preferred_element_type=F32)
        else:
            matrix = side_by_side([self.mixing[k] for k in range(self.order)])
            value = jnp.dot(matrix, terms, preferred_element_type=F32)
        return value.astype(BF16)

    def paired_with(self, indices, valid, terms):
        left = [jnp.where(valid, self.paired[i], jnp.zeros((), BF16)) for i in indices]
        return lax.dot_general(side_by_side(left), terms, CONTRACT_LANES, preferred_element_type=F32)


def valid_lanes(channels):
    lane = lane_index((channels, LANES))
    lane_in = lane % GROUP
    in_strips = ((lane_in >= 5) & (lane_in < 10)) | ((lane_in >= SIDE + 6) & (lane_in < SIDE + 11))
    return (lane >= HALO) & (lane < LANES - HALO), in_strips


def main_forward(rows_in, mixing, out, grad, *scratch):
    rows = rows_in.shape[0]
    order, channels = mixing.shape[:2]
    chain = Chain(0, channels, mixing, ((0, 1), (rows + 1, rows + 8)), scratch)
    chain.put_all(1, rows_in, 16)
    chain.run(rows // 32, ((0, rows),))
    valid, _ = valid_lanes(channels)

    def products(start, count, total_grad):
        indices = [start + 1 + i for i in range(count)]
        terms = chain.terms(indices)
        value = chain.mixed(terms)
        for i in range(count):
            out[start + i] = value[:, LANES * i:LANES * (i + 1)]
        return total_grad + chain.paired_with(indices, valid, terms)

    inner = rows - 2 * HALO
    total_grad = jnp.zeros(grad.shape, F32)
    total_grad = lax.fori_loop(0, inner // 16, lambda i, g: products(HALO + i * 16, 16, g), total_grad)
    if inner % 16:
        total_grad = products(HALO + inner // 16 * 16, inner % 16, total_grad)
    grad[...] = total_grad


def main_backward(is_last, rows_in, north, south, mixing, summed, out, summed_out, *scratch):
    rows = rows_in.shape[0]
    channels = mixing.shape[1]
    count = rows + 2 * HALO
    chain = Chain(channels, None, mixing, ((0, 1), (count + 1, scratch[0].shape[0])), scratch)
    for i in range(HALO):
        chain.put(1 + i, north, i)
        chain.put(1 + HALO + rows + i, south, i)
    chain.put_all(1 + HALO, rows_in, 16)
    chain.run(7, ((0, count),), (is_last[0] == 1, lambda row, lane: row == HALO + rows))

    def products(i, _):
        value = chain.mixed(chain.terms([1 + HALO + i * 16 + j for j in range(16)]))
        for j in range(16):
            out[i * 16 + j] = value[:, LANES * j:LANES * (j + 1)]
        return 0

    lax.fori_loop(0, rows // 16, products, 0)
    summed_out[...] = summed[...]


def edge_sizes(rows):
    block = rows // BLOCKS
    strips = block + 2 * HALO
    top = strips + 6
    bottom = top + BAND + 5
    return block, top, bottom, -(-(bottom + BAND + 5) // 8) * 8


def edge_forward(is_last, strips_in, rows_in, north, south, mixing, out, grad, *scratch):
    rows = rows_in.shape[0]
    block, top, bottom, total = edge_sizes(rows)
    channels = mixing.shape[1]
    count = block + 2 * HALO
    chain = Chain(0, channels, mixing, ((0, 1), (1 + count, top + 1), (top + 1 + BAND, bottom + 1),
                                        (bottom + 1 + BAND, total)), scratch)
    chain.put_strips(strips_in, north, south)
    for i in range(HALO):
        chain.put(top + 1 + i, north, i)
        chain.put(bottom + 1 + 2 * HALO + i, south, i)
    for i in range(2 * HALO):
        chain.put(top + 1 + HALO + i, rows_in, i)
        chain.put(bottom + 1 + i, rows_in, rows - 2 * HALO + i)

    def closed(row, lane):
        return (row == bottom + 2 * HALO) | ((row == HALO + block) & (lane >= LANES - GROUP))

    chain.run(2, ((0, count), (top, BAND), (bottom, BAND)), (is_last[0] == 1, closed))
    main_valid, strip_valid = valid_lanes(channels)
    strip_rows = [1 + HALO + i for i in range(block)]
    band_rows = [top + 1 + HALO + i for i in range(HALO)] + [bottom + 1 + HALO + i for i in range(HALO)]
    total_grad = jnp.zeros(grad.shape, F32)
    slot = 0
    for indices, valid in ((strip_rows, strip_valid), (band_rows, main_valid)):
        terms = chain.terms(indices)
        value = chain.mixed(terms)
        for i in range(len(indices)):
            out[slot + i] = value[:, LANES * i:LANES * (i + 1)]
        slot += len(indices)
        total_grad = total_grad + chain.paired_with(indices, valid, terms)
    grad[...] = total_grad


def edge_backward(is_last, strips_in, north, south, mixing, summed, out, summed_out, *scratch):
    block = strips_in.shape[0]
    count = block + 2 * HALO
    chain = Chain(mixing.shape[1], None, mixing, ((0, 1), (1 + count, scratch[0].shape[0])), scratch)
    chain.put_strips(strips_in, north, south)
    chain.run(2, ((0, count),), (is_last[0] == 1, lambda row, lane: (row == HALO + block) & (lane >= LANES - GROUP)))
    value = chain.mixed(chain.terms([1 + HALO + i for i in range(block)]))
    for i in range(block):
        out[i] = value[:, LANES * i:LANES * (i + 1)]
    summed_out[...] = summed[...]


def assemble_kernel(main, edges, summed, out_hbm, summed_out, wide, out, sent):
    summed_out[...] = summed[...]
    rows, channels, _ = main.shape
    block = rows // BLOCKS
    lane = lane_index((channels, LANES))

    def put(r, s, b, value):
        strip = edges[s]
        west = turned(strip, -(GROUP * b + 5))
        east = turned(strip, LANES - 5 - (GROUP * b + SIDE + 6))
        value = jnp.where(lane < HALO, west, jnp.where(lane >= LANES - HALO, east, value))
        wide[pl.ds(r * (3 * channels + 1), channels, stride=3), :] = value.astype(F32)

    for b in range(BLOCKS):
        def several(i, _, b=b):
            for j in range(8):
                s = i * 8 + j
                put(block * b + s, s, b, main[block * b + s])
            return 0
        lax.fori_loop(0, block // 8, several, 0)
    if edges.shape[0] > block:
        for i in range(HALO):
            put(i, i, 0, edges[block + i])
            put(rows - HALO + i, block - HALO + i, BLOCKS - 1, edges[block + HALO + i])

    pieces = 4
    size = channels // pieces

    def narrow(i, _):
        for j in range(size):
            o = i * size + j
            out[o] = wide[pl.ds(3 * o, rows, stride=3 * channels + 1), :].astype(BF16)
        copy(i).start()
        return 0

    def copy(i):
        span = pl.ds(i * size, size)
        return pltpu.make_async_copy(out.at[span], out_hbm.at[span], sent.at[i])

    lax.fori_loop(0, pieces, narrow, 0)
    for i in range(pieces):
        copy(i).wait()


def finish_kernel(scale, mine, theirs, out):
    order, channels = out.shape[:2]
    out[...] = ((mine[...] + theirs[...]) * scale).T.reshape(order, channels, channels)


def on_device(signal, cotangent, edge_weights, circle_shift, mixing):
    channels, rows, sector = signal.shape
    order = mixing.shape[0]
    block, top, bottom, edge_total = edge_sizes(rows)
    lat, lon = lax.axis_size("lat"), lax.axis_size("lon")
    vmem = pl.BlockSpec(memory_space=pltpu.VMEM)
    smem = pl.BlockSpec(memory_space=pltpu.SMEM)
    hbm = pl.BlockSpec(memory_space=pltpu.HBM)
    shape = jax.ShapeDtypeStruct

    def packed(count):
        return shape((count, PACKED, LANES), BF16)

    def weighs(mib):
        return pl.CostEstimate(flops=0, bytes_accessed=mib * 1024 * 1024, transcendentals=0)

    all_wide = pltpu.VMEM((spread_size(2 * channels + 8, rows), LANES), F32)
    raw = (signal, cotangent, edge_weights, circle_shift)
    to_west, to_east = pl.pallas_call(
        pack_kernel,
        out_shape=(packed(block // 6), packed(block // 6)),
        in_specs=[hbm, hbm, hbm, smem],
        out_specs=(vmem, vmem),
        scratch_shapes=[
            pltpu.VMEM(signal.shape, BF16),
            pltpu.VMEM(signal.shape, BF16),
            pltpu.VMEM(edge_weights.shape, BF16),
            all_wide,
            pltpu.SemaphoreType.DMA((9,)),
        ],
        compiler_params=pltpu.CompilerParams(vmem_limit_bytes=PACK_VMEM),
        name="pack",
    )(*raw)

    eastward = [(i, (i + 1) % lon) for i in range(lon)]
    westward = [(j, i) for i, j in eastward]
    from_west = lax.ppermute(to_east, "lon", eastward)
    from_east = lax.ppermute(to_west, "lon", westward)

    own_strips, rows_in, mixing = pl.pallas_call(
        own_kernel,
        out_shape=(packed(block), packed(rows), shape(mixing.shape, BF16)),
        in_specs=[vmem, vmem, hbm, hbm, hbm],
        out_specs=(vmem, vmem, vmem),
        scratch_shapes=[
            all_wide,
            pltpu.VMEM(edge_weights.shape, BF16),
            pltpu.SMEM(circle_shift.shape, jnp.int32),
            pltpu.SemaphoreType.DMA((3,)),
        ],
        compiler_params=params(20),
        cost_estimate=weighs(8),
        name="own",
    )(*raw, mixing)

    strips, to_north, to_south = pl.pallas_call(
        merge_kernel,
        out_shape=(packed(block), packed(HALO + 2), packed(HALO + 2)),
        in_specs=[vmem] * 4,
        out_specs=(vmem,) * 3,
        compiler_params=params(8),
        name="merge",
    )(own_strips, rows_in, from_west, from_east)

    southward = [(i, i + 1) for i in range(lat - 1)]
    northward = [(j, i) for i, j in southward]
    north = lax.ppermute(to_south, "lat", southward)
    south = lax.ppermute(to_north, "lat", northward)

    rows_first = shape((rows, channels, LANES), BF16)
    grad_shape = shape((channels, order * channels), F32)

    def chain_scratch(total, with_pairs):
        scratch = [pltpu.VMEM((total, channels, LANES), F32)] * 3 + [
            pltpu.VMEM((total, order * channels, LANES), BF16),
            pltpu.VMEM((7 * total, LANES), F32),
            pltpu.VMEM((8 * (total + 1), LANES), F32),
        ]
        if with_pairs:
            return scratch + [pltpu.VMEM((total, channels, LANES), BF16)]
        return scratch + [pltpu.VMEM((6, total, 16, LANES), BF16)]

    main_f, grad_main = pl.pallas_call(
        main_forward,
        out_shape=(rows_first, grad_shape),
        in_specs=[vmem, vmem],
        out_specs=(vmem, vmem),
        scratch_shapes=chain_scratch(rows + 8, True),
        compiler_params=params(20),
        cost_estimate=weighs(24),
        name="main_forward",
    )(rows_in, mixing)

    is_last = (lax.axis_index("lat") == lat - 1).astype(jnp.int32).reshape(1)
    edge_f, grad_edge = pl.pallas_call(
        edge_forward,
        out_shape=(shape((block + 2 * HALO, channels, LANES), BF16), grad_shape),
        in_specs=[smem] + [vmem] * 5,
        out_specs=(vmem, vmem),
        scratch_shapes=chain_scratch(edge_total, True),
        compiler_params=params(16),
        cost_estimate=weighs(12),
        name="edge_forward",
    )(is_last, strips, rows_in, north, south, mixing)

    rounds = []
    for axis, devices in (("lon", lon), ("lat", lat)):
        reach = 1
        while reach < devices:
            rounds.append((axis, [(i, i ^ reach) for i in range(devices)]))
            reach *= 2
    rounds = [r for r in rounds if r[0] == "lon"] + [r for r in rounds if r[0] == "lat"][::-1]

    results = {}

    def run_main_backward(share):
        results["main"], share = pl.pallas_call(
            main_backward,
            out_shape=(rows_first, grad_shape),
            in_specs=[smem] + [vmem] * 5,
            out_specs=(vmem, vmem),
            scratch_shapes=chain_scratch(-(-(rows + 2 * HALO + 8) // 8) * 8, False),
            compiler_params=params(20),
            cost_estimate=weighs(24),
            name="main_backward",
        )(is_last, rows_in, north, south, mixing, share)
        return share

    def run_edge_backward(share):
        results["edge"], share = pl.pallas_call(
            edge_backward,
            out_shape=(shape((block, channels, LANES), BF16), grad_shape),
            in_specs=[smem] + [vmem] * 5,
            out_specs=(vmem, vmem),
            scratch_shapes=chain_scratch(-(-(block + 2 * HALO + 8) // 8) * 8, False),
            compiler_params=params(12),
            cost_estimate=weighs(12),
            name="edge_backward",
        )(is_last, strips, north, south, mixing, share)
        return share

    def assemble(main, edges, share, name):
        return pl.pallas_call(
            assemble_kernel,
            out_shape=(shape(signal.shape, BF16), grad_shape),
            in_specs=[vmem] * 3,
            out_specs=(hbm, vmem),
            scratch_shapes=[
                pltpu.VMEM((spread_size(channels, rows), LANES), F32),
                pltpu.VMEM(signal.shape, BF16),
                pltpu.SemaphoreType.DMA((4,)),
            ],
            compiler_params=params(12),
            cost_estimate=weighs(8),
            name=name,
        )(main, edges, share)

    def run_assemble_forward(share):
        results["output"], share = assemble(main_f, edge_f, share, "assemble_forward")
        return share

    def run_assemble_backward(share):
        results["signal_grad"], share = assemble(results["main"], results["edge"], share, "assemble_backward")
        return share

    beside = [run_main_backward, run_assemble_forward, run_edge_backward, run_assemble_backward]
    share = grad_main + grad_edge
    theirs = jnp.zeros_like(share)
    for number in range(max(len(rounds), len(beside))):
        if number:
            share = share + theirs
        theirs = lax.ppermute(share, *rounds[number]) if number < len(rounds) else jnp.zeros_like(share)
        if number < len(beside):
            share = beside[number](share)

    norm_scale = 1.0 / math.sqrt(rows * lat * sector * lon)
    mixing_grad = pl.pallas_call(
        functools.partial(finish_kernel, norm_scale),
        out_shape=shape(mixing.shape, F32),
        in_specs=[vmem, vmem],
        out_specs=vmem,
        compiler_params=params(4),
        name="finish",
    )(share, theirs)
    return (results["output"], results["signal_grad"], mixing_grad)


def solution(mesh):
    in_specs = (P(None, "lat", "lon"), P(None, "lat", "lon"), P(None, "lat", "lon"), P("lat"), P())
    out_specs = (P(None, "lat", "lon"), P(None, "lat", "lon"), P())
    return jax.shard_map(
        on_device, mesh=mesh, in_specs=in_specs, out_specs=out_specs, check_vma=False
    )
```

```python
import functools
import math

import jax
import jax.numpy as jnp
from jax import lax
from jax.experimental import pallas as pl
from jax.experimental.pallas import tpu as pltpu
from jax.sharding import PartitionSpec as P

F32 = jnp.float32
BF16 = jnp.bfloat16
HALO = 5
LANES = 128
BLOCKS = 4
GROUP = LANES // BLOCKS
SIDE = GROUP // 2
PACKED = 80
BAND = 3 * HALO
PACK_VMEM = 63_400_000


def params(mib):
    return pltpu.CompilerParams(vmem_limit_bytes=mib * 1024 * 1024)


def lane_index(shape):
    return lax.broadcasted_iota(jnp.int32, shape, len(shape) - 1)


def turned(x, amount):
    amount = amount % LANES
    return pltpu.roll(x, amount, 1) if amount else x


def spread_size(channels, rows):
    return rows * (3 * channels + 1)


def spread(wide, channels, c, rows, x):
    wide[pl.ds(3 * c, rows, stride=3 * channels + 1), :] = x


def gather(wide, channels, r, first, count):
    return wide[pl.ds(r * (3 * channels + 1) + 3 * first, count, stride=3), :]


def widen_all(signal, cotangent, weights, wide, ready=None):
    channels, rows, _ = signal.shape
    count = 2 * channels + 8
    for which, source in enumerate((signal, cotangent)):
        for part in range(4):
            if ready is not None:
                ready(which, part)
            for c in range(part * channels // 4, (part + 1) * channels // 4):
                spread(wide, count, which * channels + c, rows, source[c].astype(F32))
    if ready is not None:
        ready(2, 0)
    for i in range(8):
        x = weights[i].astype(F32) if i < 3 else jnp.zeros((rows, LANES), F32)
        spread(wide, count, 2 * channels + i, rows, x)


def row_loader(channels, rows, shift, wide):
    count = 2 * channels + 8
    sub = lax.broadcasted_iota(jnp.int32, (8, LANES), 0)

    def load_row(r):
        body = gather(wide, count, r, 0, 2 * channels)
        tail = gather(wide, count, r, 2 * channels, 8)
        parity = jnp.where(shift[r] == 1, 1.0, 0.0).astype(F32)
        tail = jnp.where(sub == 3, parity, tail)
        return jnp.concatenate([body, tail, jnp.zeros((8, LANES), F32)], axis=0).astype(BF16)

    return load_row


def pack_kernel(signal_hbm, cotangent_hbm, weights_hbm, shift, west_out, east_out,
                signal, cotangent, weights, wide, arrived):
    channels, rows, _ = signal.shape
    block = rows // BLOCKS
    per_row = block // 6
    size = channels // 4
    copies = {(2, 0): pltpu.make_async_copy(weights_hbm, weights, arrived.at[8])}
    for which, (source, target) in enumerate(((signal_hbm, signal), (cotangent_hbm, cotangent))):
        for part in range(4):
            span = pl.ds(part * size, size)
            copies[which, part] = pltpu.make_async_copy(source.at[span], target.at[span], arrived.at[4 * which + part])
    for copy in copies.values():
        copy.start()
    widen_all(signal, cotangent, weights, wide, lambda *key: copies[key].wait())
    load_row = row_loader(channels, rows, shift, wide)
    lane = lane_index((PACKED, LANES))

    def each(t, _):
        west = jnp.zeros((PACKED, LANES), BF16)
        east = jnp.zeros((PACKED, LANES), BF16)
        for b in range(BLOCKS):
            for m in range(6):
                x = load_row(block * b + per_row * m + t)
                first = GROUP * b + 5 * m
                moved = turned(x, first + 5)
                east = jnp.where((lane >= first) & (lane < first + 5), moved, east)
                west = jnp.where((lane - (first + 5)) % LANES < 5, moved, west)
        west_out[t] = west
        east_out[t] = east
        return 0

    lax.fori_loop(0, per_row, each, 0)


def strip_selector():
    source = lax.broadcasted_iota(jnp.int32, (BLOCKS * LANES, LANES), 0)
    lane = lane_index((BLOCKS * LANES, LANES))
    lane_in = lane % GROUP
    wanted = jnp.where(lane_in < SIDE, lane_in - 5, lane_in - SIDE + 117)
    wanted = jnp.where((lane_in >= 5) & (lane_in < SIDE + 11), wanted + LANES * (lane // GROUP), -1)
    return jnp.where(source == wanted, 1.0, 0.0).astype(BF16)


def own_kernel(signal, cotangent, weights_hbm, shift_hbm, mixing_hbm, strips_out, rows_out, mixing_out,
               wide, weights, shift, arrived):
    channels, rows, _ = signal.shape
    block = rows // BLOCKS
    copies = [pltpu.make_async_copy(source, target, arrived.at[i]) for i, (source, target) in enumerate(
        ((weights_hbm, weights), (shift_hbm, shift), (mixing_hbm, mixing_out)))]
    for copy in copies:
        copy.start()
    widen_all(signal, cotangent, weights, wide, lambda which, _: copies[0].wait() if which == 2 else None)
    copies[1].wait()
    load_row = row_loader(channels, rows, shift, wide)
    selector = strip_selector()
    size = 6

    def each(i, _):
        strips = []
        for j in range(size):
            s = i * size + j
            tiles = [load_row(block * b + s) for b in range(BLOCKS)]
            for b in range(BLOCKS):
                rows_out[block * b + s] = tiles[b]
            strips.append(side_by_side(tiles))
        strips = jnp.dot(jnp.concatenate(strips, axis=0), selector, preferred_element_type=F32).astype(BF16)
        for j in range(size):
            strips_out[i * size + j] = strips[PACKED * j:PACKED * (j + 1)]
        return 0

    lax.fori_loop(0, block // size, each, 0)
    copies[2].wait()


def merge_kernel(strips_in, rows_in, from_west, from_east, strips_out, north_out, south_out):
    block = strips_in.shape[0]
    rows = rows_in.shape[0]
    per_row = block // 6
    lane = lane_index((PACKED, LANES))
    lane_in = lane % GROUP

    def each(t, _):
        west = from_west[t]
        east = from_east[t]
        for m in range(6):
            strip = strips_in[per_row * m + t]
            strip = jnp.where(lane_in < 5, turned(west, -5 * m), strip)
            strip = jnp.where(lane_in >= GROUP - 5, turned(east, 22 - 5 * m), strip)
            strips_out[per_row * m + t] = strip
        return 0

    lax.fori_loop(0, per_row, each, 0)
    for out, first_row, first_strip, side in (
        (north_out, 0, 0, 0), (south_out, rows - HALO, block - HALO, BLOCKS - 1)):
        for i in range(HALO):
            out[i] = rows_in[first_row + i]
        corner = turned(strips_out[first_strip], -GROUP * side)
        for g in range(1, BLOCKS):
            piece = turned(strips_out[first_strip + g], GROUP * (g - side))
            corner = jnp.where((lane >= GROUP * g) & (lane < GROUP * (g + 1)), piece, corner)
        out[HALO] = corner
        out[HALO + 1] = turned(strips_out[first_strip + HALO - 1], -GROUP * side)


def write_coefficients(total, first, w_east, w_south, w_diag, parity, keep, coef, shifted):
    count = w_east.shape[0]
    w_back = jnp.where(parity > 0.5, turned(w_diag, 1), turned(w_diag, -1))
    w_west = turned(w_east, 1)
    shifted[0:8, :] = jnp.zeros((8, LANES), F32)
    shifted[8:8 + count, :] = w_south + w_back
    degree = w_east + w_west + w_south + w_diag + shifted[7:7 + count, :]
    third = -1.0 / 3.0
    arrays = [degree * (1.0 / 3.0) - 2.0, w_east * third, w_west * third]
    for array in (w_south, w_diag, w_back):
        arrays.append(array * third if keep is None else array * keep * third)
    for i, array in enumerate(arrays + [parity]):
        coef[i * total + first:i * total + first + count, :] = array


def stencil_steps(order, channels, total, coef, buffers, kept, trips, regions):
    groups = channels // 8

    def coef_row(i, at):
        return coef[pl.ds(i * total + at, 8, stride=0), :]

    def step(position, now, older, newer):
        last = position == order - 1

        def one_row(at, level, down, before):
            coefs = [coef_row(i, at) for i in range(7)]
            c, e, w, s, d, back, parity = coefs
            here = parity > 0.5
            s_above, d_above, above = before
            new, next_level, next_down = [], [], []
            for g in range(groups):
                span = slice(8 * g, 8 * g + 8)
                v = now[at, span, :]
                v_east = pltpu.roll(v, LANES - 1, 1)
                v_west = pltpu.roll(v, 1, 1)
                value = level[g] + s_above * v + d_above * jnp.where(above, v_east, v_west)
                new.append(value * 0.5 if position == 1 else value)
                value = c * v + e * v_east + w * v_west + down[g]
                next_level.append(value if position == 1 else value - older[at, span, :])
                next_down.append(s * v + back * jnp.where(here, v_west, v_east))
            if not last:
                for g in range(groups):
                    newer[at - 1, 8 * g:8 * g + 8, :] = new[g]
            for h in range(groups // 2):
                first = channels * position + 16 * h
                pair = jnp.concatenate([new[2 * h], new[2 * h + 1]], axis=0)
                kept[at - 1, first:first + 16, :] = pair.astype(BF16)
            return tuple(next_level), tuple(next_down), (s, d, here)

        counts = [-(-(count + 2 - 2 * position) // trips) for _, count in regions]

        def several(trip, carry):
            states = []
            for (base, _), count, (level, down) in zip(regions, counts, carry):
                at = base + position + trip * count
                before = (coef_row(3, at - 1), coef_row(4, at - 1), coef_row(6, at - 1) > 0.5)
                states.append([at, level, down, before])
            for j in range(max(counts)):
                for state, count in zip(states, counts):
                    if j < count:
                        state[1:] = one_row(state[0] + j, *state[1:])
            return tuple((level, down) for _, level, down, _ in states)

        zeros = tuple(jnp.zeros((8, LANES), F32) for _ in range(groups))
        lax.fori_loop(0, trips, several, tuple((zeros, zeros) for _ in regions))

    for position in range(1, order):
        step(position, buffers[(position - 1) % 3], buffers[(position - 2) % 3], buffers[position % 3])


def zero_guards(buffers, coef, total, guards):
    for first, end in guards:
        for index in range(first, end):
            for buffer in buffers:
                buffer[index] = jnp.zeros(buffer.shape[1:], F32)
        for i in range(7):
            coef[i * total + first:i * total + end, :] = jnp.zeros((end - first, LANES), F32)


CONTRACT_LANES = (((1,), (1,)), ((), ()))
CONTRACT_ROWS = (((0,), (0,)), ((), ()))


def side_by_side(tiles):
    return jnp.concatenate(tiles, axis=1)


class Chain:
    def __init__(self, first, other, mixing, guards, scratch):
        self.buffers, self.kept, self.coef, self.wide = scratch[:3], *scratch[3:6]
        self.paired = scratch[6] if other is not None else None
        self.first, self.other, self.mixing = first, other, mixing
        self.order, self.channels = mixing.shape[:2]
        self.total = self.kept.shape[0]
        for begin, end in guards:
            for index in range(begin, end):
                self.kept[index] = jnp.zeros((self.order * self.channels, LANES), BF16)
        zero_guards(self.buffers, self.coef, self.total, guards)
        for begin, end in guards:
            for i in range(4):
                at = i * (self.total + 1)
                self.wide[at + begin:at + end, :] = jnp.zeros((end - begin, LANES), F32)

    def put(self, index, ref, at, tile=None):
        def part(begin, count):
            return ref[at, begin:begin + count, :] if tile is None else tile[begin:begin + count]
        self.wide[pl.ds(index, 8, stride=self.total + 1), :] = part(PACKED - 16, 16).astype(F32)[:8]
        field = part(self.first, self.channels)
        self.buffers[0][index] = field.astype(F32)
        self.kept[index, 0:self.channels, :] = field
        if self.other is not None:
            self.paired[index] = part(self.other, self.channels)

    def put_all(self, index, ref, unroll):
        count = ref.shape[0]

        def several(i, _):
            for j in range(unroll):
                self.put(index + i * unroll + j, ref, i * unroll + j)
            return 0

        lax.fori_loop(0, count // unroll, several, 0)

    def put_strips(self, strips, north, south):
        block = strips.shape[0]
        self.put_all(1 + HALO, strips, block)
        lane = lane_index((PACKED, LANES))
        for i in range(HALO):
            at_end = i == HALO - 1
            above = turned(strips[block - HALO + i], GROUP)
            corner = turned(north[HALO + at_end], 0 if at_end else -GROUP * i)
            self.put(1 + i, None, None, jnp.where(lane < GROUP, corner, above))
            below = turned(strips[i], -GROUP)
            corner = turned(south[HALO + at_end], -GROUP - (0 if at_end else GROUP * i))
            self.put(1 + HALO + block + i, None, None, jnp.where(lane >= LANES - GROUP, corner, below))

    def run(self, trips, regions, closed=None):
        total = self.total
        starts = [i * (total + 1) for i in range(4)]
        w_east, w_south, w_diag, parity = [self.wide[at:at + total, :] for at in starts]
        keep = None
        if closed is not None:
            is_end, where = closed
            row = lax.broadcasted_iota(jnp.int32, (total, LANES), 0)
            keep = jnp.where(where(row, lane_index((total, LANES))) & is_end, 0.0, 1.0).astype(F32)
        write_coefficients(total, 0, w_east, w_south, w_diag, parity, keep, self.coef, self.wide)
        stencil_steps(self.order, self.channels, total, self.coef, self.buffers, self.kept, trips, regions)

    def terms(self, indices):
        return side_by_side([self.kept[i] for i in indices])

    def mixed(self, terms):
        if self.other is not None:
            matrix = self.mixing[...].reshape(self.order * self.channels, self.channels)
            value = lax.dot_general(matrix, terms, CONTRACT_ROWS, preferred_element_type=F32)
        else:
            matrix = side_by_side([self.mixing[k] for k in range(self.order)])
            value = jnp.dot(matrix, terms, preferred_element_type=F32)
        return value.astype(BF16)

    def paired_with(self, indices, valid, terms):
        left = [jnp.where(valid, self.paired[i], jnp.zeros((), BF16)) for i in indices]
        return lax.dot_general(side_by_side(left), terms, CONTRACT_LANES, preferred_element_type=F32)


def valid_lanes(channels):
    lane = lane_index((channels, LANES))
    lane_in = lane % GROUP
    in_strips = ((lane_in >= 5) & (lane_in < 10)) | ((lane_in >= SIDE + 6) & (lane_in < SIDE + 11))
    return (lane >= HALO) & (lane < LANES - HALO), in_strips


def main_forward(rows_in, mixing, out, grad, *scratch):
    rows = rows_in.shape[0]
    order, channels = mixing.shape[:2]
    chain = Chain(0, channels, mixing, ((0, 1), (rows + 1, rows + 8)), scratch)
    chain.put_all(1, rows_in, rows // 2)
    chain.run(2, ((0, rows),))
    valid, _ = valid_lanes(channels)

    def products(start, count, total_grad):
        indices = [start + 1 + i for i in range(count)]
        terms = chain.terms(indices)
        value = chain.mixed(terms)
        for i in range(count):
            out[start + i] = value[:, LANES * i:LANES * (i + 1)]
        return total_grad + chain.paired_with(indices, valid, terms)

    inner = rows - 2 * HALO
    total_grad = jnp.zeros(grad.shape, F32)
    half = inner // 2
    grad[...] = lax.fori_loop(0, 2, lambda i, g: products(HALO + i * half, half, g), total_grad)


def main_backward(is_last, rows_in, north, south, mixing, summed, out, summed_out, *scratch):
    rows = rows_in.shape[0]
    channels = mixing.shape[1]
    count = rows + 2 * HALO
    chain = Chain(channels, None, mixing, ((0, 1), (count + 1, scratch[0].shape[0])), scratch)
    for i in range(HALO):
        chain.put(1 + i, north, i)
        chain.put(1 + HALO + rows + i, south, i)
    chain.put_all(1 + HALO, rows_in, rows // 2)
    chain.run(2, ((0, count),), (is_last[0] == 1, lambda row, lane: row == HALO + rows))

    half = rows // 2

    def products(i, _):
        value = chain.mixed(chain.terms([1 + HALO + i * half + j for j in range(half)]))
        for j in range(half):
            out[i * half + j] = value[:, LANES * j:LANES * (j + 1)]
        return 0

    lax.fori_loop(0, 2, products, 0)
    summed_out[...] = summed[...]


def edge_sizes(rows):
    block = rows // BLOCKS
    strips = block + 2 * HALO
    top = strips + 6
    bottom = top + BAND + 5
    return block, top, bottom, -(-(bottom + BAND + 5) // 8) * 8


def edge_forward(is_last, strips_in, rows_in, north, south, mixing, out, grad, *scratch):
    rows = rows_in.shape[0]
    block, top, bottom, total = edge_sizes(rows)
    channels = mixing.shape[1]
    count = block + 2 * HALO
    chain = Chain(0, channels, mixing, ((0, 1), (1 + count, top + 1), (top + 1 + BAND, bottom + 1),
                                        (bottom + 1 + BAND, total)), scratch)
    chain.put_strips(strips_in, north, south)
    for i in range(HALO):
        chain.put(top + 1 + i, north, i)
        chain.put(bottom + 1 + 2 * HALO + i, south, i)
    for i in range(2 * HALO):
        chain.put(top + 1 + HALO + i, rows_in, i)
        chain.put(bottom + 1 + i, rows_in, rows - 2 * HALO + i)

    def closed(row, lane):
        return (row == bottom + 2 * HALO) | ((row == HALO + block) & (lane >= LANES - GROUP))

    chain.run(1, ((0, count), (top, BAND), (bottom, BAND)), (is_last[0] == 1, closed))
    main_valid, strip_valid = valid_lanes(channels)
    strip_rows = [1 + HALO + i for i in range(block)]
    band_rows = [top + 1 + HALO + i for i in range(HALO)] + [bottom + 1 + HALO + i for i in range(HALO)]
    total_grad = jnp.zeros(grad.shape, F32)
    slot = 0
    for indices, valid in ((strip_rows, strip_valid), (band_rows, main_valid)):
        terms = chain.terms(indices)
        value = chain.mixed(terms)
        for i in range(len(indices)):
            out[slot + i] = value[:, LANES * i:LANES * (i + 1)]
        slot += len(indices)
        total_grad = total_grad + chain.paired_with(indices, valid, terms)
    grad[...] = total_grad


def edge_backward(is_last, strips_in, north, south, mixing, summed, out, summed_out, *scratch):
    block = strips_in.shape[0]
    count = block + 2 * HALO
    chain = Chain(mixing.shape[1], None, mixing, ((0, 1), (1 + count, scratch[0].shape[0])), scratch)
    chain.put_strips(strips_in, north, south)
    chain.run(1, ((0, count),), (is_last[0] == 1, lambda row, lane: (row == HALO + block) & (lane >= LANES - GROUP)))
    value = chain.mixed(chain.terms([1 + HALO + i for i in range(block)]))
    for i in range(block):
        out[i] = value[:, LANES * i:LANES * (i + 1)]
    summed_out[...] = summed[...]


def assemble_kernel(main, edges, summed, out_hbm, summed_out, wide, out, sent):
    summed_out[...] = summed[...]
    rows, channels, _ = main.shape
    block = rows // BLOCKS
    lane = lane_index((channels, LANES))

    def put(r, s, b, value):
        strip = edges[s]
        west = turned(strip, -(GROUP * b + 5))
        east = turned(strip, LANES - 5 - (GROUP * b + SIDE + 6))
        value = jnp.where(lane < HALO, west, jnp.where(lane >= LANES - HALO, east, value))
        wide[pl.ds(r * (3 * channels + 1), channels, stride=3), :] = value.astype(F32)

    for b in range(BLOCKS):
        for s in range(block):
            put(block * b + s, s, b, main[block * b + s])
    if edges.shape[0] > block:
        for i in range(HALO):
            put(i, i, 0, edges[block + i])
            put(rows - HALO + i, block - HALO + i, BLOCKS - 1, edges[block + HALO + i])

    pieces = 2
    size = channels // pieces

    def narrow(i, _):
        for j in range(size):
            o = i * size + j
            out[o] = wide[pl.ds(3 * o, rows, stride=3 * channels + 1), :].astype(BF16)
        copy(i).start()
        return 0

    def copy(i):
        span = pl.ds(i * size, size)
        return pltpu.make_async_copy(out.at[span], out_hbm.at[span], sent.at[i])

    lax.fori_loop(0, pieces, narrow, 0)
    for i in range(pieces):
        copy(i).wait()


def finish_kernel(scale, mine, theirs, out):
    order, channels = out.shape[:2]
    out[...] = ((mine[...] + theirs[...]) * scale).T.reshape(order, channels, channels)


def on_device(signal, cotangent, edge_weights, circle_shift, mixing):
    channels, rows, sector = signal.shape
    order = mixing.shape[0]
    block, top, bottom, edge_total = edge_sizes(rows)
    lat, lon = lax.axis_size("lat"), lax.axis_size("lon")
    vmem = pl.BlockSpec(memory_space=pltpu.VMEM)
    smem = pl.BlockSpec(memory_space=pltpu.SMEM)
    hbm = pl.BlockSpec(memory_space=pltpu.HBM)
    shape = jax.ShapeDtypeStruct

    def packed(count):
        return shape((count, PACKED, LANES), BF16)

    def weighs(mib):
        return pl.CostEstimate(flops=0, bytes_accessed=mib * 1024 * 1024, transcendentals=0)

    all_wide = pltpu.VMEM((spread_size(2 * channels + 8, rows), LANES), F32)
    raw = (signal, cotangent, edge_weights, circle_shift)
    to_west, to_east = pl.pallas_call(
        pack_kernel,
        out_shape=(packed(block // 6), packed(block // 6)),
        in_specs=[hbm, hbm, hbm, smem],
        out_specs=(vmem, vmem),
        scratch_shapes=[
            pltpu.VMEM(signal.shape, BF16),
            pltpu.VMEM(signal.shape, BF16),
            pltpu.VMEM(edge_weights.shape, BF16),
            all_wide,
            pltpu.SemaphoreType.DMA((9,)),
        ],
        compiler_params=pltpu.CompilerParams(vmem_limit_bytes=PACK_VMEM),
        name="pack",
    )(*raw)

    eastward = [(i, (i + 1) % lon) for i in range(lon)]
    westward = [(j, i) for i, j in eastward]
    from_west = lax.ppermute(to_east, "lon", eastward)
    from_east = lax.ppermute(to_west, "lon", westward)

    own_strips, rows_in, mixing = pl.pallas_call(
        own_kernel,
        out_shape=(packed(block), packed(rows), shape(mixing.shape, BF16)),
        in_specs=[vmem, vmem, hbm, hbm, hbm],
        out_specs=(vmem, vmem, vmem),
        scratch_shapes=[
            all_wide,
            pltpu.VMEM(edge_weights.shape, BF16),
            pltpu.SMEM(circle_shift.shape, jnp.int32),
            pltpu.SemaphoreType.DMA((3,)),
        ],
        compiler_params=params(20),
        cost_estimate=weighs(8),
        name="own",
    )(*raw, mixing)

    strips, to_north, to_south = pl.pallas_call(
        merge_kernel,
        out_shape=(packed(block), packed(HALO + 2), packed(HALO + 2)),
        in_specs=[vmem] * 4,
        out_specs=(vmem,) * 3,
        compiler_params=params(8),
        name="merge",
    )(own_strips, rows_in, from_west, from_east)

    southward = [(i, i + 1) for i in range(lat - 1)]
    northward = [(j, i) for i, j in southward]
    north = lax.ppermute(to_south, "lat", southward)
    south = lax.ppermute(to_north, "lat", northward)

    rows_first = shape((rows, channels, LANES), BF16)
    grad_shape = shape((channels, order * channels), F32)

    def chain_scratch(total, with_pairs):
        scratch = [pltpu.VMEM((total, channels, LANES), F32)] * 3 + [
            pltpu.VMEM((total, order * channels, LANES), BF16),
            pltpu.VMEM((7 * total, LANES), F32),
            pltpu.VMEM((8 * (total + 1), LANES), F32),
        ]
        return scratch + [pltpu.VMEM((total, channels, LANES), BF16)] * with_pairs

    main_f, grad_main = pl.pallas_call(
        main_forward,
        out_shape=(rows_first, grad_shape),
        in_specs=[vmem, vmem],
        out_specs=(vmem, vmem),
        scratch_shapes=chain_scratch(rows + 8, True),
        compiler_params=params(20),
        cost_estimate=weighs(24),
        name="main_forward",
    )(rows_in, mixing)

    is_last = (lax.axis_index("lat") == lat - 1).astype(jnp.int32).reshape(1)
    edge_f, grad_edge = pl.pallas_call(
        edge_forward,
        out_shape=(shape((block + 2 * HALO, channels, LANES), BF16), grad_shape),
        in_specs=[smem] + [vmem] * 5,
        out_specs=(vmem, vmem),
        scratch_shapes=chain_scratch(edge_total, True),
        compiler_params=params(16),
        cost_estimate=weighs(12),
        name="edge_forward",
    )(is_last, strips, rows_in, north, south, mixing)

    rounds = []
    for axis, devices in (("lon", lon), ("lat", lat)):
        reach = 1
        while reach < devices:
            rounds.append((axis, [(i, i ^ reach) for i in range(devices)]))
            reach *= 2
    rounds = [r for r in rounds if r[0] == "lon"] + [r for r in rounds if r[0] == "lat"][::-1]

    results = {}

    def run_main_backward(share):
        results["main"], share = pl.pallas_call(
            main_backward,
            out_shape=(rows_first, grad_shape),
            in_specs=[smem] + [vmem] * 5,
            out_specs=(vmem, vmem),
            scratch_shapes=chain_scratch(-(-(rows + 2 * HALO + 8) // 8) * 8, False),
            compiler_params=params(20),
            cost_estimate=weighs(24),
            name="main_backward",
        )(is_last, rows_in, north, south, mixing, share)
        return share

    def run_edge_backward(share):
        results["edge"], share = pl.pallas_call(
            edge_backward,
            out_shape=(shape((block, channels, LANES), BF16), grad_shape),
            in_specs=[smem] + [vmem] * 5,
            out_specs=(vmem, vmem),
            scratch_shapes=chain_scratch(-(-(block + 2 * HALO + 8) // 8) * 8, False),
            compiler_params=params(12),
            cost_estimate=weighs(12),
            name="edge_backward",
        )(is_last, strips, north, south, mixing, share)
        return share

    def assemble(main, edges, share, name):
        return pl.pallas_call(
            assemble_kernel,
            out_shape=(shape(signal.shape, BF16), grad_shape),
            in_specs=[vmem] * 3,
            out_specs=(hbm, vmem),
            scratch_shapes=[
                pltpu.VMEM((spread_size(channels, rows), LANES), F32),
                pltpu.VMEM(signal.shape, BF16),
                pltpu.SemaphoreType.DMA((2,)),
            ],
            compiler_params=params(12),
            cost_estimate=weighs(8),
            name=name,
        )(main, edges, share)

    def run_assemble_forward(share):
        results["output"], share = assemble(main_f, edge_f, share, "assemble_forward")
        return share

    def run_assemble_backward(share):
        results["signal_grad"], share = assemble(results["main"], results["edge"], share, "assemble_backward")
        return share

    beside = [run_main_backward, run_assemble_forward, run_edge_backward, run_assemble_backward]
    share = grad_main + grad_edge
    theirs = jnp.zeros_like(share)
    for number in range(max(len(rounds), len(beside))):
        if number:
            share = share + theirs
        theirs = lax.ppermute(share, *rounds[number]) if number < len(rounds) else jnp.zeros_like(share)
        if number < len(beside):
            share = beside[number](share)

    norm_scale = 1.0 / math.sqrt(rows * lat * sector * lon)
    mixing_grad = pl.pallas_call(
        functools.partial(finish_kernel, norm_scale),
        out_shape=shape(mixing.shape, F32),
        in_specs=[vmem, vmem],
        out_specs=vmem,
        compiler_params=params(4),
        name="finish",
    )(share, theirs)
    return (results["output"], results["signal_grad"], mixing_grad)


def solution(mesh):
    in_specs = (P(None, "lat", "lon"), P(None, "lat", "lon"), P(None, "lat", "lon"), P("lat"), P())
    out_specs = (P(None, "lat", "lon"), P(None, "lat", "lon"), P())
    return jax.shard_map(
        on_device, mesh=mesh, in_specs=in_specs, out_specs=out_specs, check_vma=False
    )
```

```python
import functools
import math

import jax
import jax.numpy as jnp
from jax import lax
from jax.experimental import pallas as pl
from jax.experimental.pallas import tpu as pltpu
from jax.sharding import PartitionSpec as P

F32 = jnp.float32
BF16 = jnp.bfloat16
HALO = 5
LANES = 128
BLOCKS = 4
GROUP = LANES // BLOCKS
SIDE = GROUP // 2
PACKED = 80
BAND = 3 * HALO
PACK_VMEM = 63_400_000


def params(mib):
    return pltpu.CompilerParams(vmem_limit_bytes=mib * 1024 * 1024)


def lane_index(shape):
    return lax.broadcasted_iota(jnp.int32, shape, len(shape) - 1)


def turned(x, amount):
    amount = amount % LANES
    return pltpu.roll(x, amount, 1) if amount else x


def spread_size(channels, rows):
    return rows * (3 * channels + 1)


def spread(wide, channels, c, rows, x):
    wide[pl.ds(3 * c, rows, stride=3 * channels + 1), :] = x


def gather(wide, channels, r, first, count):
    return wide[pl.ds(r * (3 * channels + 1) + 3 * first, count, stride=3), :]


def widen_all(signal, cotangent, weights, wide, ready=None):
    channels, rows, _ = signal.shape
    count = 2 * channels + 8
    for which, source in enumerate((signal, cotangent)):
        for part in range(4):
            if ready is not None:
                ready(which, part)
            for c in range(part * channels // 4, (part + 1) * channels // 4):
                spread(wide, count, which * channels + c, rows, source[c].astype(F32))
    if ready is not None:
        ready(2, 0)
    for i in range(8):
        x = weights[i].astype(F32) if i < 3 else jnp.zeros((rows, LANES), F32)
        spread(wide, count, 2 * channels + i, rows, x)


def row_loader(channels, rows, shift, wide):
    count = 2 * channels + 8
    sub = lax.broadcasted_iota(jnp.int32, (8, LANES), 0)

    def load_row(r):
        body = gather(wide, count, r, 0, 2 * channels)
        tail = gather(wide, count, r, 2 * channels, 8)
        parity = jnp.where(shift[r] == 1, 1.0, 0.0).astype(F32)
        tail = jnp.where(sub == 3, parity, tail)
        return jnp.concatenate([body, tail, jnp.zeros((8, LANES), F32)], axis=0).astype(BF16)

    return load_row


def strip_selector():
    source = lax.broadcasted_iota(jnp.int32, (BLOCKS * LANES, LANES), 0)
    lane = lane_index((BLOCKS * LANES, LANES))
    lane_in = lane % GROUP
    wanted = jnp.where(lane_in < SIDE, lane_in - 5, lane_in - SIDE + 117)
    wanted = jnp.where((lane_in >= 5) & (lane_in < SIDE + 11), wanted + LANES * (lane // GROUP), -1)
    return jnp.where(source == wanted, 1.0, 0.0).astype(BF16)


EXTRA = 4


def head_kernel(signal_hbm, cotangent_hbm, weights_hbm, shift_hbm, mixing_hbm, west_hbm, east_hbm, strips_hbm, rows_hbm,
                signal, cotangent, weights, shift, mixing, wide, west_out, east_out, strips_out, rows_out, arrived, sent):
    channels, rows, _ = signal.shape
    block = rows // BLOCKS
    per_row = block // 6
    copies = {}
    number = 0
    for which, (source, target) in enumerate(((signal_hbm, signal), (cotangent_hbm, cotangent))):
        for part in range(4):
            span = pl.ds(part * channels // 4, channels // 4)
            copies[which, part] = pltpu.make_async_copy(source.at[span], target.at[span], arrived.at[number])
            number += 1
    for which, (source, target) in enumerate(((weights_hbm, weights), (shift_hbm, shift), (mixing_hbm, mixing))):
        copies[2 + which, 0] = pltpu.make_async_copy(source, target, arrived.at[number])
        number += 1
    for copy in copies.values():
        copy.start()
    widen_all(signal, cotangent, weights, wide, lambda *key: copies[key].wait())
    copies[3, 0].wait()
    copies[4, 0].wait()
    order = mixing.shape[0]
    rest = jnp.zeros((channels, 2 * LANES - order * channels), BF16)
    for i in range(2):
        tiles = [mixing[k] if i else mixing[k].astype(F32).T.astype(BF16) for k in range(order)]
        matrix = side_by_side(tiles + [rest])
        rows_out[rows // per_row, i] = jnp.concatenate(
            [matrix[:, :LANES], matrix[:, LANES:], jnp.zeros((PACKED - 2 * channels, LANES), BF16)], axis=0)
    for i in range(2, EXTRA):
        rows_out[rows // per_row, i] = jnp.zeros((PACKED, LANES), BF16)
    load_row = row_loader(channels, rows, shift, wide)
    selector = strip_selector()
    lane = lane_index((PACKED, LANES))

    def sends(t):
        return [pltpu.make_async_copy(source, target, sent.at[t, i]) for i, (source, target) in enumerate((
            (west_out.at[t], west_hbm.at[t]), (east_out.at[t], east_hbm.at[t]),
            (strips_out.at[:, t], strips_hbm.at[:, t]), (rows_out.at[:, t], rows_hbm.at[:, t])))]

    def each(t, _):
        groups = []
        for m in range(6):
            tiles = [load_row(block * b + per_row * m + t) for b in range(BLOCKS)]
            for b in range(BLOCKS):
                rows_out[b * 6 + m, t] = tiles[b]
            groups.append(side_by_side(tiles))
        strips = jnp.dot(jnp.concatenate(groups, axis=0), selector, preferred_element_type=F32).astype(BF16)
        west = jnp.zeros((PACKED, LANES), BF16)
        east = jnp.zeros((PACKED, LANES), BF16)
        for m in range(6):
            strip = strips[PACKED * m:PACKED * (m + 1)]
            strips_out[m, t] = strip
            west = jnp.where((lane - 5 * m - 5) % GROUP < 5, turned(strip, 5 * m), west)
            east = jnp.where((lane - 5 * m) % GROUP < 5, turned(strip, 5 * m - SIDE - 6), east)
        west_out[t] = west
        east_out[t] = east
        for copy in sends(t):
            copy.start()
        return 0

    lax.fori_loop(0, per_row, each, 0)
    for t in range(per_row):
        for copy in sends(t):
            copy.wait()


def merge_kernel(strips_in, rows_in, from_west, from_east, _, strips_out, north_out, south_out):
    block = strips_in.shape[0]
    rows = rows_in.shape[0] - EXTRA
    per_row = block // 6
    lane = lane_index((PACKED, LANES))
    lane_in = lane % GROUP

    def each(t, _):
        west = from_west[t]
        east = from_east[t]
        for m in range(6):
            strip = strips_in[per_row * m + t]
            strip = jnp.where(lane_in < 5, turned(west, -5 * m), strip)
            strip = jnp.where(lane_in >= GROUP - 5, turned(east, 22 - 5 * m), strip)
            strips_out[per_row * m + t] = strip
        return 0

    lax.fori_loop(0, per_row, each, 0)
    for out, first_row, first_strip, side in (
        (north_out, 0, 0, 0), (south_out, rows - HALO, block - HALO, BLOCKS - 1)):
        for i in range(HALO):
            out[i] = rows_in[first_row + i]
        corner = turned(strips_out[first_strip], -GROUP * side)
        for g in range(1, BLOCKS):
            piece = turned(strips_out[first_strip + g], GROUP * (g - side))
            corner = jnp.where((lane >= GROUP * g) & (lane < GROUP * (g + 1)), piece, corner)
        out[HALO] = corner
        out[HALO + 1] = turned(strips_out[first_strip + HALO - 1], -GROUP * side)


def write_coefficients(total, first, w_east, w_south, w_diag, parity, keep, coef, shifted):
    count = w_east.shape[0]
    w_back = jnp.where(parity > 0.5, turned(w_diag, 1), turned(w_diag, -1))
    w_west = turned(w_east, 1)
    shifted[0:8, :] = jnp.zeros((8, LANES), F32)
    shifted[8:8 + count, :] = w_south + w_back
    degree = w_east + w_west + w_south + w_diag + shifted[7:7 + count, :]
    third = -1.0 / 3.0
    arrays = [degree * (1.0 / 3.0) - 2.0, w_east * third, w_west * third]
    for array in (w_south, w_diag, w_back):
        arrays.append(array * third if keep is None else array * keep * third)
    for i, array in enumerate(arrays + [parity]):
        coef[i * total + first:i * total + first + count, :] = array


def stencil_steps(order, channels, total, coef, buffers, kept, trips, regions):
    groups = channels // 8

    def coef_row(i, at):
        return coef[pl.ds(i * total + at, 8, stride=0), :]

    def step(position, now, older, newer):
        last = position == order - 1

        def one_row(at, level, down, before):
            coefs = [coef_row(i, at) for i in range(7)]
            c, e, w, s, d, back, parity = coefs
            here = parity > 0.5
            s_above, d_above, above = before
            new, next_level, next_down = [], [], []
            for g in range(groups):
                span = slice(8 * g, 8 * g + 8)
                v = now[at, span, :]
                v_east = pltpu.roll(v, LANES - 1, 1)
                v_west = pltpu.roll(v, 1, 1)
                value = level[g] + s_above * v + d_above * jnp.where(above, v_east, v_west)
                new.append(value * 0.5 if position == 1 else value)
                value = c * v + e * v_east + w * v_west + down[g]
                next_level.append(value if position == 1 else value - older[at, span, :])
                next_down.append(s * v + back * jnp.where(here, v_west, v_east))
            if not last:
                for g in range(groups):
                    newer[at - 1, 8 * g:8 * g + 8, :] = new[g]
            for h in range(groups // 2):
                first = channels * position + 16 * h
                pair = jnp.concatenate([new[2 * h], new[2 * h + 1]], axis=0)
                kept[at - 1, first:first + 16, :] = pair.astype(BF16)
            return tuple(next_level), tuple(next_down), (s, d, here)

        counts = [-(-(count + 2 - 2 * position) // trips) for _, count in regions]

        def several(trip, carry):
            states = []
            for (base, _), count, (level, down) in zip(regions, counts, carry):
                at = base + position + trip * count
                before = (coef_row(3, at - 1), coef_row(4, at - 1), coef_row(6, at - 1) > 0.5)
                states.append([at, level, down, before])
            for j in range(max(counts)):
                for state, count in zip(states, counts):
                    if j < count:
                        state[1:] = one_row(state[0] + j, *state[1:])
            return tuple((level, down) for _, level, down, _ in states)

        zeros = tuple(jnp.zeros((8, LANES), F32) for _ in range(groups))
        lax.fori_loop(0, trips, several, tuple((zeros, zeros) for _ in regions))

    for position in range(1, order):
        step(position, buffers[(position - 1) % 3], buffers[(position - 2) % 3], buffers[position % 3])


def zero_guards(buffers, coef, total, guards):
    for first, end in guards:
        for index in range(first, end):
            for buffer in buffers:
                buffer[index] = jnp.zeros(buffer.shape[1:], F32)
        for i in range(7):
            coef[i * total + first:i * total + end, :] = jnp.zeros((end - first, LANES), F32)


CONTRACT_LANES = (((1,), (1,)), ((), ()))
CONTRACT_ROWS = (((0,), (0,)), ((), ()))


def side_by_side(tiles):
    return jnp.concatenate(tiles, axis=1)


class Chain:
    def __init__(self, first, other, order, rows_in, guards, scratch):
        self.buffers, self.kept, self.coef, self.wide = scratch[:3], *scratch[3:6]
        self.paired = scratch[6] if other is not None else None
        self.first, self.other, self.rows_in, self.order = first, other, rows_in, order
        self.channels = self.buffers[0].shape[1]
        self.total = self.kept.shape[0]
        for begin, end in guards:
            for index in range(begin, end):
                self.kept[index] = jnp.zeros((self.order * self.channels, LANES), BF16)
        zero_guards(self.buffers, self.coef, self.total, guards)
        for begin, end in guards:
            for i in range(4):
                at = i * (self.total + 1)
                self.wide[at + begin:at + end, :] = jnp.zeros((end - begin, LANES), F32)

    def put(self, index, ref, at, tile=None):
        def part(begin, count):
            return ref[at, begin:begin + count, :] if tile is None else tile[begin:begin + count]
        self.wide[pl.ds(index, 8, stride=self.total + 1), :] = part(PACKED - 16, 16).astype(F32)[:8]
        field = part(self.first, self.channels)
        self.buffers[0][index] = field.astype(F32)
        self.kept[index, 0:self.channels, :] = field
        if self.other is not None:
            self.paired[index] = part(self.other, self.channels)

    def put_some(self, index, ref, first, count):
        for i in range(count):
            self.put(index + i, ref, first + i)

    def put_strips(self, strips, north, south):
        block = strips.shape[0]
        self.put_some(1 + HALO, strips, 0, block)
        lane = lane_index((PACKED, LANES))
        for i in range(HALO):
            at_end = i == HALO - 1
            above = turned(strips[block - HALO + i], GROUP)
            corner = turned(north[HALO + at_end], 0 if at_end else -GROUP * i)
            self.put(1 + i, None, None, jnp.where(lane < GROUP, corner, above))
            below = turned(strips[i], -GROUP)
            corner = turned(south[HALO + at_end], -GROUP - (0 if at_end else GROUP * i))
            self.put(1 + HALO + block + i, None, None, jnp.where(lane >= LANES - GROUP, corner, below))

    def run(self, trips, regions, closed=None):
        total = self.total
        starts = [i * (total + 1) for i in range(4)]
        w_east, w_south, w_diag, parity = [self.wide[at:at + total, :] for at in starts]
        keep = None
        if closed is not None:
            is_end, where = closed
            row = lax.broadcasted_iota(jnp.int32, (total, LANES), 0)
            keep = jnp.where(where(row, lane_index((total, LANES))) & is_end, 0.0, 1.0).astype(F32)
        write_coefficients(total, 0, w_east, w_south, w_diag, parity, keep, self.coef, self.wide)
        stencil_steps(self.order, self.channels, total, self.coef, self.buffers, self.kept, trips, regions)

    def terms(self, indices):
        return side_by_side([self.kept[i] for i in indices])

    def mixed(self, terms):
        place = self.rows_in.shape[0] - EXTRA + (self.other is None)
        matrix = side_by_side([self.rows_in[place, i:i + self.channels, :] for i in (0, self.channels)])
        matrix = matrix[:, :self.order * self.channels]
        value = jnp.dot(matrix, terms, preferred_element_type=F32)
        return value.astype(BF16)

    def paired_with(self, indices, valid, terms):
        left = [jnp.where(valid, self.paired[i], jnp.zeros((), BF16)) for i in indices]
        return lax.dot_general(side_by_side(left), terms, CONTRACT_LANES, preferred_element_type=F32)


def valid_lanes(channels):
    lane = lane_index((channels, LANES))
    lane_in = lane % GROUP
    in_strips = ((lane_in >= 5) & (lane_in < 10)) | ((lane_in >= SIDE + 6) & (lane_in < SIDE + 11))
    return (lane >= HALO) & (lane < LANES - HALO), in_strips


def main_forward(upper, order, rows_in, _, out, grad, *scratch):
    rows = rows_in.shape[0] - EXTRA
    channels = out.shape[1]
    half = rows // 2
    count = half + HALO
    chain = Chain(0, channels, order, rows_in, ((0, 1), (count + 1, count + 4)), scratch)
    chain.put_some(1, rows_in, 0 if upper else half - HALO, count)
    chain.run(1, ((0, count),))
    valid, _ = valid_lanes(channels)
    indices = [1 + HALO + i for i in range(half - HALO)]
    terms = chain.terms(indices)
    value = chain.mixed(terms)
    for i in range(len(indices)):
        out[i + HALO * upper] = value[:, LANES * i:LANES * (i + 1)]
    grad[...] = chain.paired_with(indices, valid, terms)


def main_backward(upper, order, is_last, rows_in, beyond, summed, out, summed_out, *scratch):
    rows = rows_in.shape[0] - EXTRA
    channels = out.shape[1]
    half = rows // 2
    count = half + 2 * HALO
    chain = Chain(channels, None, order, rows_in, ((0, 1), (count + 1, count + 4)), scratch)
    chain.put_some(1 if upper else 1 + HALO + half, beyond, 0, HALO)
    chain.put_some(1 + HALO * upper, rows_in, 0 if upper else half - HALO, half + HALO)
    closed = None if upper else (is_last[0] == 1, lambda row, lane: row == HALO + half)
    chain.run(1, ((0, count),), closed)
    value = chain.mixed(chain.terms([1 + HALO + i for i in range(half)]))
    for i in range(half):
        out[i] = value[:, LANES * i:LANES * (i + 1)]
    summed_out[...] = summed[...]


def edge_sizes(rows):
    block = rows // BLOCKS
    strips = block + 2 * HALO
    top = strips + 6
    bottom = top + BAND + 5
    return block, top, bottom, -(-(bottom + BAND + 5) // 8) * 8


def edge_forward(order, is_last, strips_in, rows_in, north, south, out, grad, *scratch):
    rows = rows_in.shape[0] - EXTRA
    block, top, bottom, total = edge_sizes(rows)
    channels = out.shape[1]
    count = block + 2 * HALO
    chain = Chain(0, channels, order, rows_in, ((0, 1), (1 + count, top + 1), (top + 1 + BAND, bottom + 1),
                                        (bottom + 1 + BAND, total)), scratch)
    chain.put_strips(strips_in, north, south)
    for i in range(HALO):
        chain.put(top + 1 + i, north, i)
        chain.put(bottom + 1 + 2 * HALO + i, south, i)
    for i in range(2 * HALO):
        chain.put(top + 1 + HALO + i, rows_in, i)
        chain.put(bottom + 1 + i, rows_in, rows - 2 * HALO + i)

    def closed(row, lane):
        return (row == bottom + 2 * HALO) | ((row == HALO + block) & (lane >= LANES - GROUP))

    chain.run(1, ((0, count), (top, BAND), (bottom, BAND)), (is_last[0] == 1, closed))
    main_valid, strip_valid = valid_lanes(channels)
    strip_rows = [1 + HALO + i for i in range(block)]
    band_rows = [top + 1 + HALO + i for i in range(HALO)] + [bottom + 1 + HALO + i for i in range(HALO)]
    total_grad = jnp.zeros(grad.shape, F32)
    slot = 0
    for indices, valid in ((strip_rows, strip_valid), (band_rows, main_valid)):
        terms = chain.terms(indices)
        value = chain.mixed(terms)
        for i in range(len(indices)):
            out[slot + i] = value[:, LANES * i:LANES * (i + 1)]
        slot += len(indices)
        total_grad = total_grad + chain.paired_with(indices, valid, terms)
    grad[...] = total_grad


def edge_backward(order, is_last, strips_in, rows_in, north, south, summed, out, summed_out, *scratch):
    block = strips_in.shape[0]
    count = block + 2 * HALO
    chain = Chain(out.shape[1], None, order, rows_in, ((0, 1), (1 + count, scratch[0].shape[0])), scratch)
    chain.put_strips(strips_in, north, south)
    chain.run(1, ((0, count),), (is_last[0] == 1, lambda row, lane: (row == HALO + block) & (lane >= LANES - GROUP)))
    value = chain.mixed(chain.terms([1 + HALO + i for i in range(block)]))
    for i in range(block):
        out[i] = value[:, LANES * i:LANES * (i + 1)]
    summed_out[...] = summed[...]


def assemble_kernel(upper, lower, edges, summed, out_hbm, summed_out, wide, out, sent):
    summed_out[...] = summed[...]
    half, channels, _ = upper.shape
    rows = 2 * half
    block = rows // BLOCKS
    lane = lane_index((channels, LANES))

    def put(r, s, b, value):
        strip = edges[s]
        west = turned(strip, -(GROUP * b + 5))
        east = turned(strip, LANES - 5 - (GROUP * b + SIDE + 6))
        value = jnp.where(lane < HALO, west, jnp.where(lane >= LANES - HALO, east, value))
        wide[pl.ds(r * (3 * channels + 1), channels, stride=3), :] = value.astype(F32)

    for b in range(BLOCKS):
        for s in range(block):
            r = block * b + s
            put(r, s, b, upper[r] if r < half else lower[r - half])
    if edges.shape[0] > block:
        for i in range(HALO):
            put(i, i, 0, edges[block + i])
            put(rows - HALO + i, block - HALO + i, BLOCKS - 1, edges[block + HALO + i])

    pieces = 2
    size = channels // pieces

    def narrow(i, _):
        for j in range(size):
            o = i * size + j
            out[o] = wide[pl.ds(3 * o, rows, stride=3 * channels + 1), :].astype(BF16)
        copy(i).start()
        return 0

    def copy(i):
        span = pl.ds(i * size, size)
        return pltpu.make_async_copy(out.at[span], out_hbm.at[span], sent.at[i])

    lax.fori_loop(0, pieces, narrow, 0)
    for i in range(pieces):
        copy(i).wait()


def finish_kernel(scale, mine, theirs, out):
    order, channels = out.shape[:2]
    out[...] = ((mine[...] + theirs[...]) * scale).T.reshape(order, channels, channels)


def on_device(signal, cotangent, edge_weights, circle_shift, mixing):
    channels, rows, sector = signal.shape
    order = mixing.shape[0]
    block, top, bottom, edge_total = edge_sizes(rows)
    lat, lon = lax.axis_size("lat"), lax.axis_size("lon")
    vmem = pl.BlockSpec(memory_space=pltpu.VMEM)
    smem = pl.BlockSpec(memory_space=pltpu.SMEM)
    hbm = pl.BlockSpec(memory_space=pltpu.HBM)
    shape = jax.ShapeDtypeStruct

    def packed(count):
        return shape((count, PACKED, LANES), BF16)

    def weighs(mib):
        return pl.CostEstimate(flops=0, bytes_accessed=mib * 1024 * 1024, transcendentals=0)

    per_row = block // 6
    to_west, to_east, own_strips, rows_in = pl.pallas_call(
        head_kernel,
        out_shape=(packed(per_row), packed(per_row), shape((6, per_row, PACKED, LANES), BF16),
                   shape((rows // per_row + 1, per_row, PACKED, LANES), BF16)),
        in_specs=[hbm] * 5,
        out_specs=(hbm,) * 4,
        scratch_shapes=[
            pltpu.VMEM(signal.shape, BF16),
            pltpu.VMEM(signal.shape, BF16),
            pltpu.VMEM(edge_weights.shape, BF16),
            pltpu.SMEM(circle_shift.shape, jnp.int32),
            pltpu.VMEM(mixing.shape, BF16),
            pltpu.VMEM((spread_size(2 * channels + 8, rows), LANES), F32),
            pltpu.VMEM((per_row, PACKED, LANES), BF16),
            pltpu.VMEM((per_row, PACKED, LANES), BF16),
            pltpu.VMEM((6, per_row, PACKED, LANES), BF16),
            pltpu.VMEM((rows // per_row + 1, per_row, PACKED, LANES), BF16),
            pltpu.SemaphoreType.DMA((11,)),
            pltpu.SemaphoreType.DMA((per_row, 4)),
        ],
        compiler_params=pltpu.CompilerParams(vmem_limit_bytes=PACK_VMEM),
        name="head",
    )(signal, cotangent, edge_weights, circle_shift, mixing)
    own_strips = own_strips.reshape(block, PACKED, LANES)
    rows_in = rows_in.reshape(rows + EXTRA, PACKED, LANES)

    eastward = [(i, (i + 1) % lon) for i in range(lon)]
    westward = [(j, i) for i, j in eastward]
    from_west = lax.ppermute(to_east, "lon", eastward)
    from_east = lax.ppermute(to_west, "lon", westward)

    half = rows // 2
    half_shape = shape((half, channels, LANES), BF16)
    grad_shape = shape((channels, order * channels), F32)

    def chain_scratch(total, with_pairs):
        total = -(-total // 8) * 8
        scratch = [pltpu.VMEM((total, channels, LANES), F32)] * 3 + [
            pltpu.VMEM((total, order * channels, LANES), BF16),
            pltpu.VMEM((7 * total, LANES), F32),
            pltpu.VMEM((8 * (total + 1), LANES), F32),
        ]
        return scratch + [pltpu.VMEM((total, channels, LANES), BF16)] * with_pairs

    def run_main_forward(upper, after):
        return pl.pallas_call(
            functools.partial(main_forward, upper, order),
            out_shape=(half_shape, grad_shape),
            in_specs=[vmem, vmem],
            out_specs=(vmem, vmem),
            scratch_shapes=chain_scratch(half + HALO + 4, True),
            compiler_params=params(16),
            cost_estimate=weighs(12),
            name="forward_upper" if upper else "forward_lower",
        )(rows_in, after)

    upper_f, grad_upper = run_main_forward(True, rows_in)

    strips, to_north, to_south = pl.pallas_call(
        merge_kernel,
        out_shape=(packed(block), packed(HALO + 2), packed(HALO + 2)),
        in_specs=[vmem] * 5,
        out_specs=(vmem,) * 3,
        compiler_params=params(8),
        name="merge",
    )(own_strips, rows_in, from_west, from_east, grad_upper)

    southward = [(i, i + 1) for i in range(lat - 1)]
    northward = [(j, i) for i, j in southward]
    north = lax.ppermute(to_south, "lat", southward)
    south = lax.ppermute(to_north, "lat", northward)

    lower_f, grad_lower = run_main_forward(False, to_north)

    is_last = (lax.axis_index("lat") == lat - 1).astype(jnp.int32).reshape(1)
    edge_f, grad_edge = pl.pallas_call(
        functools.partial(edge_forward, order),
        out_shape=(shape((block + 2 * HALO, channels, LANES), BF16), grad_shape),
        in_specs=[smem] + [vmem] * 4,
        out_specs=(vmem, vmem),
        scratch_shapes=chain_scratch(edge_total, True),
        compiler_params=params(16),
        cost_estimate=weighs(12),
        name="edge_forward",
    )(is_last, strips, rows_in, north, south)

    rounds = []
    for axis, devices in (("lon", lon), ("lat", lat)):
        reach = 1
        while reach < devices:
            rounds.append((axis, [(i, i ^ reach) for i in range(devices)]))
            reach *= 2
    rounds = [r for r in rounds if r[0] == "lon"] + [r for r in rounds if r[0] == "lat"][::-1]

    results = {}

    def run_backward_half(upper, share):
        name = "backward_upper" if upper else "backward_lower"
        results[name], share = pl.pallas_call(
            functools.partial(main_backward, upper, order),
            out_shape=(half_shape, grad_shape),
            in_specs=[smem] + [vmem] * 3,
            out_specs=(vmem, vmem),
            scratch_shapes=chain_scratch(half + 2 * HALO + 4, False),
            compiler_params=params(16),
            cost_estimate=weighs(12),
            name=name,
        )(is_last, rows_in, north if upper else south, share)
        return share

    def run_edge_backward(share):
        results["edge"], share = pl.pallas_call(
            functools.partial(edge_backward, order),
            out_shape=(shape((block, channels, LANES), BF16), grad_shape),
            in_specs=[smem] + [vmem] * 5,
            out_specs=(vmem, vmem),
            scratch_shapes=chain_scratch(block + 2 * HALO + 8, False),
            compiler_params=params(12),
            cost_estimate=weighs(12),
            name="edge_backward",
        )(is_last, strips, rows_in, north, south, share)
        return share

    def assemble(upper, lower, edges, share, name):
        return pl.pallas_call(
            assemble_kernel,
            out_shape=(shape(signal.shape, BF16), grad_shape),
            in_specs=[vmem] * 4,
            out_specs=(hbm, vmem),
            scratch_shapes=[
                pltpu.VMEM((spread_size(channels, rows), LANES), F32),
                pltpu.VMEM(signal.shape, BF16),
                pltpu.SemaphoreType.DMA((2,)),
            ],
            compiler_params=params(12),
            cost_estimate=weighs(8),
            name=name,
        )(upper, lower, edges, share)

    def run_assemble_forward(share):
        results["output"], share = assemble(upper_f, lower_f, edge_f, share, "assemble_forward")
        return share

    def run_assemble_backward(share):
        results["signal_grad"], share = assemble(
            results["backward_upper"], results["backward_lower"], results["edge"], share, "assemble_backward")
        return share

    beside = [functools.partial(run_backward_half, True), functools.partial(run_backward_half, False), run_edge_backward,
              run_assemble_forward, run_assemble_backward]
    share = grad_upper + grad_lower + grad_edge
    theirs = jnp.zeros_like(share)
    for number in range(max(len(rounds), len(beside))):
        if number:
            share = share + theirs
        theirs = lax.ppermute(share, *rounds[number]) if number < len(rounds) else jnp.zeros_like(share)
        if number < len(beside):
            share = beside[number](share)

    norm_scale = 1.0 / math.sqrt(rows * lat * sector * lon)
    mixing_grad = pl.pallas_call(
        functools.partial(finish_kernel, norm_scale),
        out_shape=shape(mixing.shape, F32),
        in_specs=[vmem, vmem],
        out_specs=vmem,
        compiler_params=params(4),
        name="finish",
    )(share, theirs)
    return (results["output"], results["signal_grad"], mixing_grad)


def solution(mesh):
    in_specs = (P(None, "lat", "lon"), P(None, "lat", "lon"), P(None, "lat", "lon"), P("lat"), P())
    out_specs = (P(None, "lat", "lon"), P(None, "lat", "lon"), P())
    return jax.shard_map(
        on_device, mesh=mesh, in_specs=in_specs, out_specs=out_specs, check_vma=False
    )
```

```python
import functools
import math

import jax
import jax.numpy as jnp
from jax import lax
from jax.experimental import pallas as pl
from jax.experimental.pallas import tpu as pltpu
from jax.sharding import PartitionSpec as P

F32 = jnp.float32
BF16 = jnp.bfloat16
HALO = 5
LANES = 128
BLOCKS = 4
GROUP = LANES // BLOCKS
SIDE = GROUP // 2
PACKED = 80
BAND = 3 * HALO
PACK_VMEM = 63_400_000


def params(mib):
    return pltpu.CompilerParams(vmem_limit_bytes=mib * 1024 * 1024)


def lane_index(shape):
    return lax.broadcasted_iota(jnp.int32, shape, len(shape) - 1)


def turned(x, amount):
    amount = amount % LANES
    return pltpu.roll(x, amount, 1) if amount else x


def spread_size(channels, rows):
    return rows * (3 * channels + 1)


def spread(wide, channels, c, rows, x):
    wide[pl.ds(3 * c, rows, stride=3 * channels + 1), :] = x


def gather(wide, channels, r, first, count):
    return wide[pl.ds(r * (3 * channels + 1) + 3 * first, count, stride=3), :]


def widen_all(signal, cotangent, weights, wide, ready=None):
    channels, rows, _ = signal.shape
    count = 2 * channels + 8
    for which, source in enumerate((signal, cotangent)):
        for part in range(4):
            if ready is not None:
                ready(which, part)
            for c in range(part * channels // 4, (part + 1) * channels // 4):
                spread(wide, count, which * channels + c, rows, source[c].astype(F32))
    if ready is not None:
        ready(2, 0)
    for i in range(8):
        x = weights[i].astype(F32) if i < 3 else jnp.zeros((rows, LANES), F32)
        spread(wide, count, 2 * channels + i, rows, x)


def row_loader(channels, rows, shift, wide):
    count = 2 * channels + 8
    sub = lax.broadcasted_iota(jnp.int32, (8, LANES), 0)

    def load_row(r):
        body = gather(wide, count, r, 0, 2 * channels)
        tail = gather(wide, count, r, 2 * channels, 8)
        parity = jnp.where(shift[r] == 1, 1.0, 0.0).astype(F32)
        tail = jnp.where(sub == 3, parity, tail)
        return jnp.concatenate([body, tail, jnp.zeros((8, LANES), F32)], axis=0).astype(BF16)

    return load_row


def strip_selector():
    source = lax.broadcasted_iota(jnp.int32, (BLOCKS * LANES, LANES), 0)
    lane = lane_index((BLOCKS * LANES, LANES))
    lane_in = lane % GROUP
    wanted = jnp.where(lane_in < SIDE, lane_in - 5, lane_in - SIDE + 117)
    wanted = jnp.where((lane_in >= 5) & (lane_in < SIDE + 11), wanted + LANES * (lane // GROUP), -1)
    return jnp.where(source == wanted, 1.0, 0.0).astype(BF16)


EXTRA = 4


def flags(place):
    return [(place[0] >> i) & 1 == 1 for i in range(3)]


class Either:
    def __init__(self, flag, yes, no):
        self.flag, self.yes, self.no = flag, yes, no

    def __getitem__(self, key):
        return jnp.where(self.flag, self.yes[key], self.no[key])


def head_kernel(place, signal_hbm, cotangent_hbm, weights_hbm, shift_hbm, mixing_hbm,
                first_hbm, second_hbm, strips_hbm, upper_hbm, lower_hbm,
                signal, cotangent, weights, shift, mixing, wide, first_out, second_out, strips_out, rows_out, arrived, sent):
    odd = flags(place)[1]
    channels, rows, _ = signal.shape
    block = rows // BLOCKS
    per_row = block // 6
    copies = {}
    number = 0
    for which, (source, target) in enumerate(((signal_hbm, signal), (cotangent_hbm, cotangent))):
        for part in range(4):
            span = pl.ds(part * channels // 4, channels // 4)
            copies[which, part] = pltpu.make_async_copy(source.at[span], target.at[span], arrived.at[number])
            number += 1
    for which, (source, target) in enumerate(((weights_hbm, weights), (shift_hbm, shift), (mixing_hbm, mixing))):
        copies[2 + which, 0] = pltpu.make_async_copy(source, target, arrived.at[number])
        number += 1
    for copy in copies.values():
        copy.start()
    widen_all(signal, cotangent, weights, wide, lambda *key: copies[key].wait())
    copies[3, 0].wait()
    copies[4, 0].wait()
    order = mixing.shape[0]
    rest = jnp.zeros((channels, 2 * LANES - order * channels), BF16)
    for i in range(2):
        tiles = [mixing[k] if i else mixing[k].astype(F32).T.astype(BF16) for k in range(order)]
        matrix = side_by_side(tiles + [rest])
        rows_out[rows // per_row, i] = jnp.concatenate(
            [matrix[:, :LANES], matrix[:, LANES:], jnp.zeros((PACKED - 2 * channels, LANES), BF16)], axis=0)
    for i in range(2, EXTRA):
        rows_out[rows // per_row, i] = jnp.zeros((PACKED, LANES), BF16)
    load_row = row_loader(channels, rows, shift, wide)
    selector = strip_selector()
    lane = lane_index((PACKED, LANES))

    units = rows // per_row
    near = upper_hbm.shape[0] - 1

    def sends(t):
        pairs = (
            (first_out.at[t], first_hbm.at[t]), (second_out.at[t], second_hbm.at[t]),
            (strips_out.at[:, t], strips_hbm.at[:, t]),
            (rows_out.at[pl.ds(0, near), t], upper_hbm.at[pl.ds(0, near), t]),
            (rows_out.at[pl.ds(units, 1), t], upper_hbm.at[pl.ds(near, 1), t]),
            (rows_out.at[pl.ds(units - near, near + 1), t], lower_hbm.at[:, t]))
        return [pltpu.make_async_copy(*pair, sent.at[t, i]) for i, pair in enumerate(pairs)]

    def each(t, _):
        groups = []
        for m in range(6):
            tiles = [load_row(block * b + per_row * m + t) for b in range(BLOCKS)]
            for b in range(BLOCKS):
                rows_out[b * 6 + m, t] = tiles[b]
            groups.append(side_by_side(tiles))
        strips = jnp.dot(jnp.concatenate(groups, axis=0), selector, preferred_element_type=F32).astype(BF16)
        west = jnp.zeros((PACKED, LANES), BF16)
        east = jnp.zeros((PACKED, LANES), BF16)
        for m in range(6):
            strip = strips[PACKED * m:PACKED * (m + 1)]
            strips_out[m, t] = strip
            west = jnp.where((lane - 5 * m - 5) % GROUP < 5, turned(strip, 5 * m), west)
            east = jnp.where((lane - 5 * m) % GROUP < 5, turned(strip, 5 * m - SIDE - 6), east)
        first_out[t] = jnp.where(odd, west, east)
        second_out[t] = jnp.where(odd, east, west)
        for copy in sends(t):
            copy.start()
        return 0

    lax.fori_loop(0, per_row, each, 0)
    for t in range(per_row):
        for copy in sends(t):
            copy.wait()


def merge_kernel(place, strips_in, upper, lower, lon_first, lon_second, _, strips_out, first_out, second_out):
    block = strips_in.shape[0]
    near = upper.shape[0] - EXTRA
    _, odd, odd_lat = flags(place)
    from_west = Either(odd, lon_first, lon_second)
    from_east = Either(odd, lon_second, lon_first)
    per_row = block // 6
    lane = lane_index((PACKED, LANES))
    lane_in = lane % GROUP

    def each(t, _):
        west = from_west[t]
        east = from_east[t]
        for m in range(6):
            strip = strips_in[per_row * m + t]
            strip = jnp.where(lane_in < 5, turned(west, -5 * m), strip)
            strip = jnp.where(lane_in >= GROUP - 5, turned(east, 22 - 5 * m), strip)
            strips_out[per_row * m + t] = strip
        return 0

    lax.fori_loop(0, per_row, each, 0)
    to_north, to_south = [], []
    for out, rows_in, first_row, first_strip, side in (
        (to_north, upper, 0, 0, 0), (to_south, lower, near - HALO, block - HALO, BLOCKS - 1)):
        for i in range(HALO):
            out.append(rows_in[first_row + i])
        corner = turned(strips_out[first_strip], -GROUP * side)
        for g in range(1, BLOCKS):
            piece = turned(strips_out[first_strip + g], GROUP * (g - side))
            corner = jnp.where((lane >= GROUP * g) & (lane < GROUP * (g + 1)), piece, corner)
        out.append(corner)
        out.append(turned(strips_out[first_strip + HALO - 1], -GROUP * side))
    for i in range(HALO + 2):
        first_out[i] = jnp.where(odd_lat, to_north[i], to_south[i])
        second_out[i] = jnp.where(odd_lat, to_south[i], to_north[i])


def write_coefficients(total, first, w_east, w_south, w_diag, parity, keep, coef, shifted):
    count = w_east.shape[0]
    w_back = jnp.where(parity > 0.5, turned(w_diag, 1), turned(w_diag, -1))
    w_west = turned(w_east, 1)
    shifted[0:8, :] = jnp.zeros((8, LANES), F32)
    shifted[8:8 + count, :] = w_south + w_back
    degree = w_east + w_west + w_south + w_diag + shifted[7:7 + count, :]
    third = -1.0 / 3.0
    arrays = [degree * (1.0 / 3.0) - 2.0, w_east * third, w_west * third]
    for array in (w_south, w_diag, w_back):
        arrays.append(array * third if keep is None else array * keep * third)
    for i, array in enumerate(arrays + [parity]):
        coef[i * total + first:i * total + first + count, :] = array


def stencil_steps(order, channels, total, coef, buffers, kept, trips, regions):
    groups = channels // 8

    def coef_row(i, at):
        return coef[pl.ds(i * total + at, 8, stride=0), :]

    def step(position, now, older, newer):
        last = position == order - 1

        def one_row(at, level, down, before):
            coefs = [coef_row(i, at) for i in range(7)]
            c, e, w, s, d, back, parity = coefs
            here = parity > 0.5
            s_above, d_above, above = before
            new, next_level, next_down = [], [], []
            for g in range(groups):
                span = slice(8 * g, 8 * g + 8)
                v = now[at, span, :]
                v_east = pltpu.roll(v, LANES - 1, 1)
                v_west = pltpu.roll(v, 1, 1)
                value = level[g] + s_above * v + d_above * jnp.where(above, v_east, v_west)
                new.append(value * 0.5 if position == 1 else value)
                value = c * v + e * v_east + w * v_west + down[g]
                next_level.append(value if position == 1 else value - older[at, span, :])
                next_down.append(s * v + back * jnp.where(here, v_west, v_east))
            if not last:
                for g in range(groups):
                    newer[at - 1, 8 * g:8 * g + 8, :] = new[g]
            for h in range(groups // 2):
                first = channels * position + 16 * h
                pair = jnp.concatenate([new[2 * h], new[2 * h + 1]], axis=0)
                kept[at - 1, first:first + 16, :] = pair.astype(BF16)
            return tuple(next_level), tuple(next_down), (s, d, here)

        counts = [-(-(count + 2 - 2 * position) // trips) for _, count in regions]

        def several(trip, carry):
            states = []
            for (base, _), count, (level, down) in zip(regions, counts, carry):
                at = base + position + trip * count
                before = (coef_row(3, at - 1), coef_row(4, at - 1), coef_row(6, at - 1) > 0.5)
                states.append([at, level, down, before])
            for j in range(max(counts)):
                for state, count in zip(states, counts):
                    if j < count:
                        state[1:] = one_row(state[0] + j, *state[1:])
            return tuple((level, down) for _, level, down, _ in states)

        zeros = tuple(jnp.zeros((8, LANES), F32) for _ in range(groups))
        lax.fori_loop(0, trips, several, tuple((zeros, zeros) for _ in regions))

    for position in range(1, order):
        step(position, buffers[(position - 1) % 3], buffers[(position - 2) % 3], buffers[position % 3])


def zero_guards(buffers, coef, total, guards):
    for first, end in guards:
        for index in range(first, end):
            for buffer in buffers:
                buffer[index] = jnp.zeros(buffer.shape[1:], F32)
        for i in range(7):
            coef[i * total + first:i * total + end, :] = jnp.zeros((end - first, LANES), F32)


CONTRACT_LANES = (((1,), (1,)), ((), ()))
CONTRACT_ROWS = (((0,), (0,)), ((), ()))


def side_by_side(tiles):
    return jnp.concatenate(tiles, axis=1)


class Chain:
    def __init__(self, first, other, order, rows_in, guards, scratch):
        self.buffers, self.kept, self.coef, self.wide = scratch[:3], *scratch[3:6]
        self.paired = scratch[6] if other is not None else None
        self.first, self.other, self.rows_in, self.order = first, other, rows_in, order
        self.channels = self.buffers[0].shape[1]
        self.total = self.kept.shape[0]
        for begin, end in guards:
            for index in range(begin, end):
                self.kept[index] = jnp.zeros((self.order * self.channels, LANES), BF16)
        zero_guards(self.buffers, self.coef, self.total, guards)
        for begin, end in guards:
            for i in range(4):
                at = i * (self.total + 1)
                self.wide[at + begin:at + end, :] = jnp.zeros((end - begin, LANES), F32)

    def put(self, index, ref, at, tile=None):
        def part(begin, count):
            return ref[at, begin:begin + count, :] if tile is None else tile[begin:begin + count]
        self.wide[pl.ds(index, 8, stride=self.total + 1), :] = part(PACKED - 16, 16).astype(F32)[:8]
        field = part(self.first, self.channels)
        self.buffers[0][index] = field.astype(F32)
        self.kept[index, 0:self.channels, :] = field
        if self.other is not None:
            self.paired[index] = part(self.other, self.channels)

    def put_some(self, index, ref, first, count):
        for i in range(count):
            self.put(index + i, ref, first + i)

    def put_strips(self, strips, north, south):
        block = strips.shape[0]
        self.put_some(1 + HALO, strips, 0, block)
        lane = lane_index((PACKED, LANES))
        for i in range(HALO):
            at_end = i == HALO - 1
            above = turned(strips[block - HALO + i], GROUP)
            corner = turned(north[HALO + at_end], 0 if at_end else -GROUP * i)
            self.put(1 + i, None, None, jnp.where(lane < GROUP, corner, above))
            below = turned(strips[i], -GROUP)
            corner = turned(south[HALO + at_end], -GROUP - (0 if at_end else GROUP * i))
            self.put(1 + HALO + block + i, None, None, jnp.where(lane >= LANES - GROUP, corner, below))

    def run(self, trips, regions, closed=None):
        total = self.total
        starts = [i * (total + 1) for i in range(4)]
        w_east, w_south, w_diag, parity = [self.wide[at:at + total, :] for at in starts]
        keep = None
        if closed is not None:
            is_end, where = closed
            row = lax.broadcasted_iota(jnp.int32, (total, LANES), 0)
            keep = jnp.where(where(row, lane_index((total, LANES))) & is_end, 0.0, 1.0).astype(F32)
        write_coefficients(total, 0, w_east, w_south, w_diag, parity, keep, self.coef, self.wide)
        stencil_steps(self.order, self.channels, total, self.coef, self.buffers, self.kept, trips, regions)

    def terms(self, indices):
        return side_by_side([self.kept[i] for i in indices])

    def mixed(self, terms):
        place = self.rows_in.shape[0] - EXTRA + (self.other is None)
        matrix = side_by_side([self.rows_in[place, i:i + self.channels, :] for i in (0, self.channels)])
        matrix = matrix[:, :self.order * self.channels]
        value = jnp.dot(matrix, terms, preferred_element_type=F32)
        return value.astype(BF16)

    def paired_with(self, indices, valid, terms):
        left = [jnp.where(valid, self.paired[i], jnp.zeros((), BF16)) for i in indices]
        return lax.dot_general(side_by_side(left), terms, CONTRACT_LANES, preferred_element_type=F32)


def valid_lanes(channels):
    lane = lane_index((channels, LANES))
    lane_in = lane % GROUP
    in_strips = ((lane_in >= 5) & (lane_in < 10)) | ((lane_in >= SIDE + 6) & (lane_in < SIDE + 11))
    return (lane >= HALO) & (lane < LANES - HALO), in_strips


def main_forward(upper, order, rows_in, _, out, grad, *scratch):
    channels = out.shape[1]
    half = out.shape[0]
    count = half + HALO
    near = rows_in.shape[0] - EXTRA
    chain = Chain(0, channels, order, rows_in, ((0, 1), (count + 1, count + 4)), scratch)
    chain.put_some(1, rows_in, 0 if upper else near - count, count)
    chain.run(1, ((0, count),))
    valid, _ = valid_lanes(channels)
    indices = [1 + HALO + i for i in range(half - HALO)]
    terms = chain.terms(indices)
    value = chain.mixed(terms)
    for i in range(len(indices)):
        out[i + HALO * upper] = value[:, LANES * i:LANES * (i + 1)]
    grad[...] = chain.paired_with(indices, valid, terms)


def main_backward(upper, order, place, rows_in, lat_first, lat_second, summed, out, summed_out, *scratch):
    channels = out.shape[1]
    half = out.shape[0]
    count = half + 2 * HALO
    near = rows_in.shape[0] - EXTRA
    is_last, _, odd = flags(place)
    beyond = Either(odd, lat_first, lat_second) if upper else Either(odd, lat_second, lat_first)
    chain = Chain(channels, None, order, rows_in, ((0, 1), (count + 1, count + 4)), scratch)
    chain.put_some(1 if upper else 1 + HALO + half, beyond, 0, HALO)
    chain.put_some(1 + HALO * upper, rows_in, 0 if upper else near - half - HALO, half + HALO)
    closed = None if upper else (is_last, lambda row, lane: row == HALO + half)
    chain.run(1, ((0, count),), closed)
    value = chain.mixed(chain.terms([1 + HALO + i for i in range(half)]))
    for i in range(half):
        out[i] = value[:, LANES * i:LANES * (i + 1)]
    summed_out[...] = summed[...]


def edge_sizes(rows):
    block = rows // BLOCKS
    strips = block + 2 * HALO
    top = strips + 6
    bottom = top + BAND + 5
    return block, top, bottom, -(-(bottom + BAND + 5) // 8) * 8


def edge_forward(order, place, strips_in, rows_in, lower, lat_first, lat_second, out, grad, *scratch):
    near = rows_in.shape[0] - EXTRA
    block, top, bottom, total = edge_sizes(strips_in.shape[0] * BLOCKS)
    is_last, _, odd = flags(place)
    north, south = Either(odd, lat_first, lat_second), Either(odd, lat_second, lat_first)
    channels = out.shape[1]
    count = block + 2 * HALO
    chain = Chain(0, channels, order, rows_in, ((0, 1), (1 + count, top + 1), (top + 1 + BAND, bottom + 1),
                                        (bottom + 1 + BAND, total)), scratch)
    chain.put_strips(strips_in, north, south)
    for i in range(HALO):
        chain.put(top + 1 + i, north, i)
        chain.put(bottom + 1 + 2 * HALO + i, south, i)
    for i in range(2 * HALO):
        chain.put(top + 1 + HALO + i, rows_in, i)
        chain.put(bottom + 1 + i, lower, near - 2 * HALO + i)

    def closed(row, lane):
        return (row == bottom + 2 * HALO) | ((row == HALO + block) & (lane >= LANES - GROUP))

    chain.run(1, ((0, count), (top, BAND), (bottom, BAND)), (is_last, closed))
    main_valid, strip_valid = valid_lanes(channels)
    strip_rows = [1 + HALO + i for i in range(block)]
    band_rows = [top + 1 + HALO + i for i in range(HALO)] + [bottom + 1 + HALO + i for i in range(HALO)]
    total_grad = jnp.zeros(grad.shape, F32)
    slot = 0
    for indices, valid in ((strip_rows, strip_valid), (band_rows, main_valid)):
        terms = chain.terms(indices)
        value = chain.mixed(terms)
        for i in range(len(indices)):
            out[slot + i] = value[:, LANES * i:LANES * (i + 1)]
        slot += len(indices)
        total_grad = total_grad + chain.paired_with(indices, valid, terms)
    grad[...] = total_grad


def edge_backward(order, place, strips_in, rows_in, lat_first, lat_second, summed, out, summed_out, *scratch):
    block = strips_in.shape[0]
    is_last, _, odd = flags(place)
    north, south = Either(odd, lat_first, lat_second), Either(odd, lat_second, lat_first)
    count = block + 2 * HALO
    chain = Chain(out.shape[1], None, order, rows_in, ((0, 1), (1 + count, scratch[0].shape[0])), scratch)
    chain.put_strips(strips_in, north, south)
    chain.run(1, ((0, count),), (is_last, lambda row, lane: (row == HALO + block) & (lane >= LANES - GROUP)))
    value = chain.mixed(chain.terms([1 + HALO + i for i in range(block)]))
    for i in range(block):
        out[i] = value[:, LANES * i:LANES * (i + 1)]
    summed_out[...] = summed[...]


def assemble_kernel(upper, lower, edges, summed, out_hbm, summed_out, wide, out, sent):
    summed_out[...] = summed[...]
    half, channels, _ = upper.shape
    rows = 2 * half
    block = rows // BLOCKS
    lane = lane_index((channels, LANES))

    def put(r, s, b, value):
        strip = edges[s]
        west = turned(strip, -(GROUP * b + 5))
        east = turned(strip, LANES - 5 - (GROUP * b + SIDE + 6))
        value = jnp.where(lane < HALO, west, jnp.where(lane >= LANES - HALO, east, value))
        wide[pl.ds(r * (3 * channels + 1), channels, stride=3), :] = value.astype(F32)

    for b in range(BLOCKS):
        for s in range(block):
            r = block * b + s
            put(r, s, b, upper[r] if r < half else lower[r - half])
    if edges.shape[0] > block:
        for i in range(HALO):
            put(i, i, 0, edges[block + i])
            put(rows - HALO + i, block - HALO + i, BLOCKS - 1, edges[block + HALO + i])

    pieces = 2
    size = channels // pieces

    def narrow(i, _):
        for j in range(size):
            o = i * size + j
            out[o] = wide[pl.ds(3 * o, rows, stride=3 * channels + 1), :].astype(BF16)
        copy(i).start()
        return 0

    def copy(i):
        span = pl.ds(i * size, size)
        return pltpu.make_async_copy(out.at[span], out_hbm.at[span], sent.at[i])

    lax.fori_loop(0, pieces, narrow, 0)
    for i in range(pieces):
        copy(i).wait()


def finish_kernel(scale, mine, theirs, out):
    order, channels = out.shape[:2]
    out[...] = ((mine[...] + theirs[...]) * scale).T.reshape(order, channels, channels)


def on_device(signal, cotangent, edge_weights, circle_shift, mixing):
    channels, rows, sector = signal.shape
    order = mixing.shape[0]
    block, top, bottom, edge_total = edge_sizes(rows)
    lat, lon = lax.axis_size("lat"), lax.axis_size("lon")
    vmem = pl.BlockSpec(memory_space=pltpu.VMEM)
    smem = pl.BlockSpec(memory_space=pltpu.SMEM)
    hbm = pl.BlockSpec(memory_space=pltpu.HBM)
    shape = jax.ShapeDtypeStruct

    def packed(count):
        return shape((count, PACKED, LANES), BF16)

    def weighs(mib):
        return pl.CostEstimate(flops=0, bytes_accessed=mib * 1024 * 1024, transcendentals=0)

    per_row = block // 6
    half = rows // 2
    near = -(-(half + HALO) // per_row)
    half_rows = shape((near + 1, per_row, PACKED, LANES), BF16)
    at_lat, at_lon = lax.axis_index("lat"), lax.axis_index("lon")
    place = (at_lat == lat - 1).astype(jnp.int32) + 2 * (at_lon % 2) + 4 * (at_lat % 2)
    place = place.astype(jnp.int32).reshape(1)
    lon_first, lon_second, own_strips, upper, lower = pl.pallas_call(
        head_kernel,
        out_shape=(packed(per_row), packed(per_row), shape((6, per_row, PACKED, LANES), BF16), half_rows, half_rows),
        in_specs=[smem] + [hbm] * 5,
        out_specs=(hbm,) * 5,
        scratch_shapes=[
            pltpu.VMEM(signal.shape, BF16),
            pltpu.VMEM(signal.shape, BF16),
            pltpu.VMEM(edge_weights.shape, BF16),
            pltpu.SMEM(circle_shift.shape, jnp.int32),
            pltpu.VMEM(mixing.shape, BF16),
            pltpu.VMEM((spread_size(2 * channels + 8, rows), LANES), F32),
            pltpu.VMEM((per_row, PACKED, LANES), BF16),
            pltpu.VMEM((per_row, PACKED, LANES), BF16),
            pltpu.VMEM((6, per_row, PACKED, LANES), BF16),
            pltpu.VMEM((rows // per_row + 1, per_row, PACKED, LANES), BF16),
            pltpu.SemaphoreType.DMA((11,)),
            pltpu.SemaphoreType.DMA((per_row, 6)),
        ],
        compiler_params=pltpu.CompilerParams(vmem_limit_bytes=PACK_VMEM),
        name="head",
    )(place, signal, cotangent, edge_weights, circle_shift, mixing)
    own_strips = own_strips.reshape(block, PACKED, LANES)
    upper, lower = [array.reshape((near + 1) * per_row, PACKED, LANES) for array in (upper, lower)]

    pairs = [(i, i ^ 1) for i in range(lon)]
    other_pairs = [(i, (i + 1 if i % 2 else i - 1) % lon) for i in range(lon)]
    lon_first = lax.ppermute(lon_first, "lon", pairs)
    lon_second = lax.ppermute(lon_second, "lon", other_pairs)

    half_shape = shape((half, channels, LANES), BF16)
    grad_shape = shape((channels, order * channels), F32)

    def chain_scratch(total, with_pairs):
        total = -(-total // 8) * 8
        scratch = [pltpu.VMEM((total, channels, LANES), F32)] * 3 + [
            pltpu.VMEM((total, order * channels, LANES), BF16),
            pltpu.VMEM((7 * total, LANES), F32),
            pltpu.VMEM((8 * (total + 1), LANES), F32),
        ]
        return scratch + [pltpu.VMEM((total, channels, LANES), BF16)] * with_pairs

    def run_main_forward(is_upper, after):
        return pl.pallas_call(
            functools.partial(main_forward, is_upper, order),
            out_shape=(half_shape, grad_shape),
            in_specs=[vmem, vmem],
            out_specs=(vmem, vmem),
            scratch_shapes=chain_scratch(half + HALO + 4, True),
            compiler_params=params(16),
            cost_estimate=weighs(12),
            name="forward_upper" if is_upper else "forward_lower",
        )(upper if is_upper else lower, after)

    upper_f, grad_upper = run_main_forward(True, upper)

    strips, lat_first, lat_second = pl.pallas_call(
        merge_kernel,
        out_shape=(packed(block), packed(HALO + 2), packed(HALO + 2)),
        in_specs=[smem] + [vmem] * 6,
        out_specs=(vmem,) * 3,
        compiler_params=params(8),
        name="merge",
    )(place, own_strips, upper, lower, lon_first, lon_second, grad_upper)

    pairs = [(i, i ^ 1) for i in range(lat)]
    other_pairs = [(i, i + 1 if i % 2 else i - 1) for i in range(1, lat - 1)]
    after = lat_first
    lat_first = lax.ppermute(lat_first, "lat", pairs)
    lat_second = lax.ppermute(lat_second, "lat", other_pairs)
    lower_f, grad_lower = run_main_forward(False, after)

    edge_f, grad_edge = pl.pallas_call(
        functools.partial(edge_forward, order),
        out_shape=(shape((block + 2 * HALO, channels, LANES), BF16), grad_shape),
        in_specs=[smem] + [vmem] * 5,
        out_specs=(vmem, vmem),
        scratch_shapes=chain_scratch(edge_total, True),
        compiler_params=params(16),
        cost_estimate=weighs(12),
        name="edge_forward",
    )(place, strips, upper, lower, lat_first, lat_second)

    rounds = []
    for axis, devices in (("lon", lon), ("lat", lat)):
        reach = 1
        while reach < devices:
            rounds.append((axis, [(i, i ^ reach) for i in range(devices)]))
            reach *= 2
    rounds = [r for r in rounds if r[0] == "lon"] + [r for r in rounds if r[0] == "lat"][::-1]

    results = {}

    def run_backward_half(is_upper, share):
        name = "backward_upper" if is_upper else "backward_lower"
        results[name], share = pl.pallas_call(
            functools.partial(main_backward, is_upper, order),
            out_shape=(half_shape, grad_shape),
            in_specs=[smem] + [vmem] * 4,
            out_specs=(vmem, vmem),
            scratch_shapes=chain_scratch(half + 2 * HALO + 4, False),
            compiler_params=params(16),
            cost_estimate=weighs(12),
            name=name,
        )(place, upper if is_upper else lower, lat_first, lat_second, share)
        return share

    def run_edge_backward(share):
        results["edge"], share = pl.pallas_call(
            functools.partial(edge_backward, order),
            out_shape=(shape((block, channels, LANES), BF16), grad_shape),
            in_specs=[smem] + [vmem] * 5,
            out_specs=(vmem, vmem),
            scratch_shapes=chain_scratch(block + 2 * HALO + 8, False),
            compiler_params=params(12),
            cost_estimate=weighs(12),
            name="edge_backward",
        )(place, strips, upper, lat_first, lat_second, share)
        return share

    def assemble(upper, lower, edges, share, name):
        return pl.pallas_call(
            assemble_kernel,
            out_shape=(shape(signal.shape, BF16), grad_shape),
            in_specs=[vmem] * 4,
            out_specs=(hbm, vmem),
            scratch_shapes=[
                pltpu.VMEM((spread_size(channels, rows), LANES), F32),
                pltpu.VMEM(signal.shape, BF16),
                pltpu.SemaphoreType.DMA((2,)),
            ],
            compiler_params=params(12),
            cost_estimate=weighs(8),
            name=name,
        )(upper, lower, edges, share)

    def run_assemble_forward(share):
        results["output"], share = assemble(upper_f, lower_f, edge_f, share, "assemble_forward")
        return share

    def run_assemble_backward(share):
        results["signal_grad"], share = assemble(
            results["backward_upper"], results["backward_lower"], results["edge"], share, "assemble_backward")
        return share

    beside = [functools.partial(run_backward_half, True), functools.partial(run_backward_half, False), run_edge_backward,
              run_assemble_forward, run_assemble_backward]
    share = grad_upper + grad_lower + grad_edge
    theirs = jnp.zeros_like(share)
    for number in range(max(len(rounds), len(beside))):
        if number:
            share = share + theirs
        theirs = lax.ppermute(share, *rounds[number]) if number < len(rounds) else jnp.zeros_like(share)
        if number < len(beside):
            share = beside[number](share)

    norm_scale = 1.0 / math.sqrt(rows * lat * sector * lon)
    mixing_grad = pl.pallas_call(
        functools.partial(finish_kernel, norm_scale),
        out_shape=shape(mixing.shape, F32),
        in_specs=[vmem, vmem],
        out_specs=vmem,
        compiler_params=params(4),
        name="finish",
    )(share, theirs)
    return (results["output"], results["signal_grad"], mixing_grad)


def solution(mesh):
    in_specs = (P(None, "lat", "lon"), P(None, "lat", "lon"), P(None, "lat", "lon"), P("lat"), P())
    out_specs = (P(None, "lat", "lon"), P(None, "lat", "lon"), P())
    return jax.shard_map(
        on_device, mesh=mesh, in_specs=in_specs, out_specs=out_specs, check_vma=False
    )
```

```python
import functools
import math

import jax
import jax.numpy as jnp
from jax import lax
from jax.experimental import pallas as pl
from jax.experimental.pallas import tpu as pltpu
from jax.sharding import PartitionSpec as P

F32 = jnp.float32
BF16 = jnp.bfloat16
HALO = 5
LANES = 128
BLOCKS = 4
GROUP = LANES // BLOCKS
SIDE = GROUP // 2
PACKED = 80
BAND = 3 * HALO
PACK_VMEM = 63_400_000


def params(mib):
    return pltpu.CompilerParams(vmem_limit_bytes=mib * 1024 * 1024)


def lane_index(shape):
    return lax.broadcasted_iota(jnp.int32, shape, len(shape) - 1)


def turned(x, amount):
    amount = amount % LANES
    return pltpu.roll(x, amount, 1) if amount else x


def spread_size(channels, rows):
    return rows * (3 * channels + 1)


def spread(wide, channels, c, rows, x):
    wide[pl.ds(3 * c, rows, stride=3 * channels + 1), :] = x


def gather(wide, channels, r, first, count):
    return wide[pl.ds(r * (3 * channels + 1) + 3 * first, count, stride=3), :]


def widen_all(signal, cotangent, weights, wide, ready=None):
    channels, rows, _ = signal.shape
    count = 2 * channels + 8
    for which, source in enumerate((signal, cotangent)):
        for part in range(4):
            if ready is not None:
                ready(which, part)
            for c in range(part * channels // 4, (part + 1) * channels // 4):
                spread(wide, count, which * channels + c, rows, source[c].astype(F32))
    if ready is not None:
        ready(2, 0)
    for i in range(8):
        x = weights[i].astype(F32) if i < 3 else jnp.zeros((rows, LANES), F32)
        spread(wide, count, 2 * channels + i, rows, x)


def row_loader(channels, rows, shift, wide):
    count = 2 * channels + 8
    sub = lax.broadcasted_iota(jnp.int32, (8, LANES), 0)

    def load_row(r):
        body = gather(wide, count, r, 0, 2 * channels)
        tail = gather(wide, count, r, 2 * channels, 8)
        parity = jnp.where(shift[r] == 1, 1.0, 0.0).astype(F32)
        tail = jnp.where(sub == 3, parity, tail)
        return jnp.concatenate([body, tail, jnp.zeros((8, LANES), F32)], axis=0).astype(BF16)

    return load_row


def strip_selector():
    source = lax.broadcasted_iota(jnp.int32, (BLOCKS * LANES, LANES), 0)
    lane = lane_index((BLOCKS * LANES, LANES))
    lane_in = lane % GROUP
    wanted = jnp.where(lane_in < SIDE, lane_in - 5, lane_in - SIDE + 117)
    wanted = jnp.where((lane_in >= 5) & (lane_in < SIDE + 11), wanted + LANES * (lane // GROUP), -1)
    return jnp.where(source == wanted, 1.0, 0.0).astype(BF16)


EXTRA = 4


def flags(place):
    return [(place[0] >> i) & 1 == 1 for i in range(3)]


class Either:
    def __init__(self, flag, yes, no):
        self.flag, self.yes, self.no = flag, yes, no

    def __getitem__(self, key):
        return jnp.where(self.flag, self.yes[key], self.no[key])


def head_kernel(place, signal_hbm, cotangent_hbm, weights_hbm, shift_hbm, mixing_hbm,
                first_hbm, second_hbm, strips_hbm, upper_hbm, lower_hbm,
                signal, cotangent, weights, shift, mixing, wide, first_out, second_out, strips_out, rows_out, arrived, sent):
    odd = flags(place)[1]
    channels, rows, _ = signal.shape
    block = rows // BLOCKS
    per_row = block // 6
    copies = {}
    number = 0
    for which, (source, target) in enumerate(((signal_hbm, signal), (cotangent_hbm, cotangent))):
        for part in range(4):
            span = pl.ds(part * channels // 4, channels // 4)
            copies[which, part] = pltpu.make_async_copy(source.at[span], target.at[span], arrived.at[number])
            number += 1
    for which, (source, target) in enumerate(((weights_hbm, weights), (shift_hbm, shift), (mixing_hbm, mixing))):
        copies[2 + which, 0] = pltpu.make_async_copy(source, target, arrived.at[number])
        number += 1
    for copy in copies.values():
        copy.start()
    widen_all(signal, cotangent, weights, wide, lambda *key: copies[key].wait())
    copies[3, 0].wait()
    copies[4, 0].wait()
    order = mixing.shape[0]
    rest = jnp.zeros((channels, 2 * LANES - order * channels), BF16)
    for i in range(2):
        tiles = [mixing[k] if i else mixing[k].astype(F32).T.astype(BF16) for k in range(order)]
        matrix = side_by_side(tiles + [rest])
        rows_out[rows // per_row, i] = jnp.concatenate(
            [matrix[:, :LANES], matrix[:, LANES:], jnp.zeros((PACKED - 2 * channels, LANES), BF16)], axis=0)
    for i in range(2, EXTRA):
        rows_out[rows // per_row, i] = jnp.zeros((PACKED, LANES), BF16)
    load_row = row_loader(channels, rows, shift, wide)
    selector = strip_selector()
    lane = lane_index((PACKED, LANES))

    units = rows // per_row
    near = upper_hbm.shape[0] - 1

    def sends(t):
        pairs = (
            (first_out.at[t], first_hbm.at[t]), (second_out.at[t], second_hbm.at[t]),
            (strips_out.at[:, t], strips_hbm.at[:, t]),
            (rows_out.at[pl.ds(0, near), t], upper_hbm.at[pl.ds(0, near), t]),
            (rows_out.at[pl.ds(units, 1), t], upper_hbm.at[pl.ds(near, 1), t]),
            (rows_out.at[pl.ds(units - near, near + 1), t], lower_hbm.at[:, t]))
        return [pltpu.make_async_copy(*pair, sent.at[t, i]) for i, pair in enumerate(pairs)]

    def each(t, _):
        groups = []
        for m in range(6):
            tiles = [load_row(block * b + per_row * m + t) for b in range(BLOCKS)]
            for b in range(BLOCKS):
                rows_out[b * 6 + m, t] = tiles[b]
            groups.append(side_by_side(tiles))
        strips = jnp.dot(jnp.concatenate(groups, axis=0), selector, preferred_element_type=F32).astype(BF16)
        west = jnp.zeros((PACKED, LANES), BF16)
        east = jnp.zeros((PACKED, LANES), BF16)
        for m in range(6):
            strip = strips[PACKED * m:PACKED * (m + 1)]
            strips_out[m, t] = strip
            west = jnp.where((lane - 5 * m - 5) % GROUP < 5, turned(strip, 5 * m), west)
            east = jnp.where((lane - 5 * m) % GROUP < 5, turned(strip, 5 * m - SIDE - 6), east)
        first_out[t] = jnp.where(odd, west, east)
        second_out[t] = jnp.where(odd, east, west)
        for copy in sends(t):
            copy.start()
        return 0

    lax.fori_loop(0, per_row, each, 0)
    for t in range(per_row):
        for copy in sends(t):
            copy.wait()


def merge_kernel(place, strips_in, upper, lower, lon_first, lon_second, _, strips_out, first_out, second_out):
    block = strips_in.shape[0]
    near = upper.shape[0] - EXTRA
    _, odd, odd_lat = flags(place)
    from_west = Either(odd, lon_first, lon_second)
    from_east = Either(odd, lon_second, lon_first)
    per_row = block // 6
    lane = lane_index((PACKED, LANES))
    lane_in = lane % GROUP

    def each(t, _):
        west = from_west[t]
        east = from_east[t]
        for m in range(6):
            strip = strips_in[per_row * m + t]
            strip = jnp.where(lane_in < 5, turned(west, -5 * m), strip)
            strip = jnp.where(lane_in >= GROUP - 5, turned(east, 22 - 5 * m), strip)
            strips_out[per_row * m + t] = strip
        return 0

    lax.fori_loop(0, per_row, each, 0)
    to_north, to_south = [], []
    for out, rows_in, first_row, first_strip, side in (
        (to_north, upper, 0, 0, 0), (to_south, lower, near - HALO, block - HALO, BLOCKS - 1)):
        for i in range(HALO):
            out.append(rows_in[first_row + i])
        corner = turned(strips_out[first_strip], -GROUP * side)
        for g in range(1, BLOCKS):
            piece = turned(strips_out[first_strip + g], GROUP * (g - side))
            corner = jnp.where((lane >= GROUP * g) & (lane < GROUP * (g + 1)), piece, corner)
        out.append(corner)
        out.append(turned(strips_out[first_strip + HALO - 1], -GROUP * side))
    for i in range(HALO + 2):
        first_out[i] = jnp.where(odd_lat, to_north[i], to_south[i])
        second_out[i] = jnp.where(odd_lat, to_south[i], to_north[i])


def write_coefficients(total, first, w_east, w_south, w_diag, parity, keep, coef, shifted):
    count = w_east.shape[0]
    w_back = jnp.where(parity > 0.5, turned(w_diag, 1), turned(w_diag, -1))
    w_west = turned(w_east, 1)
    shifted[0:8, :] = jnp.zeros((8, LANES), F32)
    shifted[8:8 + count, :] = w_south + w_back
    degree = w_east + w_west + w_south + w_diag + shifted[7:7 + count, :]
    third = -1.0 / 3.0
    arrays = [degree * (1.0 / 3.0) - 2.0, w_east * third, w_west * third]
    for array in (w_south, w_diag, w_back):
        arrays.append(array * third if keep is None else array * keep * third)
    for i, array in enumerate(arrays + [parity]):
        coef[i * total + first:i * total + first + count, :] = array


def stencil_steps(order, channels, total, coef, buffers, kept, trips, regions):
    groups = channels // 8

    def coef_row(i, at):
        return coef[pl.ds(i * total + at, 8, stride=0), :]

    def step(position, now, older, newer):
        last = position == order - 1

        def one_row(at, level, down, before, has_new=True, has_level=True, has_down=True):
            coefs = [coef_row(i, at) for i in range(7)]
            c, e, w, s, d, back, parity = coefs
            here = parity > 0.5
            s_above, d_above, above = before or (None, None, None)
            new, next_level, next_down = [], [], []
            for g in range(groups):
                span = slice(8 * g, 8 * g + 8)
                v = now[at, span, :]
                v_east = pltpu.roll(v, LANES - 1, 1)
                v_west = pltpu.roll(v, 1, 1)
                if has_new:
                    value = level[g] + s_above * v + d_above * jnp.where(above, v_east, v_west)
                    new.append(value * 0.5 if position == 1 else value)
                if has_level:
                    value = c * v + e * v_east + w * v_west + down[g]
                    next_level.append(value if position == 1 else value - older[at, span, :])
                if has_down:
                    next_down.append(s * v + back * jnp.where(here, v_west, v_east))
            if not has_new:
                return tuple(next_level), tuple(next_down), (s, d, here)
            if not last:
                for g in range(groups):
                    newer[at - 1, 8 * g:8 * g + 8, :] = new[g]
            for h in range(groups // 2):
                first = channels * position + 16 * h
                pair = jnp.concatenate([new[2 * h], new[2 * h + 1]], axis=0)
                kept[at - 1, first:first + 16, :] = pair.astype(BF16)
            return tuple(next_level), tuple(next_down), (s, d, here)

        counts = [-(-(count + 2 - 2 * position) // trips) for _, count in regions]

        def at_once():
            for j in range(max(counts)):
                for n, count in enumerate(counts):
                    if j < count:
                        at = regions[n][0] + position + j
                        left[n] = one_row(at, *left[n], j > 1, 0 < j < count - 1, j < count - 1)

        left = [((), (), None)] * len(regions)
        if trips == 1:
            at_once()
            return

        def several(trip, carry):
            states = []
            for (base, _), count, (level, down) in zip(regions, counts, carry):
                at = base + position + trip * count
                before = (coef_row(3, at - 1), coef_row(4, at - 1), coef_row(6, at - 1) > 0.5)
                states.append([at, level, down, before])
            for j in range(max(counts)):
                for state, count in zip(states, counts):
                    if j < count:
                        state[1:] = one_row(state[0] + j, *state[1:])
            return tuple((level, down) for _, level, down, _ in states)

        zeros = tuple(jnp.zeros((8, LANES), F32) for _ in range(groups))
        lax.fori_loop(0, trips, several, tuple((zeros, zeros) for _ in regions))

    for position in range(1, order):
        step(position, buffers[(position - 1) % 3], buffers[(position - 2) % 3], buffers[position % 3])


def zero_guards(buffers, coef, total, guards):
    for first, end in guards:
        for index in range(first, end):
            for buffer in buffers:
                buffer[index] = jnp.zeros(buffer.shape[1:], F32)
        for i in range(7):
            coef[i * total + first:i * total + end, :] = jnp.zeros((end - first, LANES), F32)


CONTRACT_LANES = (((1,), (1,)), ((), ()))
CONTRACT_ROWS = (((0,), (0,)), ((), ()))


def side_by_side(tiles):
    return jnp.concatenate(tiles, axis=1)


class Chain:
    def __init__(self, first, other, order, rows_in, guards, scratch):
        self.buffers, self.kept, self.coef, self.wide = scratch[:3], *scratch[3:6]
        self.paired = scratch[6] if other is not None else None
        self.first, self.other, self.rows_in, self.order = first, other, rows_in, order
        self.channels = self.buffers[0].shape[1]
        self.total = self.kept.shape[0]
        for begin, end in guards:
            for index in range(begin, end):
                self.kept[index] = jnp.zeros((self.order * self.channels, LANES), BF16)
        zero_guards(self.buffers, self.coef, self.total, guards)
        for begin, end in guards:
            for i in range(4):
                at = i * (self.total + 1)
                self.wide[at + begin:at + end, :] = jnp.zeros((end - begin, LANES), F32)

    def put(self, index, ref, at, tile=None):
        def part(begin, count):
            return ref[at, begin:begin + count, :] if tile is None else tile[begin:begin + count]
        self.wide[pl.ds(index, 8, stride=self.total + 1), :] = part(PACKED - 16, 16).astype(F32)[:8]
        field = part(self.first, self.channels)
        self.buffers[0][index] = field.astype(F32)
        self.kept[index, 0:self.channels, :] = field
        if self.other is not None:
            self.paired[index] = part(self.other, self.channels)

    def put_some(self, index, ref, first, count):
        for i in range(count):
            self.put(index + i, ref, first + i)

    def put_strips(self, strips, north, south):
        block = strips.shape[0]
        self.put_some(1 + HALO, strips, 0, block)
        lane = lane_index((PACKED, LANES))
        for i in range(HALO):
            at_end = i == HALO - 1
            above = turned(strips[block - HALO + i], GROUP)
            corner = turned(north[HALO + at_end], 0 if at_end else -GROUP * i)
            self.put(1 + i, None, None, jnp.where(lane < GROUP, corner, above))
            below = turned(strips[i], -GROUP)
            corner = turned(south[HALO + at_end], -GROUP - (0 if at_end else GROUP * i))
            self.put(1 + HALO + block + i, None, None, jnp.where(lane >= LANES - GROUP, corner, below))

    def run(self, trips, regions, closed=None):
        total = self.total
        starts = [i * (total + 1) for i in range(4)]
        w_east, w_south, w_diag, parity = [self.wide[at:at + total, :] for at in starts]
        keep = None
        if closed is not None:
            is_end, where = closed
            row = lax.broadcasted_iota(jnp.int32, (total, LANES), 0)
            keep = jnp.where(where(row, lane_index((total, LANES))) & is_end, 0.0, 1.0).astype(F32)
        write_coefficients(total, 0, w_east, w_south, w_diag, parity, keep, self.coef, self.wide)
        stencil_steps(self.order, self.channels, total, self.coef, self.buffers, self.kept, trips, regions)

    def terms(self, indices):
        return side_by_side([self.kept[i] for i in indices])

    def mixed(self, terms):
        place = self.rows_in.shape[0] - EXTRA + (self.other is None)
        matrix = side_by_side([self.rows_in[place, i:i + self.channels, :] for i in (0, self.channels)])
        matrix = matrix[:, :self.order * self.channels]
        value = jnp.dot(matrix, terms, preferred_element_type=F32)
        return value.astype(BF16)

    def paired_with(self, indices, valid, terms):
        left = [jnp.where(valid, self.paired[i], jnp.zeros((), BF16)) for i in indices]
        return lax.dot_general(side_by_side(left), terms, CONTRACT_LANES, preferred_element_type=F32)


def valid_lanes(channels):
    lane = lane_index((channels, LANES))
    lane_in = lane % GROUP
    in_strips = ((lane_in >= 5) & (lane_in < 10)) | ((lane_in >= SIDE + 6) & (lane_in < SIDE + 11))
    return (lane >= HALO) & (lane < LANES - HALO), in_strips


def main_forward(upper, order, rows_in, _, out, grad, *scratch):
    channels = out.shape[1]
    half = out.shape[0]
    count = half + HALO
    near = rows_in.shape[0] - EXTRA
    chain = Chain(0, channels, order, rows_in, ((0, 1), (count + 1, count + 4)), scratch)
    chain.put_some(1, rows_in, 0 if upper else near - count, count)
    chain.run(1, ((0, count),))
    valid, _ = valid_lanes(channels)
    indices = [1 + HALO + i for i in range(half - HALO)]
    terms = chain.terms(indices)
    value = chain.mixed(terms)
    for i in range(len(indices)):
        out[i + HALO * upper] = value[:, LANES * i:LANES * (i + 1)]
    grad[...] = chain.paired_with(indices, valid, terms)


def main_backward(upper, order, place, rows_in, lat_first, lat_second, summed, out, summed_out, *scratch):
    channels = out.shape[1]
    half = out.shape[0]
    count = half + 2 * HALO
    near = rows_in.shape[0] - EXTRA
    is_last, _, odd = flags(place)
    beyond = Either(odd, lat_first, lat_second) if upper else Either(odd, lat_second, lat_first)
    chain = Chain(channels, None, order, rows_in, ((0, 1), (count + 1, count + 4)), scratch)
    chain.put_some(1 if upper else 1 + HALO + half, beyond, 0, HALO)
    chain.put_some(1 + HALO * upper, rows_in, 0 if upper else near - half - HALO, half + HALO)
    closed = None if upper else (is_last, lambda row, lane: row == HALO + half)
    chain.run(1, ((0, count),), closed)
    value = chain.mixed(chain.terms([1 + HALO + i for i in range(half)]))
    for i in range(half):
        out[i] = value[:, LANES * i:LANES * (i + 1)]
    summed_out[...] = summed[...]


def edge_sizes(rows):
    block = rows // BLOCKS
    strips = block + 2 * HALO
    top = strips + 6
    bottom = top + BAND + 5
    return block, top, bottom, -(-(bottom + BAND + 5) // 8) * 8


def edge_forward(order, place, strips_in, rows_in, lower, lat_first, lat_second, out, grad, *scratch):
    near = rows_in.shape[0] - EXTRA
    block, top, bottom, total = edge_sizes(strips_in.shape[0] * BLOCKS)
    is_last, _, odd = flags(place)
    north, south = Either(odd, lat_first, lat_second), Either(odd, lat_second, lat_first)
    channels = out.shape[1]
    count = block + 2 * HALO
    chain = Chain(0, channels, order, rows_in, ((0, 1), (1 + count, top + 1), (top + 1 + BAND, bottom + 1),
                                        (bottom + 1 + BAND, total)), scratch)
    chain.put_strips(strips_in, north, south)
    for i in range(HALO):
        chain.put(top + 1 + i, north, i)
        chain.put(bottom + 1 + 2 * HALO + i, south, i)
    for i in range(2 * HALO):
        chain.put(top + 1 + HALO + i, rows_in, i)
        chain.put(bottom + 1 + i, lower, near - 2 * HALO + i)

    def closed(row, lane):
        return (row == bottom + 2 * HALO) | ((row == HALO + block) & (lane >= LANES - GROUP))

    chain.run(1, ((0, count), (top, BAND), (bottom, BAND)), (is_last, closed))
    main_valid, strip_valid = valid_lanes(channels)
    strip_rows = [1 + HALO + i for i in range(block)]
    band_rows = [top + 1 + HALO + i for i in range(HALO)] + [bottom + 1 + HALO + i for i in range(HALO)]
    total_grad = jnp.zeros(grad.shape, F32)
    slot = 0
    for indices, valid in ((strip_rows, strip_valid), (band_rows, main_valid)):
        terms = chain.terms(indices)
        value = chain.mixed(terms)
        for i in range(len(indices)):
            out[slot + i] = value[:, LANES * i:LANES * (i + 1)]
        slot += len(indices)
        total_grad = total_grad + chain.paired_with(indices, valid, terms)
    grad[...] = total_grad


def edge_backward(order, place, strips_in, rows_in, lat_first, lat_second, summed, out, summed_out, *scratch):
    block = strips_in.shape[0]
    is_last, _, odd = flags(place)
    north, south = Either(odd, lat_first, lat_second), Either(odd, lat_second, lat_first)
    count = block + 2 * HALO
    chain = Chain(out.shape[1], None, order, rows_in, ((0, 1), (1 + count, scratch[0].shape[0])), scratch)
    chain.put_strips(strips_in, north, south)
    chain.run(1, ((0, count),), (is_last, lambda row, lane: (row == HALO + block) & (lane >= LANES - GROUP)))
    value = chain.mixed(chain.terms([1 + HALO + i for i in range(block)]))
    for i in range(block):
        out[i] = value[:, LANES * i:LANES * (i + 1)]
    summed_out[...] = summed[...]


def assemble_kernel(upper, lower, edges, summed, out_hbm, summed_out, wide, out, sent):
    summed_out[...] = summed[...]
    half, channels, _ = upper.shape
    rows = 2 * half
    block = rows // BLOCKS
    lane = lane_index((channels, LANES))

    def put(r, s, b, value):
        strip = edges[s]
        west = turned(strip, -(GROUP * b + 5))
        east = turned(strip, LANES - 5 - (GROUP * b + SIDE + 6))
        value = jnp.where(lane < HALO, west, jnp.where(lane >= LANES - HALO, east, value))
        wide[pl.ds(r * (3 * channels + 1), channels, stride=3), :] = value.astype(F32)

    for b in range(BLOCKS):
        for s in range(block):
            r = block * b + s
            put(r, s, b, upper[r] if r < half else lower[r - half])
    if edges.shape[0] > block:
        for i in range(HALO):
            put(i, i, 0, edges[block + i])
            put(rows - HALO + i, block - HALO + i, BLOCKS - 1, edges[block + HALO + i])

    pieces = 2
    size = channels // pieces

    def narrow(i, _):
        for j in range(size):
            o = i * size + j
            out[o] = wide[pl.ds(3 * o, rows, stride=3 * channels + 1), :].astype(BF16)
        copy(i).start()
        return 0

    def copy(i):
        span = pl.ds(i * size, size)
        return pltpu.make_async_copy(out.at[span], out_hbm.at[span], sent.at[i])

    lax.fori_loop(0, pieces, narrow, 0)
    for i in range(pieces):
        copy(i).wait()


def finish_kernel(scale, mine, theirs, out):
    order, channels = out.shape[:2]
    out[...] = ((mine[...] + theirs[...]) * scale).T.reshape(order, channels, channels)


def on_device(signal, cotangent, edge_weights, circle_shift, mixing):
    channels, rows, sector = signal.shape
    order = mixing.shape[0]
    block, top, bottom, edge_total = edge_sizes(rows)
    lat, lon = lax.axis_size("lat"), lax.axis_size("lon")
    vmem = pl.BlockSpec(memory_space=pltpu.VMEM)
    smem = pl.BlockSpec(memory_space=pltpu.SMEM)
    hbm = pl.BlockSpec(memory_space=pltpu.HBM)
    anywhere = pl.BlockSpec(memory_space=pl.ANY)
    shape = jax.ShapeDtypeStruct

    def packed(count):
        return shape((count, PACKED, LANES), BF16)

    def weighs(mib):
        return pl.CostEstimate(flops=0, bytes_accessed=mib * 1024 * 1024, transcendentals=0)

    per_row = block // 6
    half = rows // 2
    near = -(-(half + HALO) // per_row)
    half_rows = shape((near + 1, per_row, PACKED, LANES), BF16)
    at_lat, at_lon = lax.axis_index("lat"), lax.axis_index("lon")
    place = (at_lat == lat - 1).astype(jnp.int32) + 2 * (at_lon % 2) + 4 * (at_lat % 2)
    place = place.astype(jnp.int32).reshape(1)
    lon_first, lon_second, own_strips, upper, lower = pl.pallas_call(
        head_kernel,
        out_shape=(packed(per_row), packed(per_row), shape((6, per_row, PACKED, LANES), BF16), half_rows, half_rows),
        in_specs=[smem] + [hbm] * 5,
        out_specs=(anywhere,) * 5,
        scratch_shapes=[
            pltpu.VMEM(signal.shape, BF16),
            pltpu.VMEM(signal.shape, BF16),
            pltpu.VMEM(edge_weights.shape, BF16),
            pltpu.SMEM(circle_shift.shape, jnp.int32),
            pltpu.VMEM(mixing.shape, BF16),
            pltpu.VMEM((spread_size(2 * channels + 8, rows), LANES), F32),
            pltpu.VMEM((per_row, PACKED, LANES), BF16),
            pltpu.VMEM((per_row, PACKED, LANES), BF16),
            pltpu.VMEM((6, per_row, PACKED, LANES), BF16),
            pltpu.VMEM((rows // per_row + 1, per_row, PACKED, LANES), BF16),
            pltpu.SemaphoreType.DMA((11,)),
            pltpu.SemaphoreType.DMA((per_row, 6)),
        ],
        compiler_params=pltpu.CompilerParams(vmem_limit_bytes=PACK_VMEM),
        name="head",
    )(place, signal, cotangent, edge_weights, circle_shift, mixing)
    own_strips = own_strips.reshape(block, PACKED, LANES)
    upper, lower = [array.reshape((near + 1) * per_row, PACKED, LANES) for array in (upper, lower)]

    pairs = [(i, i ^ 1) for i in range(lon)]
    other_pairs = [(i, (i + 1 if i % 2 else i - 1) % lon) for i in range(lon)]
    lon_first = lax.ppermute(lon_first, "lon", pairs)
    lon_second = lax.ppermute(lon_second, "lon", other_pairs)

    half_shape = shape((half, channels, LANES), BF16)
    grad_shape = shape((channels, order * channels), F32)

    def chain_scratch(total, with_pairs):
        total = -(-total // 8) * 8
        scratch = [pltpu.VMEM((total, channels, LANES), F32)] * 3 + [
            pltpu.VMEM((total, order * channels, LANES), BF16),
            pltpu.VMEM((7 * total, LANES), F32),
            pltpu.VMEM((8 * (total + 1), LANES), F32),
        ]
        return scratch + [pltpu.VMEM((total, channels, LANES), BF16)] * with_pairs

    def run_main_forward(is_upper, after):
        return pl.pallas_call(
            functools.partial(main_forward, is_upper, order),
            out_shape=(half_shape, grad_shape),
            in_specs=[vmem, vmem],
            out_specs=(vmem, vmem),
            scratch_shapes=chain_scratch(half + HALO + 4, True),
            compiler_params=params(16),
            cost_estimate=weighs(12),
            name="forward_upper" if is_upper else "forward_lower",
        )(upper if is_upper else lower, after)

    upper_f, grad_upper = run_main_forward(True, upper)

    strips, lat_first, lat_second = pl.pallas_call(
        merge_kernel,
        out_shape=(packed(block), packed(HALO + 2), packed(HALO + 2)),
        in_specs=[smem] + [vmem] * 6,
        out_specs=(vmem,) * 3,
        compiler_params=params(8),
        name="merge",
    )(place, own_strips, upper, lower, lon_first, lon_second, grad_upper)

    pairs = [(i, i ^ 1) for i in range(lat)]
    other_pairs = [(i, i + 1 if i % 2 else i - 1) for i in range(1, lat - 1)]
    after = lat_first
    lat_first = lax.ppermute(lat_first, "lat", pairs)
    lat_second = lax.ppermute(lat_second, "lat", other_pairs)
    lower_f, grad_lower = run_main_forward(False, after)

    edge_f, grad_edge = pl.pallas_call(
        functools.partial(edge_forward, order),
        out_shape=(shape((block + 2 * HALO, channels, LANES), BF16), grad_shape),
        in_specs=[smem] + [vmem] * 5,
        out_specs=(vmem, vmem),
        scratch_shapes=chain_scratch(edge_total, True),
        compiler_params=params(16),
        cost_estimate=weighs(12),
        name="edge_forward",
    )(place, strips, upper, lower, lat_first, lat_second)

    rounds = []
    for axis, devices in (("lon", lon), ("lat", lat)):
        reach = 1
        while reach < devices:
            rounds.append((axis, [(i, i ^ reach) for i in range(devices)]))
            reach *= 2
    rounds = [r for r in rounds if r[0] == "lon"] + [r for r in rounds if r[0] == "lat"][::-1]

    results = {}

    def run_backward_half(is_upper, share):
        name = "backward_upper" if is_upper else "backward_lower"
        results[name], share = pl.pallas_call(
            functools.partial(main_backward, is_upper, order),
            out_shape=(half_shape, grad_shape),
            in_specs=[smem] + [vmem] * 4,
            out_specs=(vmem, vmem),
            scratch_shapes=chain_scratch(half + 2 * HALO + 4, False),
            compiler_params=params(16),
            cost_estimate=weighs(12),
            name=name,
        )(place, upper if is_upper else lower, lat_first, lat_second, share)
        return share

    def run_edge_backward(share):
        results["edge"], share = pl.pallas_call(
            functools.partial(edge_backward, order),
            out_shape=(shape((block, channels, LANES), BF16), grad_shape),
            in_specs=[smem] + [vmem] * 5,
            out_specs=(vmem, vmem),
            scratch_shapes=chain_scratch(block + 2 * HALO + 8, False),
            compiler_params=params(12),
            cost_estimate=weighs(12),
            name="edge_backward",
        )(place, strips, upper, lat_first, lat_second, share)
        return share

    def assemble(upper, lower, edges, share, name):
        return pl.pallas_call(
            assemble_kernel,
            out_shape=(shape(signal.shape, BF16), grad_shape),
            in_specs=[vmem] * 4,
            out_specs=(hbm, vmem),
            scratch_shapes=[
                pltpu.VMEM((spread_size(channels, rows), LANES), F32),
                pltpu.VMEM(signal.shape, BF16),
                pltpu.SemaphoreType.DMA((2,)),
            ],
            compiler_params=params(12),
            cost_estimate=weighs(8),
            name=name,
        )(upper, lower, edges, share)

    def run_assemble_forward(share):
        results["output"], share = assemble(upper_f, lower_f, edge_f, share, "assemble_forward")
        return share

    def run_assemble_backward(share):
        results["signal_grad"], share = assemble(
            results["backward_upper"], results["backward_lower"], results["edge"], share, "assemble_backward")
        return share

    beside = [functools.partial(run_backward_half, True), functools.partial(run_backward_half, False), run_edge_backward,
              run_assemble_forward, run_assemble_backward]
    share = grad_upper + grad_lower + grad_edge
    theirs = jnp.zeros_like(share)
    for number in range(max(len(rounds), len(beside))):
        if number:
            share = share + theirs
        theirs = lax.ppermute(share, *rounds[number]) if number < len(rounds) else jnp.zeros_like(share)
        if number < len(beside):
            share = beside[number](share)

    norm_scale = 1.0 / math.sqrt(rows * lat * sector * lon)
    mixing_grad = pl.pallas_call(
        functools.partial(finish_kernel, norm_scale),
        out_shape=shape(mixing.shape, F32),
        in_specs=[vmem, vmem],
        out_specs=vmem,
        compiler_params=params(4),
        name="finish",
    )(share, theirs)
    return (results["output"], results["signal_grad"], mixing_grad)


def solution(mesh):
    in_specs = (P(None, "lat", "lon"), P(None, "lat", "lon"), P(None, "lat", "lon"), P("lat"), P())
    out_specs = (P(None, "lat", "lon"), P(None, "lat", "lon"), P())
    return jax.shard_map(
        on_device, mesh=mesh, in_specs=in_specs, out_specs=out_specs, check_vma=False
    )
```
